256 devices in a mesh: gx: 16 (over z, core), gy: 4 (over x), gz: 4 (over y).
Axes of the slice: x: 4, y: 4, z: 8, core: 2. Of those that a mesh axis runs over, the one named last changes fastest.
Arguments:
- density: float32 [512, 128, 512], P('gx', 'gy', 'gz'), may hold values from 0.8 to 1.25
- momentum: float32 [3, 512, 128, 512], P(None, 'gx', 'gy', 'gz'), may hold values from -1 to 1
- energy: float32 [512, 128, 512], P('gx', 'gy', 'gz'), may hold values from 3 to 4
- metric: float32 [128], replicated, may hold values from 0.5 to 4
Outputs:
- tendency: float32 [5, 512, 128, 512], P(None, 'gx', 'gy', 'gz')
- state_next: float32 [5, 512, 128, 512], P(None, 'gx', 'gy', 'gz')
The draws below stay inside these ranges and needn't reach their ends.
All inputs are finite; a program needn't handle non-finite values.
Results may differ from the reference program's by a relative error of at most 0.0003.
Values sent between devices are 32-bit elements; how exact they have to be, the bound alone decides.
A program may use at most 128 MiB of HBM per device.

```python
import math
import jax
import jax.numpy as jnp
from jax import lax

NX = 512
NY = 128
NZ = 512


def block_scale(key, shape, split, least, largest):
    loudness, own = 1.0, jax.random.fold_in(key, 6)
    for dim, blocks in split:
        steps = jnp.exp(jax.random.uniform(jax.random.fold_in(own, dim), (blocks,), jnp.float32, least / len(split), largest / len(split)))
        loudness = loudness * jnp.repeat(steps, shape[dim] // blocks).reshape([-1 if axis == dim else 1 for axis in range(len(shape))])
    return loudness


def gaussian(own_key, shape, deviation, limit, shards=(), kind=jnp.bfloat16):
    loudness = block_scale(own_key, shape, shards, -0.22, 0.18) if shards else 1.0
    entries = jax.random.normal(own_key, shape, jnp.float32) * deviation * loudness
    return jnp.minimum(jnp.maximum(entries, -limit), limit).astype(kind)


def setup_inputs(seed: int = 0) -> dict:
    key_of = jax.random.split(jax.random.key(seed), 5)
    return {
        "density": jnp.clip(0.8 + 0.45 * jax.random.uniform(key_of[0], (NX, NY, NZ), jnp.float32) ** block_scale(key_of[0], (NX, NY, NZ), ((0, 16), (1, 4), (2, 4)), -0.2, 0.2), 0.8, 1.25),
        "momentum": gaussian(key_of[1], (3, NX, NY, NZ), 0.3, 1.0, ((1, 16), (2, 4), (3, 4)), jnp.float32),
        "energy": jnp.clip(3.0 + 1.0 * jax.random.uniform(key_of[2], (NX, NY, NZ), jnp.float32) ** block_scale(key_of[2], (NX, NY, NZ), ((0, 16), (1, 4), (2, 4)), -0.2, 0.2), 3.0, 4.0),
        "metric": jnp.clip(jnp.exp(jax.random.uniform(key_of[3], (NY,), jnp.float32, math.log(0.5), math.log(4.0))), 0.5, 4.0),
    }


heat_ratio = 1.4
compact_alpha = 1.0 / 3.0
filter_alpha = 0.499
time_step = 0.05


def thomas(lower_band, main_band, upper_band, source):
    def forward(carried, row_data):
        c_prev, d_prev = carried
        low_val, mid_val, up_val, row_val = row_data
        denom = mid_val - low_val * c_prev
        c_now = up_val / denom
        d_now = (row_val - low_val * d_prev) / denom
        return (c_now, d_now), (c_now, d_now)

    start_state = (jnp.zeros((), source.dtype), jnp.zeros(source.shape[1:], source.dtype))
    _, (c_all, d_all) = lax.scan(forward, start_state, (lower_band, main_band, upper_band, source))

    def backward(x_next, row_data):
        c_val, d_val = row_data
        x_now = d_val - c_val * x_next
        return x_now, x_now

    _, solved = lax.scan(backward, jnp.zeros(source.shape[1:], source.dtype), (c_all, d_all), reverse=True)
    return solved


def wall_operator(metric):
    total = metric.shape[0]
    places = jnp.arange(total)
    unit = jnp.ones((total,), metric.dtype)
    near_wall = (places == 1) | (places == total - 2)
    lower_band = unit * jnp.where(places == 0, 0.0, jnp.where(places == total - 1, 2.0, jnp.where(near_wall, 0.25, compact_alpha)))
    upper_band = unit * jnp.where(places == total - 1, 0.0, jnp.where(places == 0, 2.0, jnp.where(near_wall, 0.25, compact_alpha)))
    row_place = places[:, None]
    col_place = places[None, :]
    offset = col_place - row_place
    interior = jnp.where(offset == 1, 7.0 / 9.0, jnp.where(offset == -1, -7.0 / 9.0, jnp.where(offset == 2, 1.0 / 36.0, jnp.where(offset == -2, -1.0 / 36.0, 0.0))))
    second = jnp.where(offset == 1, 0.75, jnp.where(offset == -1, -0.75, 0.0))
    top_row = jnp.where(col_place == 0, -2.5, jnp.where(col_place == 1, 2.0, jnp.where(col_place == 2, 0.5, 0.0)))
    bottom_row = jnp.where(col_place == total - 1, 2.5, jnp.where(col_place == total - 2, -2.0, jnp.where(col_place == total - 3, -0.5, 0.0)))
    near_rows = (row_place == 1) | (row_place == total - 2)
    stencil = jnp.where(row_place == 0, top_row, jnp.where(row_place == total - 1, bottom_row, jnp.where(near_rows, second, interior)))
    stencil = stencil.astype(metric.dtype)
    solved = thomas(lower_band, unit, upper_band, stencil)
    return metric[:, None] * solved


def directed_flux(state, direction):
    density = state[0]
    momentum = state[1:4]
    energy = state[4]
    velocity = momentum / density
    pressure = (heat_ratio - 1.0) * (energy - 0.5 * jnp.sum(momentum * velocity, axis=0))
    speed = velocity[direction]
    pieces = [momentum[direction]]
    for component in range(3):
        term = momentum[component] * speed
        if component == direction:
            term = term + pressure
        pieces.append(term)
    pieces.append((energy + pressure) * speed)
    return jnp.stack(pieces)


def compact_source(padded, axis_pos):
    length = padded.shape[axis_pos] - 4

    def shifted(begin):
        return lax.slice_in_dim(padded, begin, begin + length, axis=axis_pos)

    return (7.0 / 9.0) * (shifted(3) - shifted(1)) + (1.0 / 36.0) * (shifted(4) - shifted(0))


def cyclic_solve(source, coupling, axis_pos):
    moved = jnp.moveaxis(source, axis_pos, 0)
    total = moved.shape[0]
    flat = moved.reshape(total, -1)
    places = jnp.arange(total)
    unit = jnp.ones((total,), source.dtype)
    lower_band = unit * jnp.where(places == 0, 0.0, coupling)
    upper_band = unit * jnp.where(places == total - 1, 0.0, coupling)
    main_band = unit * jnp.where(places == 0, 2.0, jnp.where(places == total - 1, 1.0 + coupling * coupling, 1.0))
    first_sol = thomas(lower_band, main_band, upper_band, flat)
    corner = unit * jnp.where(places == 0, -1.0, jnp.where(places == total - 1, coupling, 0.0))
    second_sol = thomas(lower_band, main_band, upper_band, corner[:, None])[:, 0]
    factor = (first_sol[0] - coupling * first_sol[total - 1]) / (1.0 + second_sol[0] - coupling * second_sol[total - 1])
    result = first_sol - factor[None, :] * second_sol[:, None]
    return jnp.moveaxis(result.reshape(moved.shape), 0, axis_pos)


def reference(density, momentum, energy, metric):
    state = jnp.concatenate([density[None], momentum, energy[None]], axis=0)
    flux_x = directed_flux(jnp.pad(state, ((0, 0), (2, 2), (0, 0), (0, 0)), mode="wrap"), 0)
    flux_z = directed_flux(jnp.pad(state, ((0, 0), (0, 0), (0, 0), (2, 2)), mode="wrap"), 2)
    flux_y = directed_flux(state, 1)
    deriv_x = cyclic_solve(compact_source(flux_x, 1), compact_alpha, 1)
    deriv_z = cyclic_solve(compact_source(flux_z, 3), compact_alpha, 3)
    wall = wall_operator(metric)
    deriv_y = jnp.einsum("yk,fxkz->fxyz", wall, flux_y, precision=lax.Precision.HIGHEST)
    tendency = -(deriv_x + deriv_y + deriv_z)
    middle = state + time_step * tendency
    filter_source = (0.5 + filter_alpha) * (middle + 0.5 * (jnp.roll(middle, 1, axis=1) + jnp.roll(middle, -1, axis=1)))
    state_next = cyclic_solve(filter_source, filter_alpha, 1)
    return tendency, state_next
```

```python
import functools

import jax
import jax.numpy as jnp
import numpy as np
from jax import lax
from jax.experimental import pallas as pl
from jax.experimental.pallas import tpu as pltpu
from jax.sharding import PartitionSpec as P

heat_ratio = 1.4
compact_alpha = 1.0 / 3.0
filter_alpha = 0.499
time_step = 0.05
near_weight = 7.0 / 9.0
wide_weight = 1.0 / 36.0
HIGH = lax.Precision.HIGHEST
MESH = pl.DeviceIdType.MESH
KINDS_Y = ((1, "last"), (1, "ml"), (1, "mr"), (2, "ml"), (2, "mr"), (3, "ml"), (3, "mr"), (3, "first"))


def decay(alpha):
    root = np.sqrt(1.0 - 4.0 * alpha * alpha)
    return (-1.0 + root) / (2.0 * alpha), 1.0 / root


def compact_kernel():
    ratio, gain = decay(compact_alpha)

    def green(n):
        return gain * ratio ** abs(n)

    def kernel(d):
        return near_weight * (green(d + 1) - green(d - 1)) + wide_weight * (green(d + 2) - green(d - 2))

    amplitude = kernel(2) / ratio**2
    return ratio, amplitude, kernel(1) - amplitude * ratio


def local_compact(size):
    ratio, amplitude, corner = compact_kernel()
    table = np.zeros((size, size))
    for i in range(size):
        for j in range(size):
            d = abs(i - j)
            if d:
                value = amplitude * ratio**d + (corner if d == 1 else 0.0)
                table[i, j] = value if i > j else -value
    return table


def table_thomas(lower_band, main_band, upper_band, source):
    count = source.shape[0]
    c_all = np.zeros(count)
    d_all = np.zeros(source.shape)
    c_prev = 0.0
    d_prev = np.zeros(source.shape[1:])
    for place in range(count):
        denom = main_band[place] - lower_band[place] * c_prev
        c_prev = upper_band[place] / denom
        d_prev = (source[place] - lower_band[place] * d_prev) / denom
        c_all[place] = c_prev
        d_all[place] = d_prev
    solved = np.zeros(source.shape)
    x_next = np.zeros(source.shape[1:])
    for place in range(count - 1, -1, -1):
        x_next = d_all[place] - c_all[place] * x_next
        solved[place] = x_next
    return solved


def wall_bands(total):
    lower = np.full(total, compact_alpha)
    upper = np.full(total, compact_alpha)
    lower[0], lower[1], lower[total - 2], lower[total - 1] = 0.0, 0.25, 0.25, 2.0
    upper[0], upper[1], upper[total - 2], upper[total - 1] = 2.0, 0.25, 0.25, 0.0
    return lower, upper


def wall_table(total):
    lower, upper = wall_bands(total)
    stencil = np.zeros((total, total))
    for i in range(2, total - 2):
        stencil[i, i + 1], stencil[i, i - 1] = near_weight, -near_weight
        stencil[i, i + 2], stencil[i, i - 2] = wide_weight, -wide_weight
    for i in (1, total - 2):
        stencil[i, i + 1], stencil[i, i - 1] = 0.75, -0.75
    stencil[0, :3] = (-2.5, 2.0, 0.5)
    stencil[total - 1, total - 3 :] = (-0.5, -2.0, 2.5)
    return table_thomas(lower, np.ones(total), upper, stencil)


@functools.cache
def wall_tables(blocks, size):
    total = blocks * size
    table = wall_table(total)
    lower, upper = wall_bands(total)
    down = np.zeros(total)
    for i in range(total - 1, 0, -1):
        down[i - 1] = -lower[i] / (1.0 + upper[i] * down[i])
    up = np.zeros(total)
    for i in range(total - 1):
        up[i + 1] = -upper[i] / (1.0 + lower[i] * up[i])
    carry_l, carry_r, corner_l, corner_r = [], [], [], []
    moment_l, moment_r = np.zeros((blocks, size)), np.zeros((blocks, size))
    for b in range(blocks):
        head, tail = b * size, b * size + size - 1
        carry_l.append(np.concatenate([[1.0], np.cumprod(down[head:tail])]))
        carry_r.append(np.concatenate([[1.0], np.cumprod(up[head + 1 : tail + 1][::-1])])[::-1])
        corner_l.append(table[head, head - 1] - table[head + 1, head - 1] / down[head] if b else 0.0)
        corner_r.append(table[tail, tail + 1] - table[tail - 1, tail + 1] / up[tail] if b < blocks - 1 else 0.0)
        if b < blocks - 1:
            to = tail + 1
            moment_l[b] = table[to, head:to]
            moment_l[b, size - 1] = table[to + 1, tail] / down[to]
        if b:
            to = head - 1
            moment_r[b] = table[to, head : tail + 1]
            moment_r[b, 0] = table[to - 1, head] / up[to]
    apply = np.zeros((blocks, 8 * size + 32, 8 * size))
    carry = np.zeros((blocks, 8 * size, 8 * len(KINDS_Y)))
    eye = np.eye(8)
    for b in range(blocks):
        rows = slice(b * size, (b + 1) * size)
        apply[b, : 8 * size] = np.kron(eye, table[rows, rows])
        first, last = np.eye(size)[0], np.eye(size)[size - 1]
        for kind, weights in enumerate((last, moment_l[b], moment_r[b], first)):
            apply[b, 8 * size + 8 * kind : 8 * size + 8 * kind + 8] = np.kron(eye, weights[None])
        for place, (offset, kind) in enumerate(KINDS_Y):
            column = np.zeros(size)
            if b - offset >= 0:
                if kind == "ml":
                    scale = 1.0
                    for c in range(b - offset + 1, b):
                        scale *= np.prod(down[c * size : (c + 1) * size])
                    column = scale * carry_l[b]
                elif kind == "last" and offset == 1:
                    column[0] = corner_l[b]
            else:
                distance = blocks - offset
                if kind == "mr":
                    scale = 1.0
                    for c in range(b + 1, b + distance):
                        scale *= np.prod(up[c * size : (c + 1) * size])
                    column = scale * carry_r[b]
                elif kind == "first" and distance == 1:
                    column[size - 1] = corner_r[b]
            carry[b, :, 8 * place : 8 * place + 8] = np.kron(eye, column[:, None])
    return apply.astype(np.float32), carry.astype(np.float32)


@functools.cache
def span_tables(blocks, size):
    ratio, amplitude, corner = compact_kernel()
    places = np.arange(size)
    images = 1.0 / (1.0 - ratio ** (blocks * size))
    moments = np.zeros((4, size))
    moments[0, size - 1] = 1.0
    moments[1] = ratio ** (size - places)
    moments[2] = ratio ** (places + 1.0)
    moments[3, 0] = 1.0
    carries = np.zeros((blocks, 4, size))
    for slot in range(blocks):
        behind = slot if slot else blocks
        ahead = blocks - slot
        carries[slot, 1] = amplitude * images * ratio ** (size * (behind - 1.0)) * ratio**places
        carries[slot, 2] = -amplitude * images * ratio ** (size * (ahead - 1.0)) * ratio ** (size - 1.0 - places)
        if behind == 1:
            carries[slot, 0, 0] = corner
        if ahead == 1:
            carries[slot, 3, size - 1] = -corner
    both_moments = np.zeros((8, 2 * size))
    both_moments[:4, :size] = moments
    both_moments[4:, size:] = moments
    both_carries = np.zeros((blocks, 8, 2 * size))
    both_carries[:, :4, :size] = carries
    both_carries[:, 4:, size:] = carries
    return (
        local_compact(size).T.astype(np.float32),
        both_moments.astype(np.float32),
        both_carries.reshape(8 * blocks, 2 * size).astype(np.float32),
    )


def stream_weights(size):
    ratio, amplitude, _ = compact_kernel()
    filter_ratio, _ = decay(filter_alpha)
    places = np.arange(size)
    weight_u = filter_ratio ** (size - places)
    weight_v = filter_ratio ** (places + 1.0)
    local = local_compact(size)
    return np.stack(
        [
            weight_u,
            weight_v,
            -time_step * (weight_u @ local),
            -time_step * (weight_v @ local),
            ratio ** (size - places),
            ratio ** (places + 1.0),
            amplitude * ratio**places,
            amplitude * ratio ** (size - 1.0 - places),
        ]
    )


def exchange_kernel(
    nx,
    ny,
    nz,
    den,
    mom,
    ene,
    metric,
    wtab,
    ky_hbm,
    py_hbm,
    kz,
    qz,
    pz,
    tend,
    carry_x,
    carry_f,
    fx,
    fy,
    fz,
    ky,
    py,
    uv0,
    sy,
    sz,
    dys,
    dzs,
    ys_out,
    ys_in,
    zs_in,
    yb_out,
    yb_in,
    zm_in,
    xn_out,
    xn_in,
    xm_out,
    xm_in,
    uv_out,
    uv_in,
    xo_out,
    xo_in,
    io_out,
    io_in,
    load_sem,
    send_sem,
    recv_sem,
):
    fields, size_x, size_y, size_z = fx.shape
    me_x, me_y, me_z = lax.axis_index("gx"), lax.axis_index("gy"), lax.axis_index("gz")
    rows = size_y // nx
    ratio, amplitude, corner = compact_kernel()
    weights = stream_weights(size_x)
    filter_ratio, _ = decay(filter_alpha)

    def along(axis, offset):
        me, count = {"gx": (me_x, nx), "gy": (me_y, ny), "gz": (me_z, nz)}[axis]
        return lax.rem(me + offset + count, count)

    barrier = pltpu.get_barrier_semaphore()
    for axis, count in (("gx", nx), ("gy", ny), ("gz", nz)):
        for offset in range(1, count):
            pl.semaphore_signal(barrier, inc=1, device_id={axis: along(axis, offset)}, device_id_type=MESH)

    loads = [
        pltpu.make_async_copy(ky_hbm.at[me_y], ky, load_sem.at[0]),
        pltpu.make_async_copy(py_hbm.at[me_y], py, load_sem.at[1]),
    ]
    for load in loads:
        load.start()

    next_sem = [0]

    def remote(src, dst, axis, offset):
        place = next_sem[0]
        next_sem[0] = place + 1
        return pltpu.make_async_remote_copy(
            src_ref=src,
            dst_ref=dst,
            send_sem=send_sem.at[place],
            recv_sem=recv_sem.at[place],
            device_id={axis: along(axis, offset)},
            device_id_type=MESH,
        )

    unroll = 4

    def flux_chunk(chunk, _):
        ys = pl.ds(pl.multiple_of(chunk * 8, 8), 8)

        def cells(step, acc):
            acc = list(acc)
            for inner in range(unroll):
                x = step * unroll + inner
                w = [wtab[k, x] for k in range(6)]
                rho, energy = den[x, ys, :], ene[x, ys, :]
                m = [mom[j, x, ys, :] for j in range(3)]
                inverse = 1.0 / rho
                v = [m[j] * inverse for j in range(3)]
                own = [m[j] * v[j] for j in range(3)]
                pressure = (heat_ratio - 1.0) * (energy - 0.5 * (own[0] + own[1] + own[2]))
                m12, m13, m23 = m[0] * v[1], m[0] * v[2], m[1] * v[2]
                total = energy + pressure
                flux_x = (m[0], own[0] + pressure, m12, m13, total * v[0])
                flux_y = (m[1], m12, own[1] + pressure, m23, total * v[1])
                flux_z = (m[2], m13, m23, own[2] + pressure, total * v[2])
                state = (rho, m[0], m[1], m[2], energy)
                for f in range(fields):
                    fx[f, x, ys, :] = flux_x[f]
                    fy[f, x, ys, :] = flux_y[f]
                    fz[f, x, ys, :] = flux_z[f]
                    acc[f] = acc[f] + w[0] * state[f] + w[2] * flux_x[f]
                    acc[5 + f] = acc[5 + f] + w[1] * state[f] + w[3] * flux_x[f]
                    acc[10 + f] = acc[10 + f] + w[4] * flux_x[f]
                    acc[15 + f] = acc[15 + f] + w[5] * flux_x[f]
            return tuple(acc)

        zero = jnp.zeros((8, size_z), jnp.float32)
        acc = lax.fori_loop(0, size_x // unroll, cells, (zero,) * 20)
        for f in range(fields):
            uv0[0, f, ys, :] = acc[f]
            uv0[1, f, ys, :] = acc[5 + f]
            xn_out[0, 0, f, ys, :] = acc[10 + f]
            xn_out[0, 1, f, ys, :] = fx[f, size_x - 1, ys, :]
            xn_out[1, 0, f, ys, :] = acc[15 + f]
            xn_out[1, 1, f, ys, :] = fx[f, 0, ys, :]

        def sums(step, acc):
            acc = list(acc)
            for inner in range(unroll):
                x = step * unroll + inner
                w = [wtab[k, x] for k in range(2)]
                for f in range(fields):
                    value_y, value_z = fy[f, x, ys, :], fz[f, x, ys, :]
                    acc[f] = acc[f] + w[0] * value_y
                    acc[5 + f] = acc[5 + f] + w[1] * value_y
                    acc[10 + f] = acc[10 + f] + w[0] * value_z
                    acc[15 + f] = acc[15 + f] + w[1] * value_z
            return tuple(acc)

        acc = lax.fori_loop(0, size_x // unroll, sums, (zero,) * 20)
        for f in range(fields):
            sy[f, ys, :] = acc[f]
            sy[5 + f, ys, :] = acc[5 + f]
            sz[0, f, ys, :] = acc[10 + f]
            sz[1, f, ys, :] = acc[15 + f]
        return 0

    lax.fori_loop(0, size_y // 8, flux_chunk, 0)
    sy[10:16] = jnp.zeros((6, size_y, size_z), jnp.float32)
    sz[:, 5:8] = jnp.zeros((2, 3, size_y, size_z), jnp.float32)

    pl.semaphore_wait(barrier, nx + ny + nz - 3)

    xn = [
        remote(xn_out.at[0], xn_in.at[0], "gx", 1),
        remote(xn_out.at[1], xn_in.at[1], "gx", -1),
    ]
    for copy in xn:
        copy.start()
    for owner in range(nx):
        for side in range(2):
            for f in range(fields):
                xm_out[owner, side, rows * f : rows * f + rows, :] = xn_out[
                    side, 0, f, rows * owner : rows * owner + rows, :
                ]
    xm = [remote(xm_out.at[along("gx", k)], xm_in.at[k], "gx", k) for k in range(1, nx)]
    for copy in xm:
        copy.start()
    xm_in[0] = xm_out[me_x]

    for load in loads:
        load.wait()
    shape = (8 * size_y, ny * size_y)
    row_place = lax.broadcasted_iota(jnp.int32, shape, 0)
    col_place = lax.broadcasted_iota(jnp.int32, shape, 1)
    mine = col_place == me_y * size_y + lax.rem(row_place, size_y)
    metric_rows = jnp.sum(jnp.where(mine, metric[...], 0.0), axis=1, keepdims=True)
    ky[: 8 * size_y, :] = ky[: 8 * size_y, :] * metric_rows
    py[...] = py[...] * metric_rows

    def apply_wall(cells):
        result = jnp.dot(ky[...], cells, precision=HIGH, preferred_element_type=jnp.float32)
        return (
            result[: 8 * size_y].reshape(8, size_y, size_z),
            result[8 * size_y :].reshape(4, 8, size_z),
        )

    def span_moments(cells):
        return lax.dot_general(
            qz[...], cells, (((1,), (1,)), ((), ())), precision=HIGH, preferred_element_type=jnp.float32
        )

    for group in range(2):
        dys[8 * group : 8 * group + 8], ys_out[:, 8 * group : 8 * group + 8, :] = apply_wall(
            sy[8 * group : 8 * group + 8].reshape(8 * size_y, size_z)
        )
    ys = [
        remote(ys_out.at[pl.ds(0, 3)], ys_in.at[pl.ds(0, 3)], "gy", 1),
        remote(ys_out.at[pl.ds(1, 2)], ys_in.at[pl.ds(3, 2)], "gy", 2),
        remote(ys_out.at[pl.ds(1, 3)], ys_in.at[pl.ds(5, 3)], "gy", 3),
    ]
    for copy in ys:
        copy.start()
    zs_in[0] = span_moments(
        jnp.concatenate([sz[0].reshape(8 * size_y, size_z), sz[1].reshape(8 * size_y, size_z)], axis=1)
    )
    zs = [remote(zs_in.at[0], zs_in.at[k], "gz", k) for k in range(1, nz)]
    for copy in zs:
        copy.start()
    dzs[...] = jnp.dot(
        sz[...].reshape(16 * size_y, size_z), kz[...], precision=HIGH, preferred_element_type=jnp.float32
    ).reshape(2, 8, size_y, size_z)

    def wall_field(f, _):
        def wall_group(group, _):
            xs = pl.ds(pl.multiple_of(group * 8, 8), 8)
            local, moments = apply_wall(fy[f, xs].reshape(8 * size_y, size_z))
            tend[f, xs] = local
            yb_out[:, f, xs, :] = moments
            return 0

        return lax.fori_loop(0, size_x // 8, wall_group, 0)

    lax.fori_loop(0, fields, wall_field, 0)
    yb = [
        remote(yb_out.at[pl.ds(0, 3)], yb_in.at[pl.ds(0, 3)], "gy", 1),
        remote(yb_out.at[pl.ds(1, 2)], yb_in.at[pl.ds(3, 2)], "gy", 2),
        remote(yb_out.at[pl.ds(1, 3)], yb_in.at[pl.ds(5, 3)], "gy", 3),
    ]
    for copy in yb:
        copy.start()
    half = size_x // 2

    def span_field(f, _):
        pair = [fz[f, pl.ds(part * half, half)].reshape(half * size_y, size_z) for part in range(2)]
        zm_in[0, f] = span_moments(jnp.concatenate(pair, axis=1))
        return 0

    lax.fori_loop(0, fields, span_field, 0)
    zm = [remote(zm_in.at[0], zm_in.at[k], "gz", k) for k in range(1, nz)]
    for copy in zm:
        copy.start()

    def span_carries(received):
        return lax.dot_general(
            received, pz[...], (((0,), (0,)), ((), ())), precision=HIGH, preferred_element_type=jnp.float32
        )

    for copy in xn + ys + zs:
        copy.wait()
    powers = (ratio ** np.arange(size_x), ratio ** (size_x - 1.0 - np.arange(size_x)))
    span = span_carries(zs_in[...].reshape(8 * nz, 8 * size_y))
    wall = [
        jnp.dot(
            py[...],
            ys_in[:, 8 * group : 8 * group + 8, :].reshape(64, size_z),
            precision=HIGH,
            preferred_element_type=jnp.float32,
        )
        for group in range(2)
    ]
    for side in range(2):
        gains = [
            amplitude * float(weights[side] @ powers[0]),
            corner * float(weights[side][0]),
            -amplitude * float(weights[side] @ powers[1]),
            -corner * float(weights[side][size_x - 1]),
        ]
        for f in range(fields):
            unit = 5 * side + f
            place = (unit % 8) * size_y
            change = dys[unit] + wall[unit // 8][place : place + size_y]
            change = change + dzs[side, f] + span[f * size_y : (f + 1) * size_y, side * size_z : (side + 1) * size_z]
            for gain, value in zip(gains, (xn_in[0, 0, f], xn_in[0, 1, f], xn_in[1, 0, f], xn_in[1, 1, f])):
                change = change + gain * value
            value = uv0[side, f] - time_step * change
            for owner in range(nx):
                uv_out[owner, side, rows * f : rows * f + rows, :] = value[rows * owner : rows * owner + rows]
    uv = [remote(uv_out.at[along("gx", k)], uv_in.at[k], "gx", k) for k in range(1, nx)]
    for copy in uv:
        copy.start()
    uv_in[0] = uv_out[me_x]

    def sweep(behind, power, values):
        step = 1 if behind else -1
        total = values[0] if behind else values[nx - 1]
        for k in range(1, nx):
            total = total + float(power**k) * (values[k] if behind else values[nx - 1 - k])
        total = total * float(1.0 / (1.0 - power**nx))
        place = nx - 1 if behind else 0
        result = [None] * nx
        result[place] = total
        for _ in range(nx - 1):
            total = values[place] + float(power) * total
            place = place - step
            result[place] = total
        return result

    for copy in xm:
        copy.wait()
    power = ratio**size_x
    near_l = sweep(True, power, [xm_in[k, 0] for k in range(nx)])
    near_r = sweep(False, power, [xm_in[k, 1] for k in range(nx)])
    for k in range(nx):
        xo_out[k, 0] = float(power) * near_l[(k + 1) % nx]
        xo_out[k, 1] = float(power) * near_r[(k - 1) % nx]
    xo = [remote(xo_out.at[k], xo_in.at[me_x], "gx", -k) for k in range(1, nx)]
    for copy in xo:
        copy.start()
    xo_in[me_x] = xo_out[0]

    def span_local(f, _):
        for part in range(4):
            xs = pl.ds(part * (size_x // 4), size_x // 4)
            tend[f, xs] += jnp.dot(
                fz[f, xs].reshape(size_x // 4 * size_y, size_z),
                kz[...],
                precision=HIGH,
                preferred_element_type=jnp.float32,
            ).reshape(size_x // 4, size_y, size_z)
        return 0

    lax.fori_loop(0, fields, span_local, 0)

    for copy in uv:
        copy.wait()
    filter_power = filter_ratio**size_x
    for side in range(2):
        gain_l = -time_step * amplitude * float(weights[side] @ powers[0])
        gain_r = time_step * amplitude * float(weights[side] @ powers[1])
        values = [uv_in[k, side] + gain_l * xo_out[k, 0] + gain_r * xo_out[k, 1] for k in range(nx)]
        for k, value in enumerate(sweep(side == 0, filter_power, values)):
            io_out[k, side] = value
    io = [remote(io_out.at[k], io_in.at[me_x], "gx", -k) for k in range(1, nx)]
    for copy in io:
        copy.start()
    io_in[me_x] = io_out[0]

    for copy in yb + zm:
        copy.wait()

    def carries(f, _):
        for part in range(4):
            xs = pl.ds(8 * part, 8)
            tend[f, xs] += jnp.dot(
                py[...],
                yb_in[:, f, xs, :].reshape(64, size_z),
                precision=HIGH,
                preferred_element_type=jnp.float32,
            ).reshape(8, size_y, size_z)
        both = span_carries(zm_in[:, f].reshape(8 * nz, half * size_y))
        for part in range(2):
            xs = pl.ds(part * half, half)
            tend[f, xs] += both[:, part * size_z : (part + 1) * size_z].reshape(half, size_y, size_z)
        return 0

    lax.fori_loop(0, fields, carries, 0)

    def scan_chunk(chunk, _):
        ys = pl.ds(pl.multiple_of(chunk * 8, 8), 8)

        def ahead(step, carried):
            carried = list(carried)
            for inner in range(unroll):
                x = step * unroll + inner
                for f in range(fields):
                    u, before = carried[f], carried[5 + f]
                    tend[f, x, ys, :] += amplitude * u + corner * before
                    here = fx[f, x, ys, :]
                    carried[f], carried[5 + f] = ratio * (u + here), here
            return tuple(carried)

        def back(step, carried):
            carried = list(carried)
            for inner in range(unroll):
                x = size_x - 1 - (step * unroll + inner)
                for f in range(fields):
                    v, after = carried[f], carried[5 + f]
                    tend[f, x, ys, :] = amplitude * v + corner * after - tend[f, x, ys, :]
                    here = fx[f, x, ys, :]
                    carried[f], carried[5 + f] = ratio * (v + here), here
            return tuple(carried)

        for side, body in enumerate((ahead, back)):
            start = [xn_in[side, kind, f, ys, :] for kind in range(2) for f in range(fields)]
            lax.fori_loop(0, size_x // unroll, body, tuple(start))
        return 0

    lax.fori_loop(0, size_y // 8, scan_chunk, 0)

    for copy in xo + io:
        copy.wait()
    carry_x[...] = xo_in[...]
    carry_f[...] = io_in[...]


def filter_kernel(rows, den, mom, ene, part, carry_x, carry_f, wtab, tend, after, middle):
    fields, size_x = part.shape[:2]
    filter_ratio, gain = decay(filter_alpha)
    straight = 0.5 * (0.5 + filter_alpha) / filter_alpha
    amplitude = (0.5 + filter_alpha - straight) * gain
    unroll = 4

    def chunk(ref, side, f):
        return jnp.concatenate([ref[o, side, rows * f : rows * f + rows, :] for o in range(ref.shape[0])], axis=0)

    far_l = [chunk(carry_x, 0, f) for f in range(fields)]
    far_r = [chunk(carry_x, 1, f) for f in range(fields)]

    def ahead(step, carried):
        carried = list(carried)
        for inner in range(unroll):
            x = step * unroll + inner
            state = (den[x], mom[0, x], mom[1, x], mom[2, x], ene[x])
            gain_l, gain_r = wtab[6, x], wtab[7, x]
            for f in range(fields):
                rate = part[f, x] - gain_l * far_l[f] + gain_r * far_r[f]
                tend[f, x] = rate
                value = state[f] + time_step * rate
                middle[f, x] = value
                after[f, x] = (straight + amplitude) * value + amplitude * carried[f]
                carried[f] = filter_ratio * (carried[f] + value)
        return tuple(carried)

    def back(step, carried):
        carried = list(carried)
        for inner in range(unroll):
            x = size_x - 1 - (step * unroll + inner)
            for f in range(fields):
                after[f, x] += amplitude * carried[f]
                carried[f] = filter_ratio * (carried[f] + middle[f, x])
        return tuple(carried)

    for side, body in enumerate((ahead, back)):
        lax.fori_loop(0, size_x // unroll, body, tuple(chunk(carry_f, side, f) for f in range(fields)))


def solution(mesh):
    nx, ny, nz = mesh.shape["gx"], mesh.shape["gy"], mesh.shape["gz"]

    def on_device(density, momentum, energy, metric):
        size_x, size_y, size_z = density.shape
        fields = 5
        rows = size_y // nx
        float32 = jnp.float32
        ky, py = wall_tables(ny, size_y)
        kz, qz, pz = span_tables(nz, size_z)
        wtab = stream_weights(size_x).astype(np.float32)
        cells = (fields, size_x, size_y, size_z)
        owned = (nx, 2, fields * rows, size_z)
        vmem = pl.BlockSpec(memory_space=pltpu.VMEM)
        anywhere = pl.BlockSpec(memory_space=pl.ANY)
        copies = 2 + 4 * (nx - 1) + 6 + 2 * (nz - 1)
        part, carry_x, carry_f = pl.pallas_call(
            functools.partial(exchange_kernel, nx, ny, nz),
            out_shape=[
                jax.ShapeDtypeStruct(cells, float32),
                jax.ShapeDtypeStruct(owned, float32),
                jax.ShapeDtypeStruct(owned, float32),
            ],
            in_specs=[vmem, vmem, vmem, vmem, pl.BlockSpec(memory_space=pltpu.SMEM), anywhere, anywhere, vmem, vmem, vmem],
            out_specs=[vmem, vmem, vmem],
            scratch_shapes=[
                pltpu.VMEM(cells, float32),
                pltpu.VMEM(cells, float32),
                pltpu.VMEM(cells, float32),
                pltpu.VMEM(ky.shape[1:], float32),
                pltpu.VMEM(py.shape[1:], float32),
                pltpu.VMEM((2, fields, size_y, size_z), float32),
                pltpu.VMEM((16, size_y, size_z), float32),
                pltpu.VMEM((2, 8, size_y, size_z), float32),
                pltpu.VMEM((16, size_y, size_z), float32),
                pltpu.VMEM((2, 8, size_y, size_z), float32),
                pltpu.VMEM((4, 16, size_z), float32),
                pltpu.VMEM((8, 16, size_z), float32),
                pltpu.VMEM((nz, 8, 8 * size_y), float32),
                pltpu.VMEM((4, fields, size_x, size_z), float32),
                pltpu.VMEM((8, fields, size_x, size_z), float32),
                pltpu.VMEM((nz, fields, 8, size_x // 2 * size_y), float32),
                pltpu.VMEM((2, 2, fields, size_y, size_z), float32),
                pltpu.VMEM((2, 2, fields, size_y, size_z), float32),
                pltpu.VMEM(owned, float32),
                pltpu.VMEM(owned, float32),
                pltpu.VMEM(owned, float32),
                pltpu.VMEM(owned, float32),
                pltpu.VMEM(owned, float32),
                pltpu.VMEM(owned, float32),
                pltpu.VMEM(owned, float32),
                pltpu.VMEM(owned, float32),
                pltpu.SemaphoreType.DMA((2,)),
                pltpu.SemaphoreType.DMA((copies,)),
                pltpu.SemaphoreType.DMA((copies,)),
            ],
            compiler_params=pltpu.CompilerParams(
                collective_id=0, has_side_effects=True, vmem_limit_bytes=48 * 1024 * 1024
            ),
            cost_estimate=pl.CostEstimate(flops=4 * 10**9, bytes_accessed=10**7, transcendentals=0),
        )(
            density,
            momentum,
            energy,
            metric.reshape(1, -1),
            jnp.asarray(wtab),
            jnp.asarray(ky),
            jnp.asarray(py),
            jnp.asarray(kz),
            jnp.asarray(qz),
            jnp.asarray(pz),
        )
        owners = 8 // rows
        field_block = pl.BlockSpec((fields, size_x, 8, size_z), lambda i: (0, 0, i, 0))
        scalar_block = pl.BlockSpec((size_x, 8, size_z), lambda i: (0, i, 0))
        carry_block = pl.BlockSpec((owners, 2, fields * rows, size_z), lambda i: (i, 0, 0, 0))
        return pl.pallas_call(
            functools.partial(filter_kernel, rows),
            grid=(size_y // 8,),
            out_shape=[jax.ShapeDtypeStruct(cells, float32), jax.ShapeDtypeStruct(cells, float32)],
            in_specs=[
                scalar_block,
                pl.BlockSpec((3, size_x, 8, size_z), lambda i: (0, 0, i, 0)),
                scalar_block,
                field_block,
                carry_block,
                carry_block,
                pl.BlockSpec(memory_space=pltpu.SMEM),
            ],
            out_specs=[field_block, field_block],
            scratch_shapes=[pltpu.VMEM((fields, size_x, 8, size_z), float32)],
            compiler_params=pltpu.CompilerParams(vmem_limit_bytes=32 * 1024 * 1024),
            cost_estimate=pl.CostEstimate(flops=10**7, bytes_accessed=10**7, transcendentals=0),
        )(density, momentum, energy, part, carry_x, carry_f, jnp.asarray(wtab))

    return jax.shard_map(
        on_device,
        mesh=mesh,
        in_specs=(P("gx", "gy", "gz"), P(None, "gx", "gy", "gz"), P("gx", "gy", "gz"), P()),
        out_specs=(P(None, "gx", "gy", "gz"), P(None, "gx", "gy", "gz")),
        check_vma=False,
    )
```

```python
import functools

import jax
import jax.numpy as jnp
import numpy as np
from jax import lax
from jax.experimental import pallas as pl
from jax.experimental.pallas import tpu as pltpu
from jax.sharding import PartitionSpec as P

heat_ratio = 1.4
compact_alpha = 1.0 / 3.0
filter_alpha = 0.499
time_step = 0.05
near_weight = 7.0 / 9.0
wide_weight = 1.0 / 36.0
bfloat16 = jnp.bfloat16
MESH = pl.DeviceIdType.MESH
KINDS_Y = ((1, "last"), (1, "ml"), (1, "mr"), (2, "ml"), (2, "mr"), (3, "ml"), (3, "mr"), (3, "first"))


def decay(alpha):
    root = np.sqrt(1.0 - 4.0 * alpha * alpha)
    return (-1.0 + root) / (2.0 * alpha), 1.0 / root


def compact_kernel():
    ratio, gain = decay(compact_alpha)

    def green(n):
        return gain * ratio ** abs(n)

    def kernel(d):
        return near_weight * (green(d + 1) - green(d - 1)) + wide_weight * (green(d + 2) - green(d - 2))

    amplitude = kernel(2) / ratio**2
    return ratio, amplitude, kernel(1) - amplitude * ratio


def local_compact(size):
    ratio, amplitude, corner = compact_kernel()
    table = np.zeros((size, size))
    for i in range(size):
        for j in range(size):
            d = abs(i - j)
            if d:
                value = amplitude * ratio**d + (corner if d == 1 else 0.0)
                table[i, j] = value if i > j else -value
    return table


def table_thomas(lower_band, main_band, upper_band, source):
    count = source.shape[0]
    c_all = np.zeros(count)
    d_all = np.zeros(source.shape)
    c_prev = 0.0
    d_prev = np.zeros(source.shape[1:])
    for place in range(count):
        denom = main_band[place] - lower_band[place] * c_prev
        c_prev = upper_band[place] / denom
        d_prev = (source[place] - lower_band[place] * d_prev) / denom
        c_all[place] = c_prev
        d_all[place] = d_prev
    solved = np.zeros(source.shape)
    x_next = np.zeros(source.shape[1:])
    for place in range(count - 1, -1, -1):
        x_next = d_all[place] - c_all[place] * x_next
        solved[place] = x_next
    return solved


def wall_bands(total):
    lower = np.full(total, compact_alpha)
    upper = np.full(total, compact_alpha)
    lower[0], lower[1], lower[total - 2], lower[total - 1] = 0.0, 0.25, 0.25, 2.0
    upper[0], upper[1], upper[total - 2], upper[total - 1] = 2.0, 0.25, 0.25, 0.0
    return lower, upper


def wall_table(total):
    lower, upper = wall_bands(total)
    stencil = np.zeros((total, total))
    for i in range(2, total - 2):
        stencil[i, i + 1], stencil[i, i - 1] = near_weight, -near_weight
        stencil[i, i + 2], stencil[i, i - 2] = wide_weight, -wide_weight
    for i in (1, total - 2):
        stencil[i, i + 1], stencil[i, i - 1] = 0.75, -0.75
    stencil[0, :3] = (-2.5, 2.0, 0.5)
    stencil[total - 1, total - 3 :] = (-0.5, -2.0, 2.5)
    return table_thomas(lower, np.ones(total), upper, stencil)


@functools.cache
def wall_tables(blocks, size):
    total = blocks * size
    table = wall_table(total)
    lower, upper = wall_bands(total)
    down = np.zeros(total)
    for i in range(total - 1, 0, -1):
        down[i - 1] = -lower[i] / (1.0 + upper[i] * down[i])
    up = np.zeros(total)
    for i in range(total - 1):
        up[i + 1] = -upper[i] / (1.0 + lower[i] * up[i])
    carry_l, carry_r, corner_l, corner_r = [], [], [], []
    moment_l, moment_r = np.zeros((blocks, size)), np.zeros((blocks, size))
    for b in range(blocks):
        head, tail = b * size, b * size + size - 1
        carry_l.append(np.concatenate([[1.0], np.cumprod(down[head:tail])]))
        carry_r.append(np.concatenate([[1.0], np.cumprod(up[head + 1 : tail + 1][::-1])])[::-1])
        corner_l.append(table[head, head - 1] - table[head + 1, head - 1] / down[head] if b else 0.0)
        corner_r.append(table[tail, tail + 1] - table[tail - 1, tail + 1] / up[tail] if b < blocks - 1 else 0.0)
        if b < blocks - 1:
            to = tail + 1
            moment_l[b] = table[to, head:to]
            moment_l[b, size - 1] = table[to + 1, tail] / down[to]
        if b:
            to = head - 1
            moment_r[b] = table[to, head : tail + 1]
            moment_r[b, 0] = table[to - 1, head] / up[to]
    apply = np.zeros((blocks, 8 * size + 32, 8 * size))
    carry = np.zeros((blocks, 8 * size, 8 * len(KINDS_Y)))
    eye = np.eye(8)
    for b in range(blocks):
        rows = slice(b * size, (b + 1) * size)
        apply[b, : 8 * size] = np.kron(eye, table[rows, rows])
        first, last = np.eye(size)[0], np.eye(size)[size - 1]
        for kind, weights in enumerate((last, moment_l[b], moment_r[b], first)):
            apply[b, 8 * size + 8 * kind : 8 * size + 8 * kind + 8] = np.kron(eye, weights[None])
        for place, (offset, kind) in enumerate(KINDS_Y):
            column = np.zeros(size)
            if b - offset >= 0:
                if kind == "ml":
                    scale = 1.0
                    for c in range(b - offset + 1, b):
                        scale *= np.prod(down[c * size : (c + 1) * size])
                    column = scale * carry_l[b]
                elif kind == "last" and offset == 1:
                    column[0] = corner_l[b]
            else:
                distance = blocks - offset
                if kind == "mr":
                    scale = 1.0
                    for c in range(b + 1, b + distance):
                        scale *= np.prod(up[c * size : (c + 1) * size])
                    column = scale * carry_r[b]
                elif kind == "first" and distance == 1:
                    column[size - 1] = corner_r[b]
            carry[b, :, 8 * place : 8 * place + 8] = np.kron(eye, column[:, None])
    return apply.astype(np.float32), np.concatenate([carry] * 3, axis=2).astype(np.float32)


def table_split(table):
    high = table.astype(bfloat16)
    return high, (table - high.astype(np.float64)).astype(bfloat16)


@functools.cache
def span_tables(blocks, size):
    ratio, amplitude, corner = compact_kernel()
    places = np.arange(size)
    images = 1.0 / (1.0 - ratio ** (blocks * size))
    moments = np.zeros((4, size))
    moments[0, size - 1] = 1.0
    moments[1] = ratio ** (size - places)
    moments[2] = ratio ** (places + 1.0)
    moments[3, 0] = 1.0
    carries = np.zeros((blocks, 4, size))
    for slot in range(blocks):
        behind = slot if slot else blocks
        ahead = blocks - slot
        carries[slot, 1] = amplitude * images * ratio ** (size * (behind - 1.0)) * ratio**places
        carries[slot, 2] = -amplitude * images * ratio ** (size * (ahead - 1.0)) * ratio ** (size - 1.0 - places)
        if behind == 1:
            carries[slot, 0, 0] = corner
        if ahead == 1:
            carries[slot, 3, size - 1] = -corner
    both_moments = np.zeros((8, 2 * size))
    both_moments[:4, :size] = moments
    both_moments[4:, size:] = moments
    both_carries = np.zeros((blocks, 8, 2 * size))
    both_carries[:, :4, :size] = carries
    both_carries[:, 4:, size:] = carries
    local_high, local_low = table_split(local_compact(size).T)
    carry_high, carry_low = table_split(both_carries.reshape(8 * blocks, 2 * size))
    return (
        np.block([[local_high, local_low], [local_high, np.zeros_like(local_low)]]),
        np.concatenate(table_split(both_moments)),
        np.concatenate([carry_high, carry_high, carry_low]),
    )


def stream_weights(size):
    ratio, amplitude, _ = compact_kernel()
    filter_ratio, _ = decay(filter_alpha)
    places = np.arange(size)
    weight_u = filter_ratio ** (size - places)
    weight_v = filter_ratio ** (places + 1.0)
    local = local_compact(size)
    return np.stack(
        [
            weight_u,
            weight_v,
            -time_step * (weight_u @ local),
            -time_step * (weight_v @ local),
            ratio ** (size - places),
            ratio ** (places + 1.0),
        ]
    )


def split(values):
    high = values.astype(bfloat16)
    return high, (values - high.astype(jnp.float32)).astype(bfloat16)


def product(left, right, sides=((1,), (0,))):
    return lax.dot_general(left, right, (sides, ((), ())), preferred_element_type=jnp.float32)


def exchange_kernel(
    nx,
    ny,
    nz,
    den_hbm,
    mom_hbm,
    ene_hbm,
    metric_hbm,
    wtab_hbm,
    ky_hbm,
    py_hbm,
    kz_hbm,
    qz_hbm,
    pz_hbm,
    tend,
    carry_x,
    carry_f,
    den,
    mom,
    ene,
    metric,
    wtab,
    ky,
    py,
    kz,
    qz,
    pz,
    ky_high,
    ky_low,
    py_both,
    fx,
    fy,
    fz,
    uv0,
    sy,
    sz,
    dys,
    dzs,
    ys_out,
    ys_in,
    zs_in,
    yb_out,
    yb_in,
    zm_in,
    xn_out,
    xn_in,
    xm_out,
    xm_in,
    uv_out,
    uv_in,
    xo_out,
    xo_in,
    io_out,
    io_in,
    load_sem,
    send_sem,
    recv_sem,
):
    fields, size_x, size_y, size_z = fx.shape
    me_x, me_y, me_z = lax.axis_index("gx"), lax.axis_index("gy"), lax.axis_index("gz")
    rows = size_y // nx
    ratio, amplitude, corner = compact_kernel()
    weights = stream_weights(size_x)
    filter_ratio, _ = decay(filter_alpha)

    def along(axis, offset):
        me, count = {"gx": (me_x, nx), "gy": (me_y, ny), "gz": (me_z, nz)}[axis]
        return lax.rem(me + offset + count, count)

    sources = (wtab_hbm, den_hbm, mom_hbm, ene_hbm, ky_hbm.at[me_y], py_hbm.at[me_y], metric_hbm, kz_hbm, qz_hbm, pz_hbm)
    targets = (wtab, den, mom, ene, ky, py, metric, kz, qz, pz)
    loads = [
        pltpu.make_async_copy(source, target, load_sem.at[place])
        for place, (source, target) in enumerate(zip(sources, targets))
    ]
    for load in loads:
        load.start()

    barrier = pltpu.get_barrier_semaphore()
    for axis, count in (("gx", nx), ("gy", ny), ("gz", nz)):
        for offset in range(1, count):
            pl.semaphore_signal(barrier, inc=1, device_id={axis: along(axis, offset)}, device_id_type=MESH)

    next_sem = [0]

    def remote(src, dst, axis, offset):
        place = next_sem[0]
        next_sem[0] = place + 1
        return pltpu.make_async_remote_copy(
            src_ref=src,
            dst_ref=dst,
            send_sem=send_sem.at[place],
            recv_sem=recv_sem.at[place],
            device_id={axis: along(axis, offset)},
            device_id_type=MESH,
        )

    for load in loads[:4]:
        load.wait()

    unroll = 4

    def flux_chunk(chunk, _):
        ys = pl.ds(pl.multiple_of(chunk * 8, 8), 8)

        def cells(step, acc):
            acc = list(acc)
            for inner in range(unroll):
                x = step * unroll + inner
                w = [wtab[k, x] for k in range(6)]
                rho, energy = den[x, ys, :], ene[x, ys, :]
                m = [mom[j, x, ys, :] for j in range(3)]
                inverse = 1.0 / rho
                v = [m[j] * inverse for j in range(3)]
                own = [m[j] * v[j] for j in range(3)]
                pressure = (heat_ratio - 1.0) * (energy - 0.5 * (own[0] + own[1] + own[2]))
                m12, m13, m23 = m[0] * v[1], m[0] * v[2], m[1] * v[2]
                total = energy + pressure
                flux_x = (m[0], own[0] + pressure, m12, m13, total * v[0])
                flux_y = (m[1], m12, own[1] + pressure, m23, total * v[1])
                flux_z = (m[2], m13, m23, own[2] + pressure, total * v[2])
                state = (rho, m[0], m[1], m[2], energy)
                for f in range(fields):
                    fx[f, x, ys, :] = flux_x[f]
                    fy[f, x, ys, :] = flux_y[f]
                    fz[f, x, ys, :] = flux_z[f]
                    acc[f] = acc[f] + w[0] * state[f] + w[2] * flux_x[f]
                    acc[5 + f] = acc[5 + f] + w[1] * state[f] + w[3] * flux_x[f]
                    acc[10 + f] = acc[10 + f] + w[4] * flux_x[f]
                    acc[15 + f] = acc[15 + f] + w[5] * flux_x[f]
            return tuple(acc)

        zero = jnp.zeros((8, size_z), jnp.float32)
        acc = lax.fori_loop(0, size_x // unroll, cells, (zero,) * 20)
        for f in range(fields):
            uv0[0, f, ys, :] = acc[f]
            uv0[1, f, ys, :] = acc[5 + f]
            xn_out[0, 0, f, ys, :] = acc[10 + f]
            xn_out[0, 1, f, ys, :] = fx[f, size_x - 1, ys, :]
            xn_out[1, 0, f, ys, :] = acc[15 + f]
            xn_out[1, 1, f, ys, :] = fx[f, 0, ys, :]

        def sums(step, acc):
            acc = list(acc)
            for inner in range(unroll):
                x = step * unroll + inner
                w = [wtab[k, x] for k in range(2)]
                for f in range(fields):
                    value_y, value_z = fy[f, x, ys, :], fz[f, x, ys, :]
                    acc[f] = acc[f] + w[0] * value_y
                    acc[5 + f] = acc[5 + f] + w[1] * value_y
                    acc[10 + f] = acc[10 + f] + w[0] * value_z
                    acc[15 + f] = acc[15 + f] + w[1] * value_z
            return tuple(acc)

        acc = lax.fori_loop(0, size_x // unroll, sums, (zero,) * 20)
        for f in range(fields):
            sy[f, ys, :] = acc[f]
            sy[5 + f, ys, :] = acc[5 + f]
            sz[0, f, ys, :] = acc[10 + f]
            sz[1, f, ys, :] = acc[15 + f]
        return 0

    lax.fori_loop(0, size_y // 8, flux_chunk, 0)
    sy[10:16] = jnp.zeros((6, size_y, size_z), jnp.float32)
    sz[:, 5:8] = jnp.zeros((2, 3, size_y, size_z), jnp.float32)

    pl.semaphore_wait(barrier, nx + ny + nz - 3)

    xn = [
        remote(xn_out.at[0], xn_in.at[0], "gx", 1),
        remote(xn_out.at[1], xn_in.at[1], "gx", -1),
    ]
    for copy in xn:
        copy.start()
    for owner in range(nx):
        for side in range(2):
            for f in range(fields):
                xm_out[owner, side, rows * f : rows * f + rows, :] = xn_out[
                    side, 0, f, rows * owner : rows * owner + rows, :
                ]
    xm = [remote(xm_out.at[along("gx", k)], xm_in.at[k], "gx", k) for k in range(1, nx)]
    for copy in xm:
        copy.start()
    xm_in[0] = xm_out[me_x]

    for load in loads[4:]:
        load.wait()
    shape = (8 * size_y, ny * size_y)
    row_place = lax.broadcasted_iota(jnp.int32, shape, 0)
    col_place = lax.broadcasted_iota(jnp.int32, shape, 1)
    mine = col_place == me_y * size_y + lax.rem(row_place, size_y)
    metric_rows = jnp.sum(jnp.where(mine, metric[...], 0.0), axis=1, keepdims=True)
    ky[: 8 * size_y, :] = ky[: 8 * size_y, :] * metric_rows
    ky_high[...], ky_low[...] = split(ky[...])
    high, low = split(py[...] * metric_rows)
    py_both[...] = jnp.where(lax.broadcasted_iota(jnp.int32, py.shape, 1) < 128, high, low)

    def apply_wall(first, second):
        cells = jnp.concatenate(
            [first.reshape(8 * size_y, size_z), second.reshape(8 * size_y, size_z)], axis=1
        )
        high, low = split(cells)
        result = product(ky_high[...], high) + product(ky_high[...], low) + product(ky_low[...], high)
        return [
            (
                result[: 8 * size_y, lanes].reshape(8, size_y, size_z),
                result[8 * size_y :, lanes].reshape(4, 8, size_z),
            )
            for lanes in (slice(0, size_z), slice(size_z, 2 * size_z))
        ]

    def wall_carries(first, second):
        cells = jnp.concatenate([first.reshape(64, size_z), second.reshape(64, size_z)], axis=1)
        high, low = split(cells)
        return product(py_both[...], jnp.concatenate([high, low, high], axis=0))

    def span_local(cells):
        result = product(jnp.concatenate(split(cells), axis=1), kz[...])
        return result[:, :size_z] + result[:, size_z:]

    def span_moments(first, second):
        high, low = split(jnp.concatenate([first, second], axis=1))
        from_high = product(qz[...], high, ((1,), (1,)))
        from_low = product(qz[...], low, ((1,), (1,)))
        return from_high[:8] + from_high[8:] + (from_low[:8] + from_low[8:])

    def span_carries(received):
        high, low = split(received)
        return product(jnp.concatenate([high, low, high], axis=0), pz[...], ((0,), (0,)))

    for group, (local, moments) in enumerate(apply_wall(sy[0:8], sy[8:16])):
        dys[8 * group : 8 * group + 8] = local
        ys_out[:, 8 * group : 8 * group + 8, :] = moments
    ys = [
        remote(ys_out.at[pl.ds(0, 3)], ys_in.at[pl.ds(0, 3)], "gy", 1),
        remote(ys_out.at[pl.ds(1, 2)], ys_in.at[pl.ds(3, 2)], "gy", 2),
        remote(ys_out.at[pl.ds(1, 3)], ys_in.at[pl.ds(5, 3)], "gy", 3),
    ]
    for copy in ys:
        copy.start()
    zs_in[0] = span_moments(sz[0].reshape(8 * size_y, size_z), sz[1].reshape(8 * size_y, size_z))
    zs = [remote(zs_in.at[0], zs_in.at[k], "gz", k) for k in range(1, nz)]
    for copy in zs:
        copy.start()
    dzs[...] = span_local(sz[...].reshape(16 * size_y, size_z)).reshape(2, 8, size_y, size_z)

    def wall_field(f, _):
        for part in range(size_x // 16):
            pair = [pl.ds(16 * part + 8 * side, 8) for side in range(2)]
            for xs, (local, moments) in zip(pair, apply_wall(fy[f, pair[0]], fy[f, pair[1]])):
                tend[f, xs] = local
                yb_out[:, f, xs, :] = moments
        return 0

    lax.fori_loop(0, fields, wall_field, 0)
    yb = [
        remote(yb_out.at[pl.ds(0, 3)], yb_in.at[pl.ds(0, 3)], "gy", 1),
        remote(yb_out.at[pl.ds(1, 2)], yb_in.at[pl.ds(3, 2)], "gy", 2),
        remote(yb_out.at[pl.ds(1, 3)], yb_in.at[pl.ds(5, 3)], "gy", 3),
    ]
    for copy in yb:
        copy.start()
    half = size_x // 2

    def span_field(f, _):
        pair = [fz[f, pl.ds(part * half, half)].reshape(half * size_y, size_z) for part in range(2)]
        zm_in[0, f] = span_moments(*pair)
        return 0

    lax.fori_loop(0, fields, span_field, 0)
    zm = [remote(zm_in.at[0], zm_in.at[k], "gz", k) for k in range(1, nz)]
    for copy in zm:
        copy.start()

    for copy in xn + ys + zs:
        copy.wait()
    powers = (ratio ** np.arange(size_x), ratio ** (size_x - 1.0 - np.arange(size_x)))
    span = span_carries(zs_in[...].reshape(8 * nz, 8 * size_y))
    wall = wall_carries(ys_in[:, 0:8, :], ys_in[:, 8:16, :])
    for side in range(2):
        gains = [
            amplitude * float(weights[side] @ powers[0]),
            corner * float(weights[side][0]),
            -amplitude * float(weights[side] @ powers[1]),
            -corner * float(weights[side][size_x - 1]),
        ]
        for f in range(fields):
            unit = 5 * side + f
            place, lane = (unit % 8) * size_y, (unit // 8) * size_z
            change = dys[unit] + wall[place : place + size_y, lane : lane + size_z]
            change = change + dzs[side, f] + span[f * size_y : (f + 1) * size_y, side * size_z : (side + 1) * size_z]
            for gain, value in zip(gains, (xn_in[0, 0, f], xn_in[0, 1, f], xn_in[1, 0, f], xn_in[1, 1, f])):
                change = change + gain * value
            value = uv0[side, f] - time_step * change
            for owner in range(nx):
                uv_out[owner, side, rows * f : rows * f + rows, :] = value[rows * owner : rows * owner + rows]
    uv = [remote(uv_out.at[along("gx", k)], uv_in.at[k], "gx", k) for k in range(1, nx)]
    for copy in uv:
        copy.start()
    uv_in[0] = uv_out[me_x]

    def sweep(behind, power, values):
        step = 1 if behind else -1
        total = values[0] if behind else values[nx - 1]
        for k in range(1, nx):
            total = total + float(power**k) * (values[k] if behind else values[nx - 1 - k])
        total = total * float(1.0 / (1.0 - power**nx))
        place = nx - 1 if behind else 0
        result = [None] * nx
        result[place] = total
        for _ in range(nx - 1):
            total = values[place] + float(power) * total
            place = place - step
            result[place] = total
        return result

    for copy in xm:
        copy.wait()
    power = ratio**size_x
    near_l = sweep(True, power, [xm_in[k, 0] for k in range(nx)])
    near_r = sweep(False, power, [xm_in[k, 1] for k in range(nx)])
    for k in range(nx):
        xo_out[k, 0] = float(power) * near_l[(k + 1) % nx]
        xo_out[k, 1] = float(power) * near_r[(k - 1) % nx]
    xo = [remote(xo_out.at[k], xo_in.at[me_x], "gx", -k) for k in range(1, nx)]
    for copy in xo:
        copy.start()
    xo_in[me_x] = xo_out[0]

    def span_cells(f, _):
        for part in range(size_x // 8):
            xs = pl.ds(8 * part, 8)
            tend[f, xs] += span_local(fz[f, xs].reshape(8 * size_y, size_z)).reshape(8, size_y, size_z)
        return 0

    lax.fori_loop(0, fields, span_cells, 0)

    def scan_chunk(chunk, _):
        ys = pl.ds(pl.multiple_of(chunk * 8, 8), 8)

        def scan(side, step, carried):
            carried = list(carried)
            for inner in range(unroll):
                x = step * unroll + inner
                x = size_x - 1 - x if side else x
                gains = (-amplitude, -corner) if side else (amplitude, corner)
                for f in range(fields):
                    total, last = carried[f], carried[5 + f]
                    tend[f, x, ys, :] += gains[0] * total + gains[1] * last
                    here = fx[f, x, ys, :]
                    carried[f], carried[5 + f] = ratio * (total + here), here
            return tuple(carried)

        for side in range(2):
            start = [xn_in[side, kind, f, ys, :] for kind in range(2) for f in range(fields)]
            lax.fori_loop(0, size_x // unroll, functools.partial(scan, side), tuple(start))
        return 0

    lax.fori_loop(0, size_y // 8, scan_chunk, 0)

    for copy in uv:
        copy.wait()
    filter_power = filter_ratio**size_x
    for side in range(2):
        gain_l = -time_step * amplitude * float(weights[side] @ powers[0])
        gain_r = time_step * amplitude * float(weights[side] @ powers[1])
        values = [uv_in[k, side] + gain_l * xo_out[k, 0] + gain_r * xo_out[k, 1] for k in range(nx)]
        for k, value in enumerate(sweep(side == 0, filter_power, values)):
            io_out[k, side] = value
    io = [remote(io_out.at[k], io_in.at[me_x], "gx", -k) for k in range(1, nx)]
    for copy in io:
        copy.start()
    io_in[me_x] = io_out[0]

    for copy in yb + zm:
        copy.wait()

    def carries(f, _):
        both = span_carries(zm_in[:, f].reshape(8 * nz, half * size_y))
        for part in range(size_x // 16):
            pair = [pl.ds(16 * part + 8 * side, 8) for side in range(2)]
            wall = wall_carries(yb_in[:, f, pair[0], :], yb_in[:, f, pair[1], :])
            for side, xs in enumerate(pair):
                row = (16 * part + 8 * side) % half * size_y
                lane = (16 * part + 8 * side) // half * size_z
                change = wall[:, side * size_z : (side + 1) * size_z]
                change = change + both[row : row + 8 * size_y, lane : lane + size_z]
                tend[f, xs] += change.reshape(8, size_y, size_z)
        return 0

    lax.fori_loop(0, fields, carries, 0)

    for copy in xo + io:
        copy.wait()
    carry_x[...] = xo_in[...]
    carry_f[...] = io_in[...]


def filter_kernel(rows, den, mom, ene, part, carry_x, carry_f, tend, after, middle):
    fields, size_x = part.shape[:2]
    filter_ratio, gain = decay(filter_alpha)
    straight = 0.5 * (0.5 + filter_alpha) / filter_alpha
    amplitude = (0.5 + filter_alpha - straight) * gain
    unroll = 4

    def chunk(ref, side, f):
        return jnp.concatenate([ref[o, side, rows * f : rows * f + rows, :] for o in range(ref.shape[0])], axis=0)

    ratio, far_gain, _ = compact_kernel()
    start = [chunk(carry_f, 0, f) for f in range(fields)]
    start += [far_gain * chunk(carry_x, 0, f) for f in range(fields)]
    start += [float(far_gain * ratio ** (size_x - 1)) * chunk(carry_x, 1, f) for f in range(fields)]

    def ahead(step, carried):
        carried = list(carried)
        for inner in range(unroll):
            x = step * unroll + inner
            state = (den[x], mom[0, x], mom[1, x], mom[2, x], ene[x])
            for f in range(fields):
                far_l, far_r = carried[5 + f], carried[10 + f]
                rate = far_r - far_l - part[f, x]
                carried[5 + f], carried[10 + f] = ratio * far_l, (1.0 / ratio) * far_r
                tend[f, x] = rate
                value = state[f] + time_step * rate
                middle[f, x] = value
                after[f, x] = (straight + amplitude) * value + amplitude * carried[f]
                carried[f] = filter_ratio * (carried[f] + value)
        return tuple(carried)

    def back(step, carried):
        carried = list(carried)
        for inner in range(unroll):
            x = size_x - 1 - (step * unroll + inner)
            for f in range(fields):
                after[f, x] += amplitude * carried[f]
                carried[f] = filter_ratio * (carried[f] + middle[f, x])
        return tuple(carried)

    lax.fori_loop(0, size_x // unroll, ahead, tuple(start))
    lax.fori_loop(0, size_x // unroll, back, tuple(chunk(carry_f, 1, f) for f in range(fields)))


def solution(mesh):
    nx, ny, nz = mesh.shape["gx"], mesh.shape["gy"], mesh.shape["gz"]

    def on_device(density, momentum, energy, metric):
        size_x, size_y, size_z = density.shape
        fields = 5
        rows = size_y // nx
        float32 = jnp.float32
        ky, py = wall_tables(ny, size_y)
        kz, qz, pz = span_tables(nz, size_z)
        wtab = stream_weights(size_x).astype(np.float32)
        cells = (fields, size_x, size_y, size_z)
        owned = (nx, 2, fields * rows, size_z)
        vmem = pl.BlockSpec(memory_space=pltpu.VMEM)
        stays = pl.BlockSpec(memory_space=pltpu.HBM)
        copies = 2 + 4 * (nx - 1) + 6 + 2 * (nz - 1)
        part, carry_x, carry_f = pl.pallas_call(
            functools.partial(exchange_kernel, nx, ny, nz),
            out_shape=[
                jax.ShapeDtypeStruct(cells, float32),
                jax.ShapeDtypeStruct(owned, float32),
                jax.ShapeDtypeStruct(owned, float32),
            ],
            in_specs=[stays] * 10,
            out_specs=[vmem, vmem, vmem],
            scratch_shapes=[
                pltpu.VMEM(cells[1:], float32),
                pltpu.VMEM((3,) + cells[1:], float32),
                pltpu.VMEM(cells[1:], float32),
                pltpu.VMEM((1, ny * size_y), float32),
                pltpu.SMEM(wtab.shape, float32),
                pltpu.VMEM(ky.shape[1:], float32),
                pltpu.VMEM(py.shape[1:], float32),
                pltpu.VMEM(kz.shape, bfloat16),
                pltpu.VMEM(qz.shape, bfloat16),
                pltpu.VMEM(pz.shape, bfloat16),
                pltpu.VMEM(ky.shape[1:], bfloat16),
                pltpu.VMEM(ky.shape[1:], bfloat16),
                pltpu.VMEM(py.shape[1:], bfloat16),
                pltpu.VMEM(cells, float32),
                pltpu.VMEM(cells, float32),
                pltpu.VMEM(cells, float32),
                pltpu.VMEM((2, fields, size_y, size_z), float32),
                pltpu.VMEM((16, size_y, size_z), float32),
                pltpu.VMEM((2, 8, size_y, size_z), float32),
                pltpu.VMEM((16, size_y, size_z), float32),
                pltpu.VMEM((2, 8, size_y, size_z), float32),
                pltpu.VMEM((4, 16, size_z), float32),
                pltpu.VMEM((8, 16, size_z), float32),
                pltpu.VMEM((nz, 8, 8 * size_y), float32),
                pltpu.VMEM((4, fields, size_x, size_z), float32),
                pltpu.VMEM((8, fields, size_x, size_z), float32),
                pltpu.VMEM((nz, fields, 8, size_x // 2 * size_y), float32),
                pltpu.VMEM((2, 2, fields, size_y, size_z), float32),
                pltpu.VMEM((2, 2, fields, size_y, size_z), float32),
                pltpu.VMEM(owned, float32),
                pltpu.VMEM(owned, float32),
                pltpu.VMEM(owned, float32),
                pltpu.VMEM(owned, float32),
                pltpu.VMEM(owned, float32),
                pltpu.VMEM(owned, float32),
                pltpu.VMEM(owned, float32),
                pltpu.VMEM(owned, float32),
                pltpu.SemaphoreType.DMA((10,)),
                pltpu.SemaphoreType.DMA((copies,)),
                pltpu.SemaphoreType.DMA((copies,)),
            ],
            compiler_params=pltpu.CompilerParams(
                collective_id=0, has_side_effects=True, vmem_limit_bytes=24 * 1024 * 1024
            ),
            cost_estimate=pl.CostEstimate(flops=4 * 10**9, bytes_accessed=10**7, transcendentals=0),
        )(
            *[
                pltpu.with_memory_space_constraint(jnp.asarray(value), pltpu.HBM)
                for value in (density, momentum, energy, metric.reshape(1, -1), wtab, ky, py, kz, qz, pz)
            ]
        )
        owners = 8 // rows
        field_block = pl.BlockSpec((fields, size_x, 8, size_z), lambda i: (0, 0, i, 0))
        scalar_block = pl.BlockSpec((size_x, 8, size_z), lambda i: (0, i, 0))
        carry_block = pl.BlockSpec((owners, 2, fields * rows, size_z), lambda i: (i, 0, 0, 0))
        return pl.pallas_call(
            functools.partial(filter_kernel, rows),
            grid=(size_y // 8,),
            out_shape=[jax.ShapeDtypeStruct(cells, float32), jax.ShapeDtypeStruct(cells, float32)],
            in_specs=[
                scalar_block,
                pl.BlockSpec((3, size_x, 8, size_z), lambda i: (0, 0, i, 0)),
                scalar_block,
                field_block,
                carry_block,
                carry_block,
            ],
            out_specs=[field_block, field_block],
            scratch_shapes=[pltpu.VMEM((fields, size_x, 8, size_z), float32)],
            compiler_params=pltpu.CompilerParams(vmem_limit_bytes=12 * 1024 * 1024),
            cost_estimate=pl.CostEstimate(flops=10**7, bytes_accessed=10**7, transcendentals=0),
        )(density, momentum, energy, part, carry_x, carry_f)

    return jax.shard_map(
        on_device,
        mesh=mesh,
        in_specs=(P("gx", "gy", "gz"), P(None, "gx", "gy", "gz"), P("gx", "gy", "gz"), P()),
        out_specs=(P(None, "gx", "gy", "gz"), P(None, "gx", "gy", "gz")),
        check_vma=False,
    )
```

```python
import functools

import jax
import jax.numpy as jnp
import numpy as np
from jax import lax
from jax.experimental import pallas as pl
from jax.experimental.pallas import tpu as pltpu
from jax.sharding import PartitionSpec as P

heat_ratio = 1.4
compact_alpha = 1.0 / 3.0
filter_alpha = 0.499
time_step = 0.05
near_weight = 7.0 / 9.0
wide_weight = 1.0 / 36.0
bfloat16 = jnp.bfloat16
MESH = pl.DeviceIdType.MESH
KINDS_Y = ((1, "last"), (1, "ml"), (1, "mr"), (2, "ml"), (2, "mr"), (3, "ml"), (3, "mr"), (3, "first"))


def decay(alpha):
    root = np.sqrt(1.0 - 4.0 * alpha * alpha)
    return (-1.0 + root) / (2.0 * alpha), 1.0 / root


def compact_kernel():
    ratio, gain = decay(compact_alpha)

    def green(n):
        return gain * ratio ** abs(n)

    def kernel(d):
        return near_weight * (green(d + 1) - green(d - 1)) + wide_weight * (green(d + 2) - green(d - 2))

    amplitude = kernel(2) / ratio**2
    return ratio, amplitude, kernel(1) - amplitude * ratio


def local_compact(size):
    ratio, amplitude, corner = compact_kernel()
    table = np.zeros((size, size))
    for i in range(size):
        for j in range(size):
            d = abs(i - j)
            if d:
                value = amplitude * ratio**d + (corner if d == 1 else 0.0)
                table[i, j] = value if i > j else -value
    return table


def table_thomas(lower_band, main_band, upper_band, source):
    count = source.shape[0]
    c_all = np.zeros(count)
    d_all = np.zeros(source.shape)
    c_prev = 0.0
    d_prev = np.zeros(source.shape[1:])
    for place in range(count):
        denom = main_band[place] - lower_band[place] * c_prev
        c_prev = upper_band[place] / denom
        d_prev = (source[place] - lower_band[place] * d_prev) / denom
        c_all[place] = c_prev
        d_all[place] = d_prev
    solved = np.zeros(source.shape)
    x_next = np.zeros(source.shape[1:])
    for place in range(count - 1, -1, -1):
        x_next = d_all[place] - c_all[place] * x_next
        solved[place] = x_next
    return solved


def wall_bands(total):
    lower = np.full(total, compact_alpha)
    upper = np.full(total, compact_alpha)
    lower[0], lower[1], lower[total - 2], lower[total - 1] = 0.0, 0.25, 0.25, 2.0
    upper[0], upper[1], upper[total - 2], upper[total - 1] = 2.0, 0.25, 0.25, 0.0
    return lower, upper


def wall_table(total):
    lower, upper = wall_bands(total)
    stencil = np.zeros((total, total))
    for i in range(2, total - 2):
        stencil[i, i + 1], stencil[i, i - 1] = near_weight, -near_weight
        stencil[i, i + 2], stencil[i, i - 2] = wide_weight, -wide_weight
    for i in (1, total - 2):
        stencil[i, i + 1], stencil[i, i - 1] = 0.75, -0.75
    stencil[0, :3] = (-2.5, 2.0, 0.5)
    stencil[total - 1, total - 3 :] = (-0.5, -2.0, 2.5)
    return table_thomas(lower, np.ones(total), upper, stencil)


@functools.cache
def wall_tables(blocks, size):
    total = blocks * size
    table = wall_table(total)
    lower, upper = wall_bands(total)
    down = np.zeros(total)
    for i in range(total - 1, 0, -1):
        down[i - 1] = -lower[i] / (1.0 + upper[i] * down[i])
    up = np.zeros(total)
    for i in range(total - 1):
        up[i + 1] = -upper[i] / (1.0 + lower[i] * up[i])
    carry_l, carry_r, corner_l, corner_r = [], [], [], []
    moment_l, moment_r = np.zeros((blocks, size)), np.zeros((blocks, size))
    for b in range(blocks):
        head, tail = b * size, b * size + size - 1
        carry_l.append(np.concatenate([[1.0], np.cumprod(down[head:tail])]))
        carry_r.append(np.concatenate([[1.0], np.cumprod(up[head + 1 : tail + 1][::-1])])[::-1])
        corner_l.append(table[head, head - 1] - table[head + 1, head - 1] / down[head] if b else 0.0)
        corner_r.append(table[tail, tail + 1] - table[tail - 1, tail + 1] / up[tail] if b < blocks - 1 else 0.0)
        if b < blocks - 1:
            to = tail + 1
            moment_l[b] = table[to, head:to]
            moment_l[b, size - 1] = table[to + 1, tail] / down[to]
        if b:
            to = head - 1
            moment_r[b] = table[to, head : tail + 1]
            moment_r[b, 0] = table[to - 1, head] / up[to]
    apply = np.zeros((blocks, 8 * size + 32, 8 * size))
    carry = np.zeros((blocks, 8 * size, 8 * len(KINDS_Y)))
    eye = np.eye(8)
    for b in range(blocks):
        rows = slice(b * size, (b + 1) * size)
        apply[b, : 8 * size] = np.kron(eye, table[rows, rows])
        first, last = np.eye(size)[0], np.eye(size)[size - 1]
        for kind, weights in enumerate((last, moment_l[b], moment_r[b], first)):
            apply[b, 8 * size + 8 * kind : 8 * size + 8 * kind + 8] = np.kron(eye, weights[None])
        for place, (offset, kind) in enumerate(KINDS_Y):
            column = np.zeros(size)
            if b - offset >= 0:
                if kind == "ml":
                    scale = 1.0
                    for c in range(b - offset + 1, b):
                        scale *= np.prod(down[c * size : (c + 1) * size])
                    column = scale * carry_l[b]
                elif kind == "last" and offset == 1:
                    column[0] = corner_l[b]
            else:
                distance = blocks - offset
                if kind == "mr":
                    scale = 1.0
                    for c in range(b + 1, b + distance):
                        scale *= np.prod(up[c * size : (c + 1) * size])
                    column = scale * carry_r[b]
                elif kind == "first" and distance == 1:
                    column[size - 1] = corner_r[b]
            carry[b, :, 8 * place : 8 * place + 8] = np.kron(eye, column[:, None])
    return apply.astype(np.float32), np.concatenate([carry] * 3, axis=2).astype(np.float32)


def table_split(table):
    high = table.astype(bfloat16)
    return high, (table - high.astype(np.float64)).astype(bfloat16)


@functools.cache
def span_tables(blocks, size):
    ratio, amplitude, corner = compact_kernel()
    places = np.arange(size)
    images = 1.0 / (1.0 - ratio ** (blocks * size))
    moments = np.zeros((4, size))
    moments[0, size - 1] = 1.0
    moments[1] = ratio ** (size - places)
    moments[2] = ratio ** (places + 1.0)
    moments[3, 0] = 1.0
    carries = np.zeros((blocks, 4, size))
    for slot in range(blocks):
        behind = slot if slot else blocks
        ahead = blocks - slot
        carries[slot, 1] = amplitude * images * ratio ** (size * (behind - 1.0)) * ratio**places
        carries[slot, 2] = -amplitude * images * ratio ** (size * (ahead - 1.0)) * ratio ** (size - 1.0 - places)
        if behind == 1:
            carries[slot, 0, 0] = corner
        if ahead == 1:
            carries[slot, 3, size - 1] = -corner
    both_moments = np.zeros((8, 2 * size))
    both_moments[:4, :size] = moments
    both_moments[4:, size:] = moments
    both_carries = np.zeros((blocks, 8, 2 * size))
    both_carries[:, :4, :size] = carries
    both_carries[:, 4:, size:] = carries
    local_high, local_low = table_split(local_compact(size).T)
    carry_high, carry_low = table_split(both_carries.reshape(8 * blocks, 2 * size))
    return (
        np.block([[local_high, local_low], [local_high, np.zeros_like(local_low)]]),
        np.concatenate(table_split(both_moments)),
        np.concatenate([carry_high, carry_high, carry_low]),
    )


def stream_weights(size):
    ratio, _, _ = compact_kernel()
    filter_ratio, _ = decay(filter_alpha)
    places = np.arange(size)
    return np.stack(
        [
            filter_ratio ** (size - places),
            filter_ratio ** (places + 1.0),
            ratio ** (size - places),
            ratio ** (places + 1.0),
        ]
    )


def filtered_derivative():
    ratio, amplitude, corner = compact_kernel()
    filter_ratio, _ = decay(filter_alpha)
    over, times = ratio / filter_ratio, ratio * filter_ratio
    gain = amplitude * (over / (1.0 - over) - times / (1.0 - times)) + corner * (1.0 / filter_ratio - filter_ratio)
    return gain, amplitude / (1.0 - over), amplitude * filter_ratio / (1.0 - times), corner, corner * filter_ratio


def split(values):
    high = values.astype(bfloat16)
    return high, (values - high.astype(jnp.float32)).astype(bfloat16)


def product(left, right, sides=((1,), (0,))):
    return lax.dot_general(left, right, (sides, ((), ())), preferred_element_type=jnp.float32)


def exchange_kernel(
    nx,
    ny,
    nz,
    den_hbm,
    mom_hbm,
    ene_hbm,
    metric_hbm,
    wtab_hbm,
    ky_hbm,
    py_hbm,
    kz_hbm,
    qz_hbm,
    pz_hbm,
    tend,
    carry_x,
    carry_f,
    carry_d,
    den,
    mom,
    ene,
    metric,
    wtab,
    ky,
    py,
    kz,
    qz,
    pz,
    ky_high,
    ky_low,
    py_both,
    fx,
    fy,
    fz,
    uv0,
    sy,
    sz,
    dys,
    dzs,
    ys_out,
    ys_in,
    zs_in,
    yb_out,
    yb_in,
    zm_in,
    xn_out,
    xn_in,
    xm_out,
    xm_in,
    uv_out,
    uv_in,
    xo_out,
    xo_in,
    io_out,
    io_in,
    state_sem,
    load_sem,
    send_sem,
    recv_sem,
):
    fields, size_x, size_y, size_z = fx.shape
    me_x, me_y, me_z = lax.axis_index("gx"), lax.axis_index("gy"), lax.axis_index("gz")
    rows = size_y // nx
    ratio, amplitude, corner = compact_kernel()
    filter_ratio, _ = decay(filter_alpha)
    gain_d, near_d, far_d, corner_d, first_d = filtered_derivative()
    half_rows = fields * rows
    farthest = sorted(range(1, nx), key=lambda k: -min(k, nx - k))

    def along(axis, offset):
        me, count = {"gx": (me_x, nx), "gy": (me_y, ny), "gz": (me_z, nz)}[axis]
        return lax.rem(me + offset + count, count)

    def state_loads(chunk):
        ys = pl.ds(pl.multiple_of(chunk * 8, 8), 8)
        return [
            pltpu.make_async_copy(den_hbm.at[:, ys], den.at[:, ys], state_sem.at[0, chunk]),
            pltpu.make_async_copy(mom_hbm.at[:, :, ys], mom.at[:, :, ys], state_sem.at[1, chunk]),
            pltpu.make_async_copy(ene_hbm.at[:, ys], ene.at[:, ys], state_sem.at[2, chunk]),
        ]

    sources = (wtab_hbm, ky_hbm.at[me_y], py_hbm.at[me_y], metric_hbm, kz_hbm, qz_hbm, pz_hbm)
    targets = (wtab, ky, py, metric, kz, qz, pz)
    loads = [
        pltpu.make_async_copy(source, target, load_sem.at[place])
        for place, (source, target) in enumerate(zip(sources, targets))
    ]
    loads[0].start()
    for chunk in range(size_y // 8):
        for load in state_loads(chunk):
            load.start()
    for load in loads[1:]:
        load.start()

    barrier = pltpu.get_barrier_semaphore()
    for axis, count in (("gx", nx), ("gy", ny), ("gz", nz)):
        for offset in range(1, count):
            pl.semaphore_signal(barrier, inc=1, device_id={axis: along(axis, offset)}, device_id_type=MESH)

    next_sem = [0]

    def remote(src, dst, axis, offset):
        place = next_sem[0]
        next_sem[0] = place + 1
        return pltpu.make_async_remote_copy(
            src_ref=src,
            dst_ref=dst,
            send_sem=send_sem.at[place],
            recv_sem=recv_sem.at[place],
            device_id={axis: along(axis, offset)},
            device_id_type=MESH,
        )

    loads[0].wait()

    unroll = 4
    zero = jnp.zeros((8, size_z), jnp.float32)

    def flux_chunk(chunk, _):
        ys = pl.ds(pl.multiple_of(chunk * 8, 8), 8)
        for load in state_loads(chunk):
            load.wait()

        def cells(step, acc):
            acc = list(acc)
            for inner in range(unroll):
                x = step * unroll + inner
                w = [wtab[k, x] for k in range(2)]
                rho, energy = den[x, ys, :], ene[x, ys, :]
                m = [mom[j, x, ys, :] for j in range(3)]
                inverse = 1.0 / rho
                v = [m[j] * inverse for j in range(3)]
                own = [m[j] * v[j] for j in range(3)]
                pressure = (heat_ratio - 1.0) * (energy - 0.5 * (own[0] + own[1] + own[2]))
                m12, m13, m23 = m[0] * v[1], m[0] * v[2], m[1] * v[2]
                total = energy + pressure
                flux_x = (m[0], own[0] + pressure, m12, m13, total * v[0])
                flux_y = (m[1], m12, own[1] + pressure, m23, total * v[1])
                flux_z = (m[2], m13, m23, own[2] + pressure, total * v[2])
                for f in range(fields):
                    fx[f, x, ys, :] = flux_x[f]
                    fy[f, x, ys, :] = flux_y[f]
                    fz[f, x, ys, :] = flux_z[f]
                    acc[f] = acc[f] + w[0] * flux_y[f]
                    acc[5 + f] = acc[5 + f] + w[1] * flux_y[f]
                    acc[10 + f] = acc[10 + f] + w[0] * flux_z[f]
                    acc[15 + f] = acc[15 + f] + w[1] * flux_z[f]
            return tuple(acc)

        acc = lax.fori_loop(0, size_x // unroll, cells, (zero,) * 20)
        for f in range(fields):
            sy[f, ys, :] = acc[f]
            sy[5 + f, ys, :] = acc[5 + f]
            sz[0, f, ys, :] = acc[10 + f]
            sz[1, f, ys, :] = acc[15 + f]
        return 0

    sy[10:16] = jnp.zeros((6, size_y, size_z), jnp.float32)
    sz[:, 5:8] = jnp.zeros((2, 3, size_y, size_z), jnp.float32)
    lax.fori_loop(0, size_y // 8, flux_chunk, 0)

    for load in loads[1:]:
        load.wait()
    shape = (8 * size_y, ny * size_y)
    row_place = lax.broadcasted_iota(jnp.int32, shape, 0)
    col_place = lax.broadcasted_iota(jnp.int32, shape, 1)
    mine = col_place == me_y * size_y + lax.rem(row_place, size_y)
    metric_rows = jnp.sum(jnp.where(mine, metric[...], 0.0), axis=1, keepdims=True)
    ky[: 8 * size_y, :] = ky[: 8 * size_y, :] * metric_rows
    ky_high[...], ky_low[...] = split(ky[...])
    high, low = split(py[...] * metric_rows)
    py_both[...] = jnp.where(lax.broadcasted_iota(jnp.int32, py.shape, 1) < 128, high, low)

    def apply_wall(first, second):
        cells = jnp.concatenate(
            [first.reshape(8 * size_y, size_z), second.reshape(8 * size_y, size_z)], axis=1
        )
        high, low = split(cells)
        result = product(ky_high[...], high) + product(ky_high[...], low) + product(ky_low[...], high)
        return [
            (
                result[: 8 * size_y, lanes].reshape(8, size_y, size_z),
                result[8 * size_y :, lanes].reshape(4, 8, size_z),
            )
            for lanes in (slice(0, size_z), slice(size_z, 2 * size_z))
        ]

    def wall_carries(first, second):
        cells = jnp.concatenate([first.reshape(64, size_z), second.reshape(64, size_z)], axis=1)
        high, low = split(cells)
        return product(py_both[...], jnp.concatenate([high, low, high], axis=0))

    def span_local(cells):
        result = product(jnp.concatenate(split(cells), axis=1), kz[...])
        return result[:, :size_z] + result[:, size_z:]

    def span_moments(first, second):
        high, low = split(jnp.concatenate([first, second], axis=1))
        from_high = product(qz[...], high, ((1,), (1,)))
        from_low = product(qz[...], low, ((1,), (1,)))
        return from_high[:8] + from_high[8:] + (from_low[:8] + from_low[8:])

    def span_carries(received):
        high, low = split(received)
        return product(jnp.concatenate([high, low, high], axis=0), pz[...], ((0,), (0,)))

    pl.semaphore_wait(barrier, nx + ny + nz - 3)

    for group, (local, moments) in enumerate(apply_wall(sy[0:8], sy[8:16])):
        dys[8 * group : 8 * group + 8] = local
        ys_out[:, 8 * group : 8 * group + 8, :] = moments
    ys = [
        remote(ys_out.at[pl.ds(0, 3)], ys_in.at[pl.ds(0, 3)], "gy", 1),
        remote(ys_out.at[pl.ds(1, 2)], ys_in.at[pl.ds(3, 2)], "gy", 2),
        remote(ys_out.at[pl.ds(1, 3)], ys_in.at[pl.ds(5, 3)], "gy", 3),
    ]
    for copy in ys:
        copy.start()
    zs_in[0] = span_moments(sz[0].reshape(8 * size_y, size_z), sz[1].reshape(8 * size_y, size_z))
    zs = [remote(zs_in.at[0], zs_in.at[k], "gz", k) for k in range(1, nz)]
    for copy in zs:
        copy.start()
    dzs[...] = span_local(sz[...].reshape(16 * size_y, size_z)).reshape(2, 8, size_y, size_z)

    def stream_chunk(chunk, _):
        ys = pl.ds(pl.multiple_of(chunk * 8, 8), 8)

        def sums(step, acc):
            acc = list(acc)
            for inner in range(unroll):
                x = step * unroll + inner
                w = [wtab[k, x] for k in range(4)]
                state = (den[x, ys, :], mom[0, x, ys, :], mom[1, x, ys, :], mom[2, x, ys, :], ene[x, ys, :])
                for f in range(fields):
                    flux = fx[f, x, ys, :]
                    change = (time_step * gain_d) * flux
                    acc[f] = acc[f] + w[0] * (state[f] - change)
                    acc[5 + f] = acc[5 + f] + w[1] * (state[f] + change)
                    acc[10 + f] = acc[10 + f] + w[2] * flux
                    acc[15 + f] = acc[15 + f] + w[3] * flux
            return tuple(acc)

        acc = lax.fori_loop(0, size_x // unroll, sums, (zero,) * 20)
        for f in range(fields):
            uv0[0, f, ys, :] = acc[f]
            uv0[1, f, ys, :] = acc[5 + f]
            xn_out[0, 0, f, ys, :] = acc[10 + f]
            xn_out[0, 1, f, ys, :] = fx[f, size_x - 1, ys, :]
            xn_out[1, 0, f, ys, :] = acc[15 + f]
            xn_out[1, 1, f, ys, :] = fx[f, 0, ys, :]
        return 0

    lax.fori_loop(0, size_y // 8, stream_chunk, 0)

    def wall_field(f, _):
        for part in range(size_x // 16):
            pair = [pl.ds(16 * part + 8 * side, 8) for side in range(2)]
            for xs, (local, moments) in zip(pair, apply_wall(fy[f, pair[0]], fy[f, pair[1]])):
                tend[f, xs] = local
                yb_out[:, f, xs, :] = moments
        return 0

    lax.fori_loop(0, fields, wall_field, 0)
    yb = [
        remote(yb_out.at[pl.ds(0, 3)], yb_in.at[pl.ds(0, 3)], "gy", 1),
        remote(yb_out.at[pl.ds(1, 2)], yb_in.at[pl.ds(3, 2)], "gy", 2),
        remote(yb_out.at[pl.ds(1, 3)], yb_in.at[pl.ds(5, 3)], "gy", 3),
    ]
    for copy in yb:
        copy.start()

    def span_carries(received):
        high, low = split(received)
        return product(jnp.concatenate([high, low, high], axis=0), pz[...], ((0,), (0,)))

    def deal(message, side, f, values):
        for owner in range(nx):
            place = side * half_rows + rows * f
            message[owner, place : place + rows, :] = values[rows * owner : rows * owner + rows]

    for copy in ys + zs:
        copy.wait()
    span = span_carries(zs_in[...].reshape(8 * nz, 8 * size_y))
    wall = wall_carries(ys_in[:, 0:8, :], ys_in[:, 8:16, :])
    for side in range(2):
        for f in range(fields):
            unit = 5 * side + f
            place, lane = (unit % 8) * size_y, (unit // 8) * size_z
            change = dys[unit] + wall[place : place + size_y, lane : lane + size_z]
            change = change + dzs[side, f] + span[f * size_y : (f + 1) * size_y, side * size_z : (side + 1) * size_z]
            deal(uv_out, side, f, uv0[side, f] - time_step * change)
    uv = [remote(uv_out.at[along("gx", k)], uv_in.at[k], "gx", k) for k in farthest]
    for copy in uv:
        copy.start()
    uv_in[0] = uv_out[me_x]

    xn = [
        remote(xn_out.at[0], xn_in.at[0], "gx", 1),
        remote(xn_out.at[1], xn_in.at[1], "gx", -1),
    ]
    for copy in xn:
        copy.start()
    for side in range(2):
        for f in range(fields):
            deal(xm_out, side, f, xn_out[side, 0, f])
    xm = [remote(xm_out.at[along("gx", k)], xm_in.at[k], "gx", k) for k in farthest]
    for copy in xm:
        copy.start()
    xm_in[0] = xm_out[me_x]

    half = size_x // 2

    def span_field(f, _):
        pair = [fz[f, pl.ds(part * half, half)].reshape(half * size_y, size_z) for part in range(2)]
        zm_in[0, f] = span_moments(*pair)
        return 0

    lax.fori_loop(0, fields, span_field, 0)
    zm = [remote(zm_in.at[0], zm_in.at[k], "gz", k) for k in range(1, nz)]
    for copy in zm:
        copy.start()

    def span_cells(f, _):
        for part in range(size_x // 8):
            xs = pl.ds(8 * part, 8)
            tend[f, xs] += span_local(fz[f, xs].reshape(8 * size_y, size_z)).reshape(8, size_y, size_z)
        return 0

    lax.fori_loop(0, fields, span_cells, 0)

    def sweep(behind, power, values):
        step = 1 if behind else -1
        total = values[0] if behind else values[nx - 1]
        for k in range(1, nx):
            total = total + float(power**k) * (values[k] if behind else values[nx - 1 - k])
        total = total * float(1.0 / (1.0 - power**nx))
        place = nx - 1 if behind else 0
        result = [None] * nx
        result[place] = total
        for _ in range(nx - 1):
            total = values[place] + float(power) * total
            place = place - step
            result[place] = total
        return result

    from_behind = lax.broadcasted_iota(jnp.int32, (2 * half_rows, size_z), 0) < half_rows
    for copy in xm:
        copy.wait()
    power = ratio**size_x
    values = [xm_in[k] for k in range(nx)]
    near_l, near_r = sweep(True, power, values), sweep(False, power, values)
    for k in range(nx):
        xo_out[k] = float(power) * jnp.where(from_behind, near_l[(k + 1) % nx], near_r[(k - 1) % nx])
    xo = [remote(xo_out.at[k], xo_in.at[me_x], "gx", -k) for k in farthest]
    for copy in xo:
        copy.start()
    xo_in[me_x] = xo_out[0]
    for copy in xn:
        copy.wait()

    def scan_chunk(chunk, _):
        ys = pl.ds(pl.multiple_of(chunk * 8, 8), 8)

        def scan(side, step, carried):
            carried = list(carried)
            for inner in range(unroll):
                x = step * unroll + inner
                x = size_x - 1 - x if side else x
                gains = (-amplitude, -corner) if side else (amplitude, corner)
                for f in range(fields):
                    total, last = carried[f], carried[5 + f]
                    tend[f, x, ys, :] += gains[0] * total + gains[1] * last
                    here = fx[f, x, ys, :]
                    carried[f], carried[5 + f] = ratio * (total + here), here
            return tuple(carried)

        for side in range(2):
            start = [xn_in[side, kind, f, ys, :] for kind in range(2) for f in range(fields)]
            lax.fori_loop(0, size_x // unroll, functools.partial(scan, side), tuple(start))
        return 0

    lax.fori_loop(0, size_y // 8, scan_chunk, 0)

    for copy in uv:
        copy.wait()
    filter_power = filter_ratio**size_x
    values = [uv_in[k] for k in range(nx)]
    filter_l, filter_r = sweep(True, filter_power, values), sweep(False, filter_power, values)
    for k in range(nx):
        io_out[k] = jnp.where(from_behind, filter_l[k], filter_r[k])
    io = [remote(io_out.at[k], io_in.at[me_x], "gx", -k) for k in farthest]
    for copy in io:
        copy.start()
    io_in[me_x] = io_out[0]

    for side in range(2):
        sign = -time_step if side else time_step
        for f in range(fields):
            past = xn_out[1 - side, 0, f] + float(power) * xn_in[1 - side, 0, f]
            carry_d[side, f] = (
                (sign * near_d) * xn_in[side, 0, f]
                + (sign * corner_d) * xn_in[side, 1, f]
                + (sign * far_d) * past
                + (sign * first_d) * xn_out[1 - side, 1, f]
            )

    for copy in yb + zm:
        copy.wait()

    def carries(f, _):
        both = span_carries(zm_in[:, f].reshape(8 * nz, half * size_y))
        for part in range(size_x // 16):
            pair = [pl.ds(16 * part + 8 * side, 8) for side in range(2)]
            wall = wall_carries(yb_in[:, f, pair[0], :], yb_in[:, f, pair[1], :])
            for side, xs in enumerate(pair):
                row = (16 * part + 8 * side) % half * size_y
                lane = (16 * part + 8 * side) // half * size_z
                change = wall[:, side * size_z : (side + 1) * size_z]
                change = change + both[row : row + 8 * size_y, lane : lane + size_z]
                tend[f, xs] += change.reshape(8, size_y, size_z)
        return 0

    lax.fori_loop(0, fields, carries, 0)

    for copy in xo + io:
        copy.wait()
    carry_x[...] = xo_in[...]
    carry_f[...] = io_in[...]


def filter_kernel(den, mom, ene, part, carry_x, carry_f, carry_d, tend_hbm, after_hbm, tend, after, sems):
    chunks, fields, size_x = tend.shape[:3]
    half_rows = carry_x.shape[1] // 2
    rows = half_rows // fields
    owners = 8 // rows
    ratio, far_gain, _ = compact_kernel()
    filter_ratio, gain = decay(filter_alpha)
    straight = 0.5 * (0.5 + filter_alpha) / filter_alpha
    amplitude = (0.5 + filter_alpha - straight) * gain
    _, near_d, far_d, _, _ = filtered_derivative()
    power = ratio**size_x
    unroll = 4

    def copies(chunk):
        ys = pl.ds(pl.multiple_of(chunk * 8, 8), 8)
        return (
            pltpu.make_async_copy(tend.at[chunk], tend_hbm.at[:, :, ys], sems.at[0, chunk]),
            pltpu.make_async_copy(after.at[chunk], after_hbm.at[:, :, ys], sems.at[1, chunk]),
        )

    def chunk_body(chunk, _):
        ys = pl.ds(pl.multiple_of(chunk * 8, 8), 8)

        def carried_in(ref, side, f):
            place = side * half_rows + rows * f
            return jnp.concatenate(
                [ref[chunk * owners + o, place : place + rows, :] for o in range(owners)], axis=0
            )

        def state(f, x):
            return den[x, ys, :] if f == 0 else ene[x, ys, :] if f == 4 else mom[f - 1, x, ys, :]

        far_l = [carried_in(carry_x, 0, f) for f in range(fields)]
        far_r = [carried_in(carry_x, 1, f) for f in range(fields)]
        start_l = [
            carried_in(carry_f, 0, f)
            + carry_d[0, f, ys, :]
            + time_step * (near_d * far_l[f] + float(far_d * power) * far_r[f])
            for f in range(fields)
        ]
        start_r = [
            carried_in(carry_f, 1, f)
            + carry_d[1, f, ys, :]
            - time_step * (near_d * far_r[f] + float(far_d * power) * far_l[f])
            for f in range(fields)
        ]
        head = [float(far_gain * ratio ** (size_x - 1)) * far_l[f] for f in range(fields)]
        tail = [far_gain * far_r[f] for f in range(fields)]

        def back(step, carried):
            carried = list(carried)
            for inner in range(unroll):
                x = size_x - 1 - (step * unroll + inner)
                for f in range(fields):
                    behind, ahead = carried[5 + f], carried[10 + f]
                    rate = ahead - behind - part[f, x, ys, :]
                    tend[chunk, f, x] = rate
                    after[chunk, f, x] = amplitude * carried[f]
                    carried[f] = filter_ratio * (carried[f] + (state(f, x) + time_step * rate))
                    carried[5 + f], carried[10 + f] = (1.0 / ratio) * behind, ratio * ahead
            return tuple(carried)

        def ahead(step, carried):
            carried = list(carried)
            for inner in range(unroll):
                x = step * unroll + inner
                for f in range(fields):
                    middle = state(f, x) + time_step * tend[chunk, f, x]
                    after[chunk, f, x] += (straight + amplitude) * middle + amplitude * carried[f]
                    carried[f] = filter_ratio * (carried[f] + middle)
            return tuple(carried)

        lax.fori_loop(0, size_x // unroll, back, tuple(start_r + head + tail))
        rate_copy, after_copy = copies(chunk)
        rate_copy.start()
        lax.fori_loop(0, size_x // unroll, ahead, tuple(start_l))
        after_copy.start()
        return 0

    lax.fori_loop(0, chunks, chunk_body, 0)
    for chunk in range(chunks):
        for copy in copies(chunk):
            copy.wait()


def solution(mesh):
    nx, ny, nz = mesh.shape["gx"], mesh.shape["gy"], mesh.shape["gz"]

    def on_device(density, momentum, energy, metric):
        size_x, size_y, size_z = density.shape
        fields = 5
        rows = size_y // nx
        float32 = jnp.float32
        ky, py = wall_tables(ny, size_y)
        kz, qz, pz = span_tables(nz, size_z)
        wtab = stream_weights(size_x).astype(np.float32)
        cells = (fields, size_x, size_y, size_z)
        owned = (nx, 2 * fields * rows, size_z)
        sides = (2, fields, size_y, size_z)
        vmem = pl.BlockSpec(memory_space=pltpu.VMEM)
        stays = pl.BlockSpec(memory_space=pltpu.HBM)
        copies = 2 + 4 * (nx - 1) + 6 + 2 * (nz - 1)
        chunks = size_y // 8
        part, carry_x, carry_f, carry_d = pl.pallas_call(
            functools.partial(exchange_kernel, nx, ny, nz),
            out_shape=[
                jax.ShapeDtypeStruct(cells, float32),
                jax.ShapeDtypeStruct(owned, float32),
                jax.ShapeDtypeStruct(owned, float32),
                jax.ShapeDtypeStruct(sides, float32),
            ],
            in_specs=[stays] * 10,
            out_specs=[vmem] * 4,
            scratch_shapes=[
                pltpu.VMEM(cells[1:], float32),
                pltpu.VMEM((3,) + cells[1:], float32),
                pltpu.VMEM(cells[1:], float32),
                pltpu.VMEM((1, ny * size_y), float32),
                pltpu.SMEM(wtab.shape, float32),
                pltpu.VMEM(ky.shape[1:], float32),
                pltpu.VMEM(py.shape[1:], float32),
                pltpu.VMEM(kz.shape, bfloat16),
                pltpu.VMEM(qz.shape, bfloat16),
                pltpu.VMEM(pz.shape, bfloat16),
                pltpu.VMEM(ky.shape[1:], bfloat16),
                pltpu.VMEM(ky.shape[1:], bfloat16),
                pltpu.VMEM(py.shape[1:], bfloat16),
                pltpu.VMEM(cells, float32),
                pltpu.VMEM(cells, float32),
                pltpu.VMEM(cells, float32),
                pltpu.VMEM(sides, float32),
                pltpu.VMEM((16, size_y, size_z), float32),
                pltpu.VMEM((2, 8, size_y, size_z), float32),
                pltpu.VMEM((16, size_y, size_z), float32),
                pltpu.VMEM((2, 8, size_y, size_z), float32),
                pltpu.VMEM((4, 16, size_z), float32),
                pltpu.VMEM((8, 16, size_z), float32),
                pltpu.VMEM((nz, 8, 8 * size_y), float32),
                pltpu.VMEM((4, fields, size_x, size_z), float32),
                pltpu.VMEM((8, fields, size_x, size_z), float32),
                pltpu.VMEM((nz, fields, 8, size_x // 2 * size_y), float32),
                pltpu.VMEM((2, 2, fields, size_y, size_z), float32),
                pltpu.VMEM((2, 2, fields, size_y, size_z), float32),
                pltpu.VMEM(owned, float32),
                pltpu.VMEM(owned, float32),
                pltpu.VMEM(owned, float32),
                pltpu.VMEM(owned, float32),
                pltpu.VMEM(owned, float32),
                pltpu.VMEM(owned, float32),
                pltpu.VMEM(owned, float32),
                pltpu.VMEM(owned, float32),
                pltpu.SemaphoreType.DMA((3, chunks)),
                pltpu.SemaphoreType.DMA((7,)),
                pltpu.SemaphoreType.DMA((copies,)),
                pltpu.SemaphoreType.DMA((copies,)),
            ],
            compiler_params=pltpu.CompilerParams(
                collective_id=0, has_side_effects=True, vmem_limit_bytes=24 * 1024 * 1024
            ),
            cost_estimate=pl.CostEstimate(flops=4 * 10**9, bytes_accessed=10**7, transcendentals=0),
        )(
            *[
                pltpu.with_memory_space_constraint(jnp.asarray(value), pltpu.HBM)
                for value in (density, momentum, energy, metric.reshape(1, -1), wtab, ky, py, kz, qz, pz)
            ]
        )
        return pl.pallas_call(
            filter_kernel,
            out_shape=[jax.ShapeDtypeStruct(cells, float32), jax.ShapeDtypeStruct(cells, float32)],
            in_specs=[vmem] * 7,
            out_specs=[stays] * 2,
            scratch_shapes=[
                pltpu.VMEM((chunks, fields, size_x, 8, size_z), float32),
                pltpu.VMEM((chunks, fields, size_x, 8, size_z), float32),
                pltpu.SemaphoreType.DMA((2, chunks)),
            ],
            compiler_params=pltpu.CompilerParams(vmem_limit_bytes=16 * 1024 * 1024),
            cost_estimate=pl.CostEstimate(flops=10**7, bytes_accessed=10**7, transcendentals=0),
        )(density, momentum, energy, part, carry_x, carry_f, carry_d)

    return jax.shard_map(
        on_device,
        mesh=mesh,
        in_specs=(P("gx", "gy", "gz"), P(None, "gx", "gy", "gz"), P("gx", "gy", "gz"), P()),
        out_specs=(P(None, "gx", "gy", "gz"), P(None, "gx", "gy", "gz")),
        check_vma=False,
    )
```

```python
import functools

import jax
import jax.numpy as jnp
import numpy as np
from jax import lax
from jax.experimental import pallas as pl
from jax.experimental.pallas import tpu as pltpu
from jax.sharding import PartitionSpec as P

heat_ratio = 1.4
compact_alpha = 1.0 / 3.0
filter_alpha = 0.499
time_step = 0.05
near_weight = 7.0 / 9.0
wide_weight = 1.0 / 36.0
bfloat16 = jnp.bfloat16
MESH = pl.DeviceIdType.MESH
KINDS_Y = ((1, "last"), (1, "ml"), (1, "mr"), (2, "ml"), (2, "mr"), (3, "ml"), (3, "mr"), (3, "first"))


def decay(alpha):
    root = np.sqrt(1.0 - 4.0 * alpha * alpha)
    return (-1.0 + root) / (2.0 * alpha), 1.0 / root


def compact_kernel():
    ratio, gain = decay(compact_alpha)

    def green(n):
        return gain * ratio ** abs(n)

    def kernel(d):
        return near_weight * (green(d + 1) - green(d - 1)) + wide_weight * (green(d + 2) - green(d - 2))

    amplitude = kernel(2) / ratio**2
    return ratio, amplitude, kernel(1) - amplitude * ratio


def local_compact(size):
    ratio, amplitude, corner = compact_kernel()
    table = np.zeros((size, size))
    for i in range(size):
        for j in range(size):
            d = abs(i - j)
            if d:
                value = amplitude * ratio**d + (corner if d == 1 else 0.0)
                table[i, j] = value if i > j else -value
    return table


def table_thomas(lower_band, main_band, upper_band, source):
    count = source.shape[0]
    c_all = np.zeros(count)
    d_all = np.zeros(source.shape)
    c_prev = 0.0
    d_prev = np.zeros(source.shape[1:])
    for place in range(count):
        denom = main_band[place] - lower_band[place] * c_prev
        c_prev = upper_band[place] / denom
        d_prev = (source[place] - lower_band[place] * d_prev) / denom
        c_all[place] = c_prev
        d_all[place] = d_prev
    solved = np.zeros(source.shape)
    x_next = np.zeros(source.shape[1:])
    for place in range(count - 1, -1, -1):
        x_next = d_all[place] - c_all[place] * x_next
        solved[place] = x_next
    return solved


def wall_bands(total):
    lower = np.full(total, compact_alpha)
    upper = np.full(total, compact_alpha)
    lower[0], lower[1], lower[total - 2], lower[total - 1] = 0.0, 0.25, 0.25, 2.0
    upper[0], upper[1], upper[total - 2], upper[total - 1] = 2.0, 0.25, 0.25, 0.0
    return lower, upper


def wall_table(total):
    lower, upper = wall_bands(total)
    stencil = np.zeros((total, total))
    for i in range(2, total - 2):
        stencil[i, i + 1], stencil[i, i - 1] = near_weight, -near_weight
        stencil[i, i + 2], stencil[i, i - 2] = wide_weight, -wide_weight
    for i in (1, total - 2):
        stencil[i, i + 1], stencil[i, i - 1] = 0.75, -0.75
    stencil[0, :3] = (-2.5, 2.0, 0.5)
    stencil[total - 1, total - 3 :] = (-0.5, -2.0, 2.5)
    return table_thomas(lower, np.ones(total), upper, stencil)


@functools.cache
def wall_tables(blocks, size):
    total = blocks * size
    table = wall_table(total)
    lower, upper = wall_bands(total)
    down = np.zeros(total)
    for i in range(total - 1, 0, -1):
        down[i - 1] = -lower[i] / (1.0 + upper[i] * down[i])
    up = np.zeros(total)
    for i in range(total - 1):
        up[i + 1] = -upper[i] / (1.0 + lower[i] * up[i])
    carry_l, carry_r, corner_l, corner_r = [], [], [], []
    moment_l, moment_r = np.zeros((blocks, size)), np.zeros((blocks, size))
    for b in range(blocks):
        head, tail = b * size, b * size + size - 1
        carry_l.append(np.concatenate([[1.0], np.cumprod(down[head:tail])]))
        carry_r.append(np.concatenate([[1.0], np.cumprod(up[head + 1 : tail + 1][::-1])])[::-1])
        corner_l.append(table[head, head - 1] - table[head + 1, head - 1] / down[head] if b else 0.0)
        corner_r.append(table[tail, tail + 1] - table[tail - 1, tail + 1] / up[tail] if b < blocks - 1 else 0.0)
        if b < blocks - 1:
            to = tail + 1
            moment_l[b] = table[to, head:to]
            moment_l[b, size - 1] = table[to + 1, tail] / down[to]
        if b:
            to = head - 1
            moment_r[b] = table[to, head : tail + 1]
            moment_r[b, 0] = table[to - 1, head] / up[to]
    apply = np.zeros((blocks, 8 * size + 32, 8 * size))
    carry = np.zeros((blocks, 8 * size, 8 * len(KINDS_Y)))
    eye = np.eye(8)
    for b in range(blocks):
        rows = slice(b * size, (b + 1) * size)
        apply[b, : 8 * size] = np.kron(eye, table[rows, rows])
        first, last = np.eye(size)[0], np.eye(size)[size - 1]
        for kind, weights in enumerate((last, moment_l[b], moment_r[b], first)):
            apply[b, 8 * size + 8 * kind : 8 * size + 8 * kind + 8] = np.kron(eye, weights[None])
        for place, (offset, kind) in enumerate(KINDS_Y):
            column = np.zeros(size)
            if b - offset >= 0:
                if kind == "ml":
                    scale = 1.0
                    for c in range(b - offset + 1, b):
                        scale *= np.prod(down[c * size : (c + 1) * size])
                    column = scale * carry_l[b]
                elif kind == "last" and offset == 1:
                    column[0] = corner_l[b]
            else:
                distance = blocks - offset
                if kind == "mr":
                    scale = 1.0
                    for c in range(b + 1, b + distance):
                        scale *= np.prod(up[c * size : (c + 1) * size])
                    column = scale * carry_r[b]
                elif kind == "first" and distance == 1:
                    column[size - 1] = corner_r[b]
            carry[b, :, 8 * place : 8 * place + 8] = np.kron(eye, column[:, None])
    return apply.astype(np.float32), np.concatenate([carry] * 3, axis=2).astype(np.float32)


def table_split(table):
    high = table.astype(bfloat16)
    return high, (table - high.astype(np.float64)).astype(bfloat16)


@functools.cache
def span_tables(blocks, size):
    ratio, amplitude, corner = compact_kernel()
    places = np.arange(size)
    images = 1.0 / (1.0 - ratio ** (blocks * size))
    moments = np.zeros((4, size))
    moments[0, size - 1] = 1.0
    moments[1] = ratio ** (size - places)
    moments[2] = ratio ** (places + 1.0)
    moments[3, 0] = 1.0
    carries = np.zeros((blocks, 4, size))
    for slot in range(blocks):
        behind = slot if slot else blocks
        ahead = blocks - slot
        carries[slot, 1] = amplitude * images * ratio ** (size * (behind - 1.0)) * ratio**places
        carries[slot, 2] = -amplitude * images * ratio ** (size * (ahead - 1.0)) * ratio ** (size - 1.0 - places)
        if behind == 1:
            carries[slot, 0, 0] = corner
        if ahead == 1:
            carries[slot, 3, size - 1] = -corner
    both_moments = np.zeros((8, 2 * size))
    both_moments[:4, :size] = moments
    both_moments[4:, size:] = moments
    both_carries = np.zeros((blocks, 8, 2 * size))
    both_carries[:, :4, :size] = carries
    both_carries[:, 4:, size:] = carries
    local_high, local_low = table_split(local_compact(size).T)
    carry_high, carry_low = table_split(both_carries.reshape(8 * blocks, 2 * size))
    return (
        np.block([[local_high, local_low], [local_high, np.zeros_like(local_low)]]),
        np.concatenate(table_split(both_moments)),
        np.concatenate([carry_high, carry_high, carry_low]),
    )


def stream_weights(size):
    ratio, _, _ = compact_kernel()
    filter_ratio, _ = decay(filter_alpha)
    places = np.arange(size)
    return np.stack(
        [
            filter_ratio ** (size - places),
            filter_ratio ** (places + 1.0),
            ratio ** (size - places),
            ratio ** (places + 1.0),
        ]
    )


def filtered_derivative():
    ratio, amplitude, corner = compact_kernel()
    filter_ratio, _ = decay(filter_alpha)
    over, times = ratio / filter_ratio, ratio * filter_ratio
    gain = amplitude * (over / (1.0 - over) - times / (1.0 - times)) + corner * (1.0 / filter_ratio - filter_ratio)
    return gain, amplitude / (1.0 - over), amplitude * filter_ratio / (1.0 - times), corner, corner * filter_ratio


def split(values):
    high = values.astype(bfloat16)
    return high, (values - high.astype(jnp.float32)).astype(bfloat16)


def product(left, right, sides=((1,), (0,))):
    return lax.dot_general(left, right, (sides, ((), ())), preferred_element_type=jnp.float32)


def exchange_kernel(
    nx,
    ny,
    nz,
    den_hbm,
    mom_hbm,
    ene_hbm,
    metric_hbm,
    wtab_hbm,
    ky_hbm,
    py_hbm,
    kz_hbm,
    qz_hbm,
    pz_hbm,
    tend,
    carry_x,
    carry_f,
    carry_d,
    den,
    mom,
    ene,
    metric,
    wtab,
    ky,
    py,
    kz,
    qz,
    pz,
    ky_high,
    ky_low,
    py_both,
    fx,
    fy,
    fz,
    uv0,
    moments_x,
    sy,
    sz,
    dys,
    dzs,
    ys_out,
    ys_in,
    zs_in,
    yb_out,
    yb_in,
    zm_in,
    xn_out,
    xn_in,
    xm_out,
    xm_in,
    uv_out,
    uv_in,
    xo_out,
    xo_in,
    io_out,
    io_in,
    state_sem,
    load_sem,
    send_sem,
    recv_sem,
):
    fields, size_x, size_y, size_z = fx.shape
    me_x, me_y, me_z = lax.axis_index("gx"), lax.axis_index("gy"), lax.axis_index("gz")
    rows = size_y // nx
    ratio, amplitude, corner = compact_kernel()
    filter_ratio, _ = decay(filter_alpha)
    gain_d, _, far_d, corner_d, first_d = filtered_derivative()
    half_rows = fields * rows
    farthest = sorted(range(1, nx), key=lambda k: -min(k, nx - k))

    def along(axis, offset):
        me, count = {"gx": (me_x, nx), "gy": (me_y, ny), "gz": (me_z, nz)}[axis]
        return lax.rem(me + offset + count, count)

    def state_loads(chunk):
        ys = pl.ds(pl.multiple_of(chunk * 8, 8), 8)
        return [
            pltpu.make_async_copy(den_hbm.at[:, ys], den.at[:, ys], state_sem.at[0, chunk]),
            pltpu.make_async_copy(mom_hbm.at[:, :, ys], mom.at[:, :, ys], state_sem.at[1, chunk]),
            pltpu.make_async_copy(ene_hbm.at[:, ys], ene.at[:, ys], state_sem.at[2, chunk]),
        ]

    sources = (wtab_hbm, ky_hbm.at[me_y], py_hbm.at[me_y], metric_hbm, kz_hbm, qz_hbm, pz_hbm)
    targets = (wtab, ky, py, metric, kz, qz, pz)
    loads = [
        pltpu.make_async_copy(source, target, load_sem.at[place])
        for place, (source, target) in enumerate(zip(sources, targets))
    ]
    loads[0].start()
    for chunk in range(size_y // 8):
        for load in state_loads(chunk):
            load.start()
    for load in loads[1:]:
        load.start()

    barrier = pltpu.get_barrier_semaphore()
    for axis, count in (("gx", nx), ("gy", ny), ("gz", nz)):
        for offset in range(1, count):
            pl.semaphore_signal(barrier, inc=1, device_id={axis: along(axis, offset)}, device_id_type=MESH)

    next_sem = [0]

    def remote(src, dst, axis, offset):
        place = next_sem[0]
        next_sem[0] = place + 1
        return pltpu.make_async_remote_copy(
            src_ref=src,
            dst_ref=dst,
            send_sem=send_sem.at[place],
            recv_sem=recv_sem.at[place],
            device_id={axis: along(axis, offset)},
            device_id_type=MESH,
        )

    loads[0].wait()

    unroll = 4
    zero = jnp.zeros((8, size_z), jnp.float32)

    def flux_chunk(chunk, _):
        ys = pl.ds(pl.multiple_of(chunk * 8, 8), 8)
        for load in state_loads(chunk):
            load.wait()

        def cells(step, acc):
            acc = list(acc)
            for inner in range(unroll):
                x = step * unroll + inner
                w = [wtab[k, x] for k in range(4)]
                rho, energy = den[x, ys, :], ene[x, ys, :]
                m = [mom[j, x, ys, :] for j in range(3)]
                inverse = 1.0 / rho
                v = [m[j] * inverse for j in range(3)]
                own = [m[j] * v[j] for j in range(3)]
                pressure = (heat_ratio - 1.0) * (energy - 0.5 * (own[0] + own[1] + own[2]))
                m12, m13, m23 = m[0] * v[1], m[0] * v[2], m[1] * v[2]
                total = energy + pressure
                flux_x = (m[0], own[0] + pressure, m12, m13, total * v[0])
                flux_y = (m[1], m12, own[1] + pressure, m23, total * v[1])
                flux_z = (m[2], m13, m23, own[2] + pressure, total * v[2])
                state = (rho, m[0], m[1], m[2], energy)
                for f in range(fields):
                    fx[f, x, ys, :] = flux_x[f]
                    fy[f, x, ys, :] = flux_y[f]
                    fz[f, x, ys, :] = flux_z[f]
                    change = (time_step * gain_d) * flux_x[f]
                    acc[f] = acc[f] + w[0] * (state[f] - change)
                    acc[5 + f] = acc[5 + f] + w[1] * (state[f] + change)
                    acc[10 + f] = acc[10 + f] + w[2] * flux_x[f]
                    acc[15 + f] = acc[15 + f] + w[3] * flux_x[f]
            return tuple(acc)

        acc = lax.fori_loop(0, size_x // unroll, cells, (zero,) * 20)
        for f in range(fields):
            uv0[0, f, ys, :] = acc[f]
            uv0[1, f, ys, :] = acc[5 + f]
            moments_x[0, f, ys, :] = acc[10 + f]
            moments_x[1, f, ys, :] = acc[15 + f]
            xn_out[0, f, ys, :] = fx[f, size_x - 1, ys, :]
            xn_out[1, f, ys, :] = fx[f, 0, ys, :]
        return 0

    sy[10:16] = jnp.zeros((6, size_y, size_z), jnp.float32)
    sz[:, 5:8] = jnp.zeros((2, 3, size_y, size_z), jnp.float32)
    lax.fori_loop(0, size_y // 8, flux_chunk, 0)

    def deal(message, side, f, values):
        for owner in range(nx):
            place = side * half_rows + rows * f
            message[owner, place : place + rows, :] = values[rows * owner : rows * owner + rows]

    pl.semaphore_wait(barrier, nx + ny + nz - 3)
    for side in range(2):
        for f in range(fields):
            deal(xm_out, side, f, moments_x[side, f])
    xm = [remote(xm_out.at[along("gx", k)], xm_in.at[k], "gx", k) for k in farthest]
    for copy in xm:
        copy.start()
    xm_in[0] = xm_out[me_x]

    def sums_chunk(chunk, _):
        ys = pl.ds(pl.multiple_of(chunk * 8, 8), 8)

        def sums(step, acc):
            acc = list(acc)
            for inner in range(unroll):
                x = step * unroll + inner
                w = [wtab[k, x] for k in range(2)]
                for f in range(fields):
                    value_y, value_z = fy[f, x, ys, :], fz[f, x, ys, :]
                    acc[f] = acc[f] + w[0] * value_y
                    acc[5 + f] = acc[5 + f] + w[1] * value_y
                    acc[10 + f] = acc[10 + f] + w[0] * value_z
                    acc[15 + f] = acc[15 + f] + w[1] * value_z
            return tuple(acc)

        acc = lax.fori_loop(0, size_x // unroll, sums, (zero,) * 20)
        for f in range(fields):
            sy[f, ys, :] = acc[f]
            sy[5 + f, ys, :] = acc[5 + f]
            sz[0, f, ys, :] = acc[10 + f]
            sz[1, f, ys, :] = acc[15 + f]
        return 0

    lax.fori_loop(0, size_y // 8, sums_chunk, 0)

    for load in loads[1:]:
        load.wait()
    shape = (8 * size_y, ny * size_y)
    row_place = lax.broadcasted_iota(jnp.int32, shape, 0)
    col_place = lax.broadcasted_iota(jnp.int32, shape, 1)
    mine = col_place == me_y * size_y + lax.rem(row_place, size_y)
    metric_rows = jnp.sum(jnp.where(mine, metric[...], 0.0), axis=1, keepdims=True)
    ky[: 8 * size_y, :] = ky[: 8 * size_y, :] * metric_rows
    ky_high[...], ky_low[...] = split(ky[...])
    high, low = split(py[...] * metric_rows)
    py_both[...] = jnp.where(lax.broadcasted_iota(jnp.int32, py.shape, 1) < 128, high, low)

    def apply_wall(first, second):
        cells = jnp.concatenate(
            [first.reshape(8 * size_y, size_z), second.reshape(8 * size_y, size_z)], axis=1
        )
        high, low = split(cells)
        result = product(ky_high[...], high) + product(ky_high[...], low) + product(ky_low[...], high)
        return [
            (
                result[: 8 * size_y, lanes].reshape(8, size_y, size_z),
                result[8 * size_y :, lanes].reshape(4, 8, size_z),
            )
            for lanes in (slice(0, size_z), slice(size_z, 2 * size_z))
        ]

    def wall_carries(first, second):
        cells = jnp.concatenate([first.reshape(64, size_z), second.reshape(64, size_z)], axis=1)
        high, low = split(cells)
        return product(py_both[...], jnp.concatenate([high, low, high], axis=0))

    def span_local(cells):
        result = product(jnp.concatenate(split(cells), axis=1), kz[...])
        return result[:, :size_z] + result[:, size_z:]

    def span_moments(first, second):
        high, low = split(jnp.concatenate([first, second], axis=1))
        from_high = product(qz[...], high, ((1,), (1,)))
        from_low = product(qz[...], low, ((1,), (1,)))
        return from_high[:8] + from_high[8:] + (from_low[:8] + from_low[8:])

    def span_carries(received):
        high, low = split(received)
        return product(jnp.concatenate([high, low, high], axis=0), pz[...], ((0,), (0,)))

    for group, (local, moments) in enumerate(apply_wall(sy[0:8], sy[8:16])):
        dys[8 * group : 8 * group + 8] = local
        ys_out[:, 8 * group : 8 * group + 8, :] = moments
    ys = [
        remote(ys_out.at[pl.ds(0, 3)], ys_in.at[pl.ds(0, 3)], "gy", 1),
        remote(ys_out.at[pl.ds(1, 2)], ys_in.at[pl.ds(3, 2)], "gy", 2),
        remote(ys_out.at[pl.ds(1, 3)], ys_in.at[pl.ds(5, 3)], "gy", 3),
    ]
    for copy in ys:
        copy.start()
    zs_in[0] = span_moments(sz[0].reshape(8 * size_y, size_z), sz[1].reshape(8 * size_y, size_z))
    zs = [remote(zs_in.at[0], zs_in.at[k], "gz", k) for k in range(1, nz)]
    for copy in zs:
        copy.start()
    dzs[...] = span_local(sz[...].reshape(16 * size_y, size_z)).reshape(2, 8, size_y, size_z)

    def wall_field(f, _):
        for part in range(size_x // 16):
            pair = [pl.ds(16 * part + 8 * side, 8) for side in range(2)]
            for xs, (local, moments) in zip(pair, apply_wall(fy[f, pair[0]], fy[f, pair[1]])):
                tend[f, xs] = local
                yb_out[:, f, xs, :] = moments
        return 0

    lax.fori_loop(0, fields, wall_field, 0)
    yb = [
        remote(yb_out.at[pl.ds(0, 3)], yb_in.at[pl.ds(0, 3)], "gy", 1),
        remote(yb_out.at[pl.ds(1, 2)], yb_in.at[pl.ds(3, 2)], "gy", 2),
        remote(yb_out.at[pl.ds(1, 3)], yb_in.at[pl.ds(5, 3)], "gy", 3),
    ]
    for copy in yb:
        copy.start()

    def span_carries(received):
        high, low = split(received)
        return product(jnp.concatenate([high, low, high], axis=0), pz[...], ((0,), (0,)))

    for copy in ys + zs:
        copy.wait()
    span = span_carries(zs_in[...].reshape(8 * nz, 8 * size_y))
    wall = wall_carries(ys_in[:, 0:8, :], ys_in[:, 8:16, :])
    for side in range(2):
        for f in range(fields):
            unit = 5 * side + f
            place, lane = (unit % 8) * size_y, (unit // 8) * size_z
            change = dys[unit] + wall[place : place + size_y, lane : lane + size_z]
            change = change + dzs[side, f] + span[f * size_y : (f + 1) * size_y, side * size_z : (side + 1) * size_z]
            deal(uv_out, side, f, uv0[side, f] - time_step * change)
    uv = [remote(uv_out.at[along("gx", k)], uv_in.at[k], "gx", k) for k in farthest]
    for copy in uv:
        copy.start()
    uv_in[0] = uv_out[me_x]

    xn = [
        remote(xn_out.at[0], xn_in.at[0], "gx", 1),
        remote(xn_out.at[1], xn_in.at[1], "gx", -1),
    ]
    for copy in xn:
        copy.start()

    half = size_x // 2

    def span_field(f, _):
        pair = [fz[f, pl.ds(part * half, half)].reshape(half * size_y, size_z) for part in range(2)]
        zm_in[0, f] = span_moments(*pair)
        return 0

    lax.fori_loop(0, fields, span_field, 0)
    zm = [remote(zm_in.at[0], zm_in.at[k], "gz", k) for k in range(1, nz)]
    for copy in zm:
        copy.start()

    def span_cells(f, _):
        for part in range(size_x // 8):
            xs = pl.ds(8 * part, 8)
            tend[f, xs] += span_local(fz[f, xs].reshape(8 * size_y, size_z)).reshape(8, size_y, size_z)
        return 0

    lax.fori_loop(0, fields, span_cells, 0)

    def sweep(behind, power, values):
        step = 1 if behind else -1
        total = values[0] if behind else values[nx - 1]
        for k in range(1, nx):
            total = total + float(power**k) * (values[k] if behind else values[nx - 1 - k])
        total = total * float(1.0 / (1.0 - power**nx))
        place = nx - 1 if behind else 0
        result = [None] * nx
        result[place] = total
        for _ in range(nx - 1):
            total = values[place] + float(power) * total
            place = place - step
            result[place] = total
        return result

    from_behind = lax.broadcasted_iota(jnp.int32, (2 * half_rows, size_z), 0) < half_rows
    from_behind = lax.broadcasted_iota(jnp.int32, (2 * half_rows, size_z), 0) < half_rows

    def solve_lines(arriving, received, power, answers, landing):
        for copy in arriving:
            copy.wait()
        values = [received[k] for k in range(nx)]
        behind, ahead = sweep(True, power, values), sweep(False, power, values)
        for k in range(nx):
            answers[k] = jnp.where(from_behind, behind[k], ahead[k])
        leaving = [remote(answers.at[k], landing.at[me_x], "gx", -k) for k in farthest]
        for copy in leaving:
            copy.start()
        landing[me_x] = answers[0]
        return leaving

    xo = solve_lines(xm, xm_in, ratio**size_x, xo_out, xo_in)

    def scan_chunk(chunk, _):
        ys = pl.ds(pl.multiple_of(chunk * 8, 8), 8)

        def scan(side, step, carried):
            carried = list(carried)
            for inner in range(unroll):
                x = step * unroll + inner
                x = size_x - 1 - x if side else x
                gains = (-amplitude, -corner) if side else (amplitude, corner)
                for f in range(fields):
                    total, last = carried[f], carried[5 + f]
                    tend[f, x, ys, :] += gains[0] * total + gains[1] * last
                    here = fx[f, x, ys, :]
                    carried[f], carried[5 + f] = ratio * (total + here), here
            return tuple(carried)

        for side in range(2):
            lax.fori_loop(0, size_x // unroll, functools.partial(scan, side), (zero,) * 10)
        return 0

    lax.fori_loop(0, size_y // 8, scan_chunk, 0)

    io = solve_lines(uv, uv_in, filter_ratio**size_x, io_out, io_in)
    for copy in xn:
        copy.wait()
    tend[:, 0] += corner * xn_in[0]
    tend[:, size_x - 1] -= corner * xn_in[1]

    for side in range(2):
        sign = -time_step if side else time_step
        carry_d[side] = sign * (corner_d * xn_in[side] + far_d * moments_x[1 - side] + first_d * xn_out[1 - side])

    for copy in yb + zm:
        copy.wait()

    def carries(f, _):
        both = span_carries(zm_in[:, f].reshape(8 * nz, half * size_y))
        for part in range(size_x // 16):
            pair = [pl.ds(16 * part + 8 * side, 8) for side in range(2)]
            wall = wall_carries(yb_in[:, f, pair[0], :], yb_in[:, f, pair[1], :])
            for side, xs in enumerate(pair):
                row = (16 * part + 8 * side) % half * size_y
                lane = (16 * part + 8 * side) // half * size_z
                change = wall[:, side * size_z : (side + 1) * size_z]
                change = change + both[row : row + 8 * size_y, lane : lane + size_z]
                tend[f, xs] += change.reshape(8, size_y, size_z)
        return 0

    lax.fori_loop(0, fields, carries, 0)

    for copy in xo + io:
        copy.wait()
    carry_x[...] = xo_in[...]
    carry_f[...] = io_in[...]


def filter_kernel(den, mom, ene, part, carry_x, carry_f, carry_d, tend_hbm, after_hbm, tend, after, sems):
    chunks, fields, size_x = tend.shape[:3]
    half_rows = carry_x.shape[1] // 2
    rows = half_rows // fields
    owners = 8 // rows
    ratio, far_gain, _ = compact_kernel()
    filter_ratio, gain = decay(filter_alpha)
    straight = 0.5 * (0.5 + filter_alpha) / filter_alpha
    amplitude = (0.5 + filter_alpha - straight) * gain
    _, near_d, far_d, _, _ = filtered_derivative()
    power = ratio**size_x
    unroll = 4

    def copies(chunk):
        ys = pl.ds(pl.multiple_of(chunk * 8, 8), 8)
        return (
            pltpu.make_async_copy(tend.at[chunk], tend_hbm.at[:, :, ys], sems.at[0, chunk]),
            pltpu.make_async_copy(after.at[chunk], after_hbm.at[:, :, ys], sems.at[1, chunk]),
        )

    def chunk_body(chunk, _):
        ys = pl.ds(pl.multiple_of(chunk * 8, 8), 8)

        def carried_in(ref, side, f):
            place = side * half_rows + rows * f
            return jnp.concatenate(
                [ref[chunk * owners + o, place : place + rows, :] for o in range(owners)], axis=0
            )

        def state(f, x):
            return den[x, ys, :] if f == 0 else ene[x, ys, :] if f == 4 else mom[f - 1, x, ys, :]

        from_l = [carried_in(carry_x, 0, f) for f in range(fields)]
        from_r = [carried_in(carry_x, 1, f) for f in range(fields)]
        start_l = [
            carried_in(carry_f, 0, f)
            + carry_d[0, f, ys, :]
            + time_step * (near_d * from_l[f] + float(far_d * power) * from_r[f])
            for f in range(fields)
        ]
        start_r = [
            carried_in(carry_f, 1, f)
            + carry_d[1, f, ys, :]
            - time_step * (near_d * from_r[f] + float(far_d * power) * from_l[f])
            for f in range(fields)
        ]
        head = [float(far_gain * ratio ** (size_x - 1)) * from_l[f] for f in range(fields)]
        tail = [far_gain * from_r[f] for f in range(fields)]

        def back(step, carried):
            carried = list(carried)
            for inner in range(unroll):
                x = size_x - 1 - (step * unroll + inner)
                for f in range(fields):
                    behind, ahead = carried[5 + f], carried[10 + f]
                    rate = ahead - behind - part[f, x, ys, :]
                    tend[chunk, f, x] = rate
                    after[chunk, f, x] = amplitude * carried[f]
                    carried[f] = filter_ratio * (carried[f] + (state(f, x) + time_step * rate))
                    carried[5 + f], carried[10 + f] = (1.0 / ratio) * behind, ratio * ahead
            return tuple(carried)

        def ahead(step, carried):
            carried = list(carried)
            for inner in range(unroll):
                x = step * unroll + inner
                for f in range(fields):
                    middle = state(f, x) + time_step * tend[chunk, f, x]
                    after[chunk, f, x] += (straight + amplitude) * middle + amplitude * carried[f]
                    carried[f] = filter_ratio * (carried[f] + middle)
            return tuple(carried)

        lax.fori_loop(0, size_x // unroll, back, tuple(start_r + head + tail))
        rate_copy, after_copy = copies(chunk)
        rate_copy.start()
        lax.fori_loop(0, size_x // unroll, ahead, tuple(start_l))
        after_copy.start()
        return 0

    lax.fori_loop(0, chunks, chunk_body, 0)
    for chunk in range(chunks):
        for copy in copies(chunk):
            copy.wait()


def solution(mesh):
    nx, ny, nz = mesh.shape["gx"], mesh.shape["gy"], mesh.shape["gz"]

    def on_device(density, momentum, energy, metric):
        size_x, size_y, size_z = density.shape
        fields = 5
        rows = size_y // nx
        float32 = jnp.float32
        ky, py = wall_tables(ny, size_y)
        kz, qz, pz = span_tables(nz, size_z)
        wtab = stream_weights(size_x).astype(np.float32)
        cells = (fields, size_x, size_y, size_z)
        owned = (nx, 2 * fields * rows, size_z)
        sides = (2, fields, size_y, size_z)
        vmem = pl.BlockSpec(memory_space=pltpu.VMEM)
        stays = pl.BlockSpec(memory_space=pltpu.HBM)
        copies = 2 + 4 * (nx - 1) + 6 + 2 * (nz - 1)
        chunks = size_y // 8
        part, carry_x, carry_f, carry_d = pl.pallas_call(
            functools.partial(exchange_kernel, nx, ny, nz),
            out_shape=[
                jax.ShapeDtypeStruct(cells, float32),
                jax.ShapeDtypeStruct(owned, float32),
                jax.ShapeDtypeStruct(owned, float32),
                jax.ShapeDtypeStruct(sides, float32),
            ],
            in_specs=[stays] * 10,
            out_specs=[vmem] * 4,
            scratch_shapes=[
                pltpu.VMEM(cells[1:], float32),
                pltpu.VMEM((3,) + cells[1:], float32),
                pltpu.VMEM(cells[1:], float32),
                pltpu.VMEM((1, ny * size_y), float32),
                pltpu.SMEM(wtab.shape, float32),
                pltpu.VMEM(ky.shape[1:], float32),
                pltpu.VMEM(py.shape[1:], float32),
                pltpu.VMEM(kz.shape, bfloat16),
                pltpu.VMEM(qz.shape, bfloat16),
                pltpu.VMEM(pz.shape, bfloat16),
                pltpu.VMEM(ky.shape[1:], bfloat16),
                pltpu.VMEM(ky.shape[1:], bfloat16),
                pltpu.VMEM(py.shape[1:], bfloat16),
                pltpu.VMEM(cells, float32),
                pltpu.VMEM(cells, float32),
                pltpu.VMEM(cells, float32),
                pltpu.VMEM(sides, float32),
                pltpu.VMEM(sides, float32),
                pltpu.VMEM((16, size_y, size_z), float32),
                pltpu.VMEM((2, 8, size_y, size_z), float32),
                pltpu.VMEM((16, size_y, size_z), float32),
                pltpu.VMEM((2, 8, size_y, size_z), float32),
                pltpu.VMEM((4, 16, size_z), float32),
                pltpu.VMEM((8, 16, size_z), float32),
                pltpu.VMEM((nz, 8, 8 * size_y), float32),
                pltpu.VMEM((4, fields, size_x, size_z), float32),
                pltpu.VMEM((8, fields, size_x, size_z), float32),
                pltpu.VMEM((nz, fields, 8, size_x // 2 * size_y), float32),
                pltpu.VMEM(sides, float32),
                pltpu.VMEM(sides, float32),
                pltpu.VMEM(owned, float32),
                pltpu.VMEM(owned, float32),
                pltpu.VMEM(owned, float32),
                pltpu.VMEM(owned, float32),
                pltpu.VMEM(owned, float32),
                pltpu.VMEM(owned, float32),
                pltpu.VMEM(owned, float32),
                pltpu.VMEM(owned, float32),
                pltpu.SemaphoreType.DMA((3, chunks)),
                pltpu.SemaphoreType.DMA((7,)),
                pltpu.SemaphoreType.DMA((copies,)),
                pltpu.SemaphoreType.DMA((copies,)),
            ],
            compiler_params=pltpu.CompilerParams(
                collective_id=0, has_side_effects=True, vmem_limit_bytes=24 * 1024 * 1024
            ),
            cost_estimate=pl.CostEstimate(flops=4 * 10**9, bytes_accessed=10**7, transcendentals=0),
        )(
            *[
                pltpu.with_memory_space_constraint(jnp.asarray(value), pltpu.HBM)
                for value in (density, momentum, energy, metric.reshape(1, -1), wtab, ky, py, kz, qz, pz)
            ]
        )
        return pl.pallas_call(
            filter_kernel,
            out_shape=[jax.ShapeDtypeStruct(cells, float32), jax.ShapeDtypeStruct(cells, float32)],
            in_specs=[vmem] * 7,
            out_specs=[stays] * 2,
            scratch_shapes=[
                pltpu.VMEM((chunks, fields, size_x, 8, size_z), float32),
                pltpu.VMEM((chunks, fields, size_x, 8, size_z), float32),
                pltpu.SemaphoreType.DMA((2, chunks)),
            ],
            compiler_params=pltpu.CompilerParams(vmem_limit_bytes=16 * 1024 * 1024),
            cost_estimate=pl.CostEstimate(flops=10**7, bytes_accessed=10**7, transcendentals=0),
        )(density, momentum, energy, part, carry_x, carry_f, carry_d)

    return jax.shard_map(
        on_device,
        mesh=mesh,
        in_specs=(P("gx", "gy", "gz"), P(None, "gx", "gy", "gz"), P("gx", "gy", "gz"), P()),
        out_specs=(P(None, "gx", "gy", "gz"), P(None, "gx", "gy", "gz")),
        check_vma=False,
    )
```

```python
import functools

import jax
import jax.numpy as jnp
import numpy as np
from jax import lax
from jax.experimental import pallas as pl
from jax.experimental.pallas import tpu as pltpu
from jax.sharding import PartitionSpec as P

heat_ratio = 1.4
compact_alpha = 1.0 / 3.0
filter_alpha = 0.499
time_step = 0.05
near_weight = 7.0 / 9.0
wide_weight = 1.0 / 36.0
bfloat16 = jnp.bfloat16
MESH = pl.DeviceIdType.MESH
KINDS_Y = ((1, "last"), (1, "ml"), (1, "mr"), (2, "ml"), (2, "mr"), (3, "ml"), (3, "mr"), (3, "first"))


def decay(alpha):
    root = np.sqrt(1.0 - 4.0 * alpha * alpha)
    return (-1.0 + root) / (2.0 * alpha), 1.0 / root


def compact_kernel():
    ratio, gain = decay(compact_alpha)

    def green(n):
        return gain * ratio ** abs(n)

    def kernel(d):
        return near_weight * (green(d + 1) - green(d - 1)) + wide_weight * (green(d + 2) - green(d - 2))

    amplitude = kernel(2) / ratio**2
    return ratio, amplitude, kernel(1) - amplitude * ratio


def local_compact(size):
    ratio, amplitude, corner = compact_kernel()
    table = np.zeros((size, size))
    for i in range(size):
        for j in range(size):
            d = abs(i - j)
            if d:
                value = amplitude * ratio**d + (corner if d == 1 else 0.0)
                table[i, j] = value if i > j else -value
    return table


def table_thomas(lower_band, main_band, upper_band, source):
    count = source.shape[0]
    c_all = np.zeros(count)
    d_all = np.zeros(source.shape)
    c_prev = 0.0
    d_prev = np.zeros(source.shape[1:])
    for place in range(count):
        denom = main_band[place] - lower_band[place] * c_prev
        c_prev = upper_band[place] / denom
        d_prev = (source[place] - lower_band[place] * d_prev) / denom
        c_all[place] = c_prev
        d_all[place] = d_prev
    solved = np.zeros(source.shape)
    x_next = np.zeros(source.shape[1:])
    for place in range(count - 1, -1, -1):
        x_next = d_all[place] - c_all[place] * x_next
        solved[place] = x_next
    return solved


def wall_bands(total):
    lower = np.full(total, compact_alpha)
    upper = np.full(total, compact_alpha)
    lower[0], lower[1], lower[total - 2], lower[total - 1] = 0.0, 0.25, 0.25, 2.0
    upper[0], upper[1], upper[total - 2], upper[total - 1] = 2.0, 0.25, 0.25, 0.0
    return lower, upper


def wall_table(total):
    lower, upper = wall_bands(total)
    stencil = np.zeros((total, total))
    for i in range(2, total - 2):
        stencil[i, i + 1], stencil[i, i - 1] = near_weight, -near_weight
        stencil[i, i + 2], stencil[i, i - 2] = wide_weight, -wide_weight
    for i in (1, total - 2):
        stencil[i, i + 1], stencil[i, i - 1] = 0.75, -0.75
    stencil[0, :3] = (-2.5, 2.0, 0.5)
    stencil[total - 1, total - 3 :] = (-0.5, -2.0, 2.5)
    return table_thomas(lower, np.ones(total), upper, stencil)


@functools.cache
def wall_tables(blocks, size):
    total = blocks * size
    table = wall_table(total)
    lower, upper = wall_bands(total)
    down = np.zeros(total)
    for i in range(total - 1, 0, -1):
        down[i - 1] = -lower[i] / (1.0 + upper[i] * down[i])
    up = np.zeros(total)
    for i in range(total - 1):
        up[i + 1] = -upper[i] / (1.0 + lower[i] * up[i])
    carry_l, carry_r, corner_l, corner_r = [], [], [], []
    moment_l, moment_r = np.zeros((blocks, size)), np.zeros((blocks, size))
    for b in range(blocks):
        head, tail = b * size, b * size + size - 1
        carry_l.append(np.concatenate([[1.0], np.cumprod(down[head:tail])]))
        carry_r.append(np.concatenate([[1.0], np.cumprod(up[head + 1 : tail + 1][::-1])])[::-1])
        corner_l.append(table[head, head - 1] - table[head + 1, head - 1] / down[head] if b else 0.0)
        corner_r.append(table[tail, tail + 1] - table[tail - 1, tail + 1] / up[tail] if b < blocks - 1 else 0.0)
        if b < blocks - 1:
            to = tail + 1
            moment_l[b] = table[to, head:to]
            moment_l[b, size - 1] = table[to + 1, tail] / down[to]
        if b:
            to = head - 1
            moment_r[b] = table[to, head : tail + 1]
            moment_r[b, 0] = table[to - 1, head] / up[to]
    apply = np.zeros((blocks, 8 * size + 32, 8 * size))
    carry = np.zeros((blocks, 8 * size, 8 * len(KINDS_Y)))
    eye = np.eye(8)
    for b in range(blocks):
        rows = slice(b * size, (b + 1) * size)
        apply[b, : 8 * size] = np.kron(eye, table[rows, rows])
        first, last = np.eye(size)[0], np.eye(size)[size - 1]
        for kind, weights in enumerate((last, moment_l[b], moment_r[b], first)):
            apply[b, 8 * size + 8 * kind : 8 * size + 8 * kind + 8] = np.kron(eye, weights[None])
        for place, (offset, kind) in enumerate(KINDS_Y):
            column = np.zeros(size)
            if b - offset >= 0:
                if kind == "ml":
                    scale = 1.0
                    for c in range(b - offset + 1, b):
                        scale *= np.prod(down[c * size : (c + 1) * size])
                    column = scale * carry_l[b]
                elif kind == "last" and offset == 1:
                    column[0] = corner_l[b]
            else:
                distance = blocks - offset
                if kind == "mr":
                    scale = 1.0
                    for c in range(b + 1, b + distance):
                        scale *= np.prod(up[c * size : (c + 1) * size])
                    column = scale * carry_r[b]
                elif kind == "first" and distance == 1:
                    column[size - 1] = corner_r[b]
            carry[b, :, 8 * place : 8 * place + 8] = np.kron(eye, column[:, None])
    return apply.astype(np.float32), np.concatenate([carry] * 3, axis=2).astype(np.float32)


def table_split(table):
    high = table.astype(bfloat16)
    return high, (table - high.astype(np.float64)).astype(bfloat16)


@functools.cache
def span_tables(blocks, size):
    ratio, amplitude, corner = compact_kernel()
    places = np.arange(size)
    images = 1.0 / (1.0 - ratio ** (blocks * size))
    moments = np.zeros((4, size))
    moments[0, size - 1] = 1.0
    moments[1] = ratio ** (size - places)
    moments[2] = ratio ** (places + 1.0)
    moments[3, 0] = 1.0
    carries = np.zeros((blocks, 4, size))
    for slot in range(blocks):
        behind = slot if slot else blocks
        ahead = blocks - slot
        carries[slot, 1] = amplitude * images * ratio ** (size * (behind - 1.0)) * ratio**places
        carries[slot, 2] = -amplitude * images * ratio ** (size * (ahead - 1.0)) * ratio ** (size - 1.0 - places)
        if behind == 1:
            carries[slot, 0, 0] = corner
        if ahead == 1:
            carries[slot, 3, size - 1] = -corner
    both_moments = np.zeros((8, 2 * size))
    both_moments[:4, :size] = moments
    both_moments[4:, size:] = moments
    both_carries = np.zeros((blocks, 8, 2 * size))
    both_carries[:, :4, :size] = carries
    both_carries[:, 4:, size:] = carries
    local_high, local_low = table_split(local_compact(size).T)
    carry_high, carry_low = table_split(both_carries.reshape(8 * blocks, 2 * size))
    return (
        np.block([[local_high, local_low], [local_high, np.zeros_like(local_low)]]),
        np.concatenate(table_split(both_moments)),
        np.concatenate([carry_high, carry_high, carry_low]),
    )


def stream_weights(size):
    ratio, _, _ = compact_kernel()
    filter_ratio, _ = decay(filter_alpha)
    places = np.arange(size)
    return np.stack(
        [
            filter_ratio ** (size - places),
            filter_ratio ** (places + 1.0),
            ratio ** (size - places),
            ratio ** (places + 1.0),
        ]
    )


def filtered_derivative():
    ratio, amplitude, corner = compact_kernel()
    filter_ratio, _ = decay(filter_alpha)
    over, times = ratio / filter_ratio, ratio * filter_ratio
    gain = amplitude * (over / (1.0 - over) - times / (1.0 - times)) + corner * (1.0 / filter_ratio - filter_ratio)
    return gain, amplitude / (1.0 - over), amplitude * filter_ratio / (1.0 - times), corner, corner * filter_ratio


def split(values):
    high = values.astype(bfloat16)
    return high, (values - high.astype(jnp.float32)).astype(bfloat16)


def product(left, right, sides=((1,), (0,))):
    return lax.dot_general(left, right, (sides, ((), ())), preferred_element_type=jnp.float32)


def exchange_kernel(
    nx,
    ny,
    nz,
    den_hbm,
    mom_hbm,
    ene_hbm,
    metric_hbm,
    wtab_hbm,
    ky_hbm,
    py_hbm,
    kz_hbm,
    qz_hbm,
    pz_hbm,
    tend,
    carry_x,
    carry_f,
    carry_d,
    carry_n,
    den,
    mom,
    ene,
    metric,
    wtab,
    ky,
    py,
    kz,
    qz,
    pz,
    ky_high,
    ky_low,
    py_both,
    fx,
    fy,
    fz,
    uv0,
    moments_x,
    sy,
    sz,
    dys,
    dzs,
    ys_out,
    ys_in,
    zs_in,
    yb_out,
    yb_in,
    zm_in,
    xn_out,
    xn_in,
    pair_in,
    xm_out,
    xm_in,
    uv_out,
    uv_in,
    xo_out,
    xo_in,
    xp_in,
    io_out,
    io_in,
    state_sem,
    load_sem,
    send_sem,
    recv_sem,
):
    fields, size_x, size_y, size_z = fx.shape
    me_x, me_y, me_z = lax.axis_index("gx"), lax.axis_index("gy"), lax.axis_index("gz")
    rows = size_y // nx
    ratio, amplitude, corner = compact_kernel()
    filter_ratio, _ = decay(filter_alpha)
    gain_d, _, far_d, corner_d, first_d = filtered_derivative()
    half_rows = fields * rows
    chips = nx // 2
    chip, core = me_x // 2, lax.rem(me_x, 2)
    pair = 1 - 2 * core
    half_y = size_y // 2

    def farthest(count):
        return sorted(range(1, count), key=lambda k: -min(k, count - k))

    def along(axis, offset):
        me, count = {"gx": (me_x, nx), "gy": (me_y, ny), "gz": (me_z, nz)}[axis]
        return lax.rem(me + offset + count, count)

    def state_loads(chunk):
        ys = pl.ds(pl.multiple_of(chunk * 8, 8), 8)
        return [
            pltpu.make_async_copy(den_hbm.at[:, ys], den.at[:, ys], state_sem.at[0, chunk]),
            pltpu.make_async_copy(mom_hbm.at[:, :, ys], mom.at[:, :, ys], state_sem.at[1, chunk]),
            pltpu.make_async_copy(ene_hbm.at[:, ys], ene.at[:, ys], state_sem.at[2, chunk]),
        ]

    sources = (wtab_hbm, ky_hbm.at[me_y], py_hbm.at[me_y], metric_hbm, kz_hbm, qz_hbm, pz_hbm)
    targets = (wtab, ky, py, metric, kz, qz, pz)
    loads = [
        pltpu.make_async_copy(source, target, load_sem.at[place])
        for place, (source, target) in enumerate(zip(sources, targets))
    ]
    loads[0].start()
    for chunk in range(size_y // 8):
        for load in state_loads(chunk):
            load.start()
    for load in loads[1:]:
        load.start()

    yb_in[...] = jnp.zeros(yb_in.shape, jnp.float32)

    barrier = pltpu.get_barrier_semaphore()
    for axis, count in (("gx", nx), ("gy", ny), ("gz", nz)):
        for offset in range(1, count):
            pl.semaphore_signal(barrier, inc=1, device_id={axis: along(axis, offset)}, device_id_type=MESH)

    next_sem = [0]

    def remote(src, dst, axis, offset):
        place = next_sem[0]
        next_sem[0] = place + 1
        return pltpu.make_async_remote_copy(
            src_ref=src,
            dst_ref=dst,
            send_sem=send_sem.at[place],
            recv_sem=recv_sem.at[place],
            device_id={axis: along(axis, offset)},
            device_id_type=MESH,
        )

    loads[0].wait()

    unroll = 4
    zero = jnp.zeros((8, size_z), jnp.float32)

    def flux_chunk(chunk, _):
        ys = pl.ds(pl.multiple_of(chunk * 8, 8), 8)
        for load in state_loads(chunk):
            load.wait()

        def cells(step, acc):
            acc = list(acc)
            for inner in range(unroll):
                x = step * unroll + inner
                w = [wtab[k, x] for k in range(4)]
                rho, energy = den[x, ys, :], ene[x, ys, :]
                m = [mom[j, x, ys, :] for j in range(3)]
                inverse = 1.0 / rho
                v = [m[j] * inverse for j in range(3)]
                own = [m[j] * v[j] for j in range(3)]
                pressure = (heat_ratio - 1.0) * (energy - 0.5 * (own[0] + own[1] + own[2]))
                m12, m13, m23 = m[0] * v[1], m[0] * v[2], m[1] * v[2]
                total = energy + pressure
                flux_x = (m[0], own[0] + pressure, m12, m13, total * v[0])
                flux_y = (m[1], m12, own[1] + pressure, m23, total * v[1])
                flux_z = (m[2], m13, m23, own[2] + pressure, total * v[2])
                state = (rho, m[0], m[1], m[2], energy)
                for f in range(fields):
                    fx[f, x, ys, :] = flux_x[f]
                    fy[f, x, ys, :] = flux_y[f]
                    fz[f, x, ys, :] = flux_z[f]
                    change = (time_step * gain_d) * flux_x[f]
                    acc[f] = acc[f] + w[0] * (state[f] - change)
                    acc[5 + f] = acc[5 + f] + w[1] * (state[f] + change)
                    acc[10 + f] = acc[10 + f] + w[2] * flux_x[f]
                    acc[15 + f] = acc[15 + f] + w[3] * flux_x[f]
            return tuple(acc)

        acc = lax.fori_loop(0, size_x // unroll, cells, (zero,) * 20)
        for f in range(fields):
            uv0[0, f, ys, :] = acc[f]
            uv0[1, f, ys, :] = acc[5 + f]
            moments_x[0, f, ys, :] = acc[10 + f]
            moments_x[1, f, ys, :] = acc[15 + f]
            xn_out[0, f, ys, :] = fx[f, size_x - 1, ys, :]
            xn_out[1, f, ys, :] = fx[f, 0, ys, :]
        return 0

    sy[10:16] = jnp.zeros((6, size_y, size_z), jnp.float32)
    sz[:, 5:8] = jnp.zeros((2, 3, size_y, size_z), jnp.float32)
    lax.fori_loop(0, size_y // 8, flux_chunk, 0)

    def deal(message, side, f, values):
        for owner in range(values.shape[0] // rows):
            place = side * half_rows + rows * f
            message[owner, place : place + rows, :] = values[rows * owner : rows * owner + rows]

    pl.semaphore_wait(barrier, nx + ny + nz - 3)
    to_pair = remote(moments_x, pair_in, "gx", pair)
    to_pair.start()

    def sums_chunk(chunk, _):
        ys = pl.ds(pl.multiple_of(chunk * 8, 8), 8)

        def sums(step, acc):
            acc = list(acc)
            for inner in range(unroll):
                x = step * unroll + inner
                w = [wtab[k, x] for k in range(2)]
                for f in range(fields):
                    value_y, value_z = fy[f, x, ys, :], fz[f, x, ys, :]
                    acc[f] = acc[f] + w[0] * value_y
                    acc[5 + f] = acc[5 + f] + w[1] * value_y
                    acc[10 + f] = acc[10 + f] + w[0] * value_z
                    acc[15 + f] = acc[15 + f] + w[1] * value_z
            return tuple(acc)

        acc = lax.fori_loop(0, size_x // unroll, sums, (zero,) * 20)
        for f in range(fields):
            sy[f, ys, :] = acc[f]
            sy[5 + f, ys, :] = acc[5 + f]
            sz[0, f, ys, :] = acc[10 + f]
            sz[1, f, ys, :] = acc[15 + f]
        return 0

    lax.fori_loop(0, size_y // 8, sums_chunk, 0)

    for load in loads[1:]:
        load.wait()
    shape = (8 * size_y, ny * size_y)
    row_place = lax.broadcasted_iota(jnp.int32, shape, 0)
    col_place = lax.broadcasted_iota(jnp.int32, shape, 1)
    mine = col_place == me_y * size_y + lax.rem(row_place, size_y)
    metric_rows = jnp.sum(jnp.where(mine, metric[...], 0.0), axis=1, keepdims=True)
    ky[: 8 * size_y, :] = ky[: 8 * size_y, :] * metric_rows
    ky_high[...], ky_low[...] = split(ky[...])
    high, low = split(py[...] * metric_rows)
    py_both[...] = jnp.where(lax.broadcasted_iota(jnp.int32, py.shape, 1) < 128, high, low)

    def apply_wall(first, second):
        cells = jnp.concatenate(
            [first.reshape(8 * size_y, size_z), second.reshape(8 * size_y, size_z)], axis=1
        )
        high, low = split(cells)
        result = product(ky_high[...], high) + product(ky_high[...], low) + product(ky_low[...], high)
        return [
            (
                result[: 8 * size_y, lanes].reshape(8, size_y, size_z),
                result[8 * size_y :, lanes].reshape(4, 8, size_z),
            )
            for lanes in (slice(0, size_z), slice(size_z, 2 * size_z))
        ]

    def wall_carries(first, second):
        cells = jnp.concatenate([first.reshape(64, size_z), second.reshape(64, size_z)], axis=1)
        high, low = split(cells)
        return product(py_both[...], jnp.concatenate([high, low, high], axis=0))

    def span_local(cells):
        result = product(jnp.concatenate(split(cells), axis=1), kz[...])
        return result[:, :size_z] + result[:, size_z:]

    def span_moments(first, second):
        high, low = split(jnp.concatenate([first, second], axis=1))
        from_high = product(qz[...], high, ((1,), (1,)))
        from_low = product(qz[...], low, ((1,), (1,)))
        return from_high[:8] + from_high[8:] + (from_low[:8] + from_low[8:])

    def span_carries(received):
        high, low = split(received)
        return product(jnp.concatenate([high, low, high], axis=0), pz[...], ((0,), (0,)))

    for group, (local, moments) in enumerate(apply_wall(sy[0:8], sy[8:16])):
        dys[8 * group : 8 * group + 8] = local
        ys_out[:, 8 * group : 8 * group + 8, :] = moments
    ys = [
        remote(ys_out.at[pl.ds(0, 3)], ys_in.at[pl.ds(0, 3)], "gy", 1),
        remote(ys_out.at[pl.ds(1, 2)], ys_in.at[pl.ds(3, 2)], "gy", 2),
        remote(ys_out.at[pl.ds(1, 3)], ys_in.at[pl.ds(5, 3)], "gy", 3),
    ]
    for copy in ys:
        copy.start()
    zs_in[0] = span_moments(sz[0].reshape(8 * size_y, size_z), sz[1].reshape(8 * size_y, size_z))
    zs = [remote(zs_in.at[0], zs_in.at[k], "gz", k) for k in range(1, nz)]
    for copy in zs:
        copy.start()
    dzs[...] = span_local(sz[...].reshape(16 * size_y, size_z)).reshape(2, 8, size_y, size_z)

    to_pair.wait()
    power = float(ratio**size_x)
    second = core == 1
    mine = pl.ds(pl.multiple_of(half_y * core, 8), half_y)
    for side in range(2):
        is_near = second if side == 0 else jnp.logical_not(second)
        own_gain, pair_gain = jnp.where(is_near, 1.0, power), jnp.where(is_near, power, 1.0)
        for f in range(fields):
            deal(xm_out, side, f, own_gain * moments_x[side, f, mine, :] + pair_gain * pair_in[side, f, mine, :])
        carry_n[side] = jnp.where(is_near, 1.0, 0.0) * pair_in[side]
    xm = [remote(xm_out.at[lax.rem(chip + k, chips)], xm_in.at[k], "gx", 2 * k) for k in farthest(chips)]
    for copy in xm:
        copy.start()
    xm_in[0] = xm_out[chip]

    def wall_field(f, _):
        for part in range(size_x // 16):
            pair = [pl.ds(16 * part + 8 * side, 8) for side in range(2)]
            for xs, (local, moments) in zip(pair, apply_wall(fy[f, pair[0]], fy[f, pair[1]])):
                tend[f, xs] = local
                yb_out[:, f, xs, :] = moments
        return 0

    lax.fori_loop(0, fields, wall_field, 0)
    yb = []
    for distance in range(1, ny):
        count = 2 if distance == 1 else 1
        up_place = KINDS_Y.index((distance, "last" if distance == 1 else "ml"))
        down_place = KINDS_Y.index((ny - distance, "mr"))
        up = remote(yb_out.at[pl.ds(2 - count, count)], yb_in.at[pl.ds(up_place, count)], "gy", distance)
        down = remote(yb_out.at[pl.ds(2, count)], yb_in.at[pl.ds(down_place, count)], "gy", -distance)
        has_above, has_below = me_y < ny - distance, me_y >= distance
        yb += [(up, has_above, has_below), (down, has_below, has_above)]
    for copy, sends, _ in yb:
        pl.when(sends)(copy.start)

    for copy in ys + zs:
        copy.wait()
    span = span_carries(zs_in[...].reshape(8 * nz, 8 * size_y))
    wall = wall_carries(ys_in[:, 0:8, :], ys_in[:, 8:16, :])
    for side in range(2):
        for f in range(fields):
            unit = 5 * side + f
            place, lane = (unit % 8) * size_y, (unit // 8) * size_z
            change = dys[unit] + wall[place : place + size_y, lane : lane + size_z]
            change = change + dzs[side, f] + span[f * size_y : (f + 1) * size_y, side * size_z : (side + 1) * size_z]
            deal(uv_out, side, f, uv0[side, f] - time_step * change)
    uv = [remote(uv_out.at[along("gx", k)], uv_in.at[k], "gx", k) for k in farthest(nx)]
    for copy in uv:
        copy.start()
    uv_in[0] = uv_out[me_x]

    xn = [
        remote(xn_out.at[0], xn_in.at[0], "gx", 1),
        remote(xn_out.at[1], xn_in.at[1], "gx", -1),
    ]
    for copy in xn:
        copy.start()

    half = size_x // 2

    def span_field(f, _):
        pair = [fz[f, pl.ds(part * half, half)].reshape(half * size_y, size_z) for part in range(2)]
        zm_in[0, f] = span_moments(*pair)
        return 0

    lax.fori_loop(0, fields, span_field, 0)
    zm = [remote(zm_in.at[0], zm_in.at[k], "gz", k) for k in range(1, nz)]
    for copy in zm:
        copy.start()

    def span_cells(f, _):
        for part in range(size_x // 8):
            xs = pl.ds(8 * part, 8)
            tend[f, xs] += span_local(fz[f, xs].reshape(8 * size_y, size_z)).reshape(8, size_y, size_z)
        return 0

    lax.fori_loop(0, fields, span_cells, 0)

    def sweep(behind, power, values):
        step, count = 1 if behind else -1, len(values)
        total = values[0] if behind else values[count - 1]
        for k in range(1, count):
            total = total + float(power**k) * (values[k] if behind else values[count - 1 - k])
        total = total * float(1.0 / (1.0 - power**count))
        place = count - 1 if behind else 0
        result = [None] * count
        result[place] = total
        for _ in range(count - 1):
            total = values[place] + float(power) * total
            place = place - step
            result[place] = total
        return result

    from_behind = lax.broadcasted_iota(jnp.int32, (2 * half_rows, size_z), 0) < half_rows

    def solve_lines(received, power, answers):
        values = [received[k] for k in range(received.shape[0])]
        behind, ahead = sweep(True, power, values), sweep(False, power, values)
        for k in range(len(values)):
            answers[k] = jnp.where(from_behind, behind[k], ahead[k])

    for copy in xm:
        copy.wait()
    solve_lines(xm_in, ratio ** (2 * size_x), xo_out)
    xo = [remote(xo_out.at[k], xo_in.at[chip], "gx", -2 * k) for k in farthest(chips)]
    for copy in xo:
        copy.start()
    xo_in[chip] = xo_out[0]

    for copy in uv:
        copy.wait()
    solve_lines(uv_in, filter_ratio**size_x, io_out)
    io = [remote(io_out.at[k], io_in.at[me_x], "gx", -k) for k in farthest(nx)]
    for copy in io:
        copy.start()
    io_in[me_x] = io_out[0]

    for copy in xn:
        copy.wait()
    tend[:, 0] += corner * xn_in[0]
    tend[:, size_x - 1] -= corner * xn_in[1]

    for side in range(2):
        sign = -time_step if side else time_step
        carry_d[side] = sign * (corner_d * xn_in[side] + far_d * moments_x[1 - side] + first_d * xn_out[1 - side])

    def scan_chunk(chunk, _):
        ys = pl.ds(pl.multiple_of(chunk * 8, 8), 8)

        def scan(side, step, carried):
            carried = list(carried)
            for inner in range(unroll):
                x = step * unroll + inner
                x = size_x - 1 - x if side else x
                gains = (-amplitude, -corner) if side else (amplitude, corner)
                for f in range(fields):
                    total, last = carried[f], carried[5 + f]
                    tend[f, x, ys, :] += gains[0] * total + gains[1] * last
                    here = fx[f, x, ys, :]
                    carried[f], carried[5 + f] = ratio * (total + here), here
            return tuple(carried)

        for side in range(2):
            lax.fori_loop(0, size_x // unroll, functools.partial(scan, side), (zero,) * 10)
        return 0

    lax.fori_loop(0, size_y // 8, scan_chunk, 0)

    for copy in xo:
        copy.wait()
    halves = remote(xo_in, xp_in, "gx", pair)
    halves.start()

    for copy in zm:
        copy.wait()
    for copy, sends, receives in yb:
        pl.when(sends)(copy.wait_send)
        pl.when(receives)(copy.wait_recv)

    def carries(f, _):
        both = span_carries(zm_in[:, f].reshape(8 * nz, half * size_y))
        for part in range(size_x // 16):
            pair = [pl.ds(16 * part + 8 * side, 8) for side in range(2)]
            wall = wall_carries(yb_in[:, f, pair[0], :], yb_in[:, f, pair[1], :])
            for side, xs in enumerate(pair):
                row = (16 * part + 8 * side) % half * size_y
                lane = (16 * part + 8 * side) // half * size_z
                change = wall[:, side * size_z : (side + 1) * size_z]
                change = change + both[row : row + 8 * size_y, lane : lane + size_z]
                tend[f, xs] += change.reshape(8, size_y, size_z)
        return 0

    lax.fori_loop(0, fields, carries, 0)

    halves.wait()
    gains = jnp.where(from_behind, jnp.where(second, power, 1.0), jnp.where(second, 1.0, power))
    carry_x[pl.ds(chips * core, chips)] = xo_in[...] * gains
    carry_x[pl.ds(chips * (1 - core), chips)] = xp_in[...] * gains
    for copy in io:
        copy.wait()
    carry_f[...] = io_in[...]


def filter_kernel(den, mom, ene, part, carry_x, carry_f, carry_d, carry_n, tend_hbm, after_hbm, tend, after, sems):
    chunks, fields, size_x = tend.shape[:3]
    half_rows = carry_x.shape[1] // 2
    rows = half_rows // fields
    owners = 8 // rows
    ratio, far_gain, _ = compact_kernel()
    filter_ratio, gain = decay(filter_alpha)
    straight = 0.5 * (0.5 + filter_alpha) / filter_alpha
    amplitude = (0.5 + filter_alpha - straight) * gain
    _, near_d, far_d, _, _ = filtered_derivative()
    power = ratio**size_x
    unroll = 4

    def copies(chunk):
        ys = pl.ds(pl.multiple_of(chunk * 8, 8), 8)
        return (
            pltpu.make_async_copy(tend.at[chunk], tend_hbm.at[:, :, ys], sems.at[0, chunk]),
            pltpu.make_async_copy(after.at[chunk], after_hbm.at[:, :, ys], sems.at[1, chunk]),
        )

    def chunk_body(chunk, _):
        ys = pl.ds(pl.multiple_of(chunk * 8, 8), 8)

        def carried_in(ref, side, f):
            place = side * half_rows + rows * f
            return jnp.concatenate(
                [ref[chunk * owners + o, place : place + rows, :] for o in range(owners)], axis=0
            )

        def state(f, x):
            return den[x, ys, :] if f == 0 else ene[x, ys, :] if f == 4 else mom[f - 1, x, ys, :]

        from_l = [carried_in(carry_x, 0, f) + carry_n[0, f, ys, :] for f in range(fields)]
        from_r = [carried_in(carry_x, 1, f) + carry_n[1, f, ys, :] for f in range(fields)]
        start_l = [
            carried_in(carry_f, 0, f)
            + carry_d[0, f, ys, :]
            + time_step * (near_d * from_l[f] + float(far_d * power) * from_r[f])
            for f in range(fields)
        ]
        start_r = [
            carried_in(carry_f, 1, f)
            + carry_d[1, f, ys, :]
            - time_step * (near_d * from_r[f] + float(far_d * power) * from_l[f])
            for f in range(fields)
        ]
        head = [float(far_gain * ratio ** (size_x - 1)) * from_l[f] for f in range(fields)]
        tail = [far_gain * from_r[f] for f in range(fields)]

        def back(step, carried):
            carried = list(carried)
            for inner in range(unroll):
                x = size_x - 1 - (step * unroll + inner)
                for f in range(fields):
                    behind, ahead = carried[5 + f], carried[10 + f]
                    rate = ahead - behind - part[f, x, ys, :]
                    tend[chunk, f, x] = rate
                    after[chunk, f, x] = amplitude * carried[f]
                    carried[f] = filter_ratio * (carried[f] + (state(f, x) + time_step * rate))
                    carried[5 + f], carried[10 + f] = (1.0 / ratio) * behind, ratio * ahead
            return tuple(carried)

        def ahead(step, carried):
            carried = list(carried)
            for inner in range(unroll):
                x = step * unroll + inner
                for f in range(fields):
                    middle = state(f, x) + time_step * tend[chunk, f, x]
                    after[chunk, f, x] += (straight + amplitude) * middle + amplitude * carried[f]
                    carried[f] = filter_ratio * (carried[f] + middle)
            return tuple(carried)

        lax.fori_loop(0, size_x // unroll, back, tuple(start_r + head + tail))
        rate_copy, after_copy = copies(chunk)
        rate_copy.start()
        lax.fori_loop(0, size_x // unroll, ahead, tuple(start_l))
        after_copy.start()
        return 0

    lax.fori_loop(0, chunks, chunk_body, 0)
    for chunk in range(chunks):
        for copy in copies(chunk):
            copy.wait()


def solution(mesh):
    nx, ny, nz = mesh.shape["gx"], mesh.shape["gy"], mesh.shape["gz"]

    def on_device(density, momentum, energy, metric):
        size_x, size_y, size_z = density.shape
        fields = 5
        rows = size_y // nx
        float32 = jnp.float32
        ky, py = wall_tables(ny, size_y)
        kz, qz, pz = span_tables(nz, size_z)
        wtab = stream_weights(size_x).astype(np.float32)
        cells = (fields, size_x, size_y, size_z)
        owned = (nx, 2 * fields * rows, size_z)
        chipwise = (nx // 2, 2 * fields * rows, size_z)
        sides = (2, fields, size_y, size_z)
        vmem = pl.BlockSpec(memory_space=pltpu.VMEM)
        stays = pl.BlockSpec(memory_space=pltpu.HBM)
        copies = 7 + 2 * (nx - 1) + 2 * (nx // 2 - 1) + 2 * (ny - 1) + 2 * (nz - 1)
        chunks = size_y // 8
        part, carry_x, carry_f, carry_d, carry_n = pl.pallas_call(
            functools.partial(exchange_kernel, nx, ny, nz),
            out_shape=[
                jax.ShapeDtypeStruct(cells, float32),
                jax.ShapeDtypeStruct(owned, float32),
                jax.ShapeDtypeStruct(owned, float32),
                jax.ShapeDtypeStruct(sides, float32),
                jax.ShapeDtypeStruct(sides, float32),
            ],
            in_specs=[stays] * 10,
            out_specs=[vmem] * 5,
            scratch_shapes=[
                pltpu.VMEM(cells[1:], float32),
                pltpu.VMEM((3,) + cells[1:], float32),
                pltpu.VMEM(cells[1:], float32),
                pltpu.VMEM((1, ny * size_y), float32),
                pltpu.SMEM(wtab.shape, float32),
                pltpu.VMEM(ky.shape[1:], float32),
                pltpu.VMEM(py.shape[1:], float32),
                pltpu.VMEM(kz.shape, bfloat16),
                pltpu.VMEM(qz.shape, bfloat16),
                pltpu.VMEM(pz.shape, bfloat16),
                pltpu.VMEM(ky.shape[1:], bfloat16),
                pltpu.VMEM(ky.shape[1:], bfloat16),
                pltpu.VMEM(py.shape[1:], bfloat16),
                pltpu.VMEM(cells, float32),
                pltpu.VMEM(cells, float32),
                pltpu.VMEM(cells, float32),
                pltpu.VMEM(sides, float32),
                pltpu.VMEM(sides, float32),
                pltpu.VMEM((16, size_y, size_z), float32),
                pltpu.VMEM((2, 8, size_y, size_z), float32),
                pltpu.VMEM((16, size_y, size_z), float32),
                pltpu.VMEM((2, 8, size_y, size_z), float32),
                pltpu.VMEM((4, 16, size_z), float32),
                pltpu.VMEM((8, 16, size_z), float32),
                pltpu.VMEM((nz, 8, 8 * size_y), float32),
                pltpu.VMEM((4, fields, size_x, size_z), float32),
                pltpu.VMEM((8, fields, size_x, size_z), float32),
                pltpu.VMEM((nz, fields, 8, size_x // 2 * size_y), float32),
                pltpu.VMEM(sides, float32),
                pltpu.VMEM(sides, float32),
                pltpu.VMEM(sides, float32),
                pltpu.VMEM(chipwise, float32),
                pltpu.VMEM(chipwise, float32),
                pltpu.VMEM(owned, float32),
                pltpu.VMEM(owned, float32),
                pltpu.VMEM(chipwise, float32),
                pltpu.VMEM(chipwise, float32),
                pltpu.VMEM(chipwise, float32),
                pltpu.VMEM(owned, float32),
                pltpu.VMEM(owned, float32),
                pltpu.SemaphoreType.DMA((3, chunks)),
                pltpu.SemaphoreType.DMA((7,)),
                pltpu.SemaphoreType.DMA((copies,)),
                pltpu.SemaphoreType.DMA((copies,)),
            ],
            compiler_params=pltpu.CompilerParams(
                collective_id=0, has_side_effects=True, vmem_limit_bytes=24 * 1024 * 1024
            ),
            cost_estimate=pl.CostEstimate(flops=4 * 10**9, bytes_accessed=10**7, transcendentals=0),
        )(
            *[
                pltpu.with_memory_space_constraint(jnp.asarray(value), pltpu.HBM)
                for value in (density, momentum, energy, metric.reshape(1, -1), wtab, ky, py, kz, qz, pz)
            ]
        )
        return pl.pallas_call(
            filter_kernel,
            out_shape=[jax.ShapeDtypeStruct(cells, float32), jax.ShapeDtypeStruct(cells, float32)],
            in_specs=[vmem] * 8,
            out_specs=[stays] * 2,
            scratch_shapes=[
                pltpu.VMEM((chunks, fields, size_x, 8, size_z), float32),
                pltpu.VMEM((chunks, fields, size_x, 8, size_z), float32),
                pltpu.SemaphoreType.DMA((2, chunks)),
            ],
            compiler_params=pltpu.CompilerParams(vmem_limit_bytes=16 * 1024 * 1024),
            cost_estimate=pl.CostEstimate(flops=10**7, bytes_accessed=10**7, transcendentals=0),
        )(density, momentum, energy, part, carry_x, carry_f, carry_d, carry_n)

    return jax.shard_map(
        on_device,
        mesh=mesh,
        in_specs=(P("gx", "gy", "gz"), P(None, "gx", "gy", "gz"), P("gx", "gy", "gz"), P()),
        out_specs=(P(None, "gx", "gy", "gz"), P(None, "gx", "gy", "gz")),
        check_vma=False,
    )
```

```python
import functools

import jax
import jax.numpy as jnp
import numpy as np
from jax import lax
from jax.experimental import pallas as pl
from jax.experimental.pallas import tpu as pltpu
from jax.sharding import PartitionSpec as P

heat_ratio = 1.4
compact_alpha = 1.0 / 3.0
filter_alpha = 0.499
time_step = 0.05
near_weight = 7.0 / 9.0
wide_weight = 1.0 / 36.0
bfloat16 = jnp.bfloat16
MESH = pl.DeviceIdType.MESH
KINDS_Y = ((1, "last"), (1, "ml"), (1, "mr"), (2, "ml"), (2, "mr"), (3, "ml"), (3, "mr"), (3, "first"))


def decay(alpha):
    root = np.sqrt(1.0 - 4.0 * alpha * alpha)
    return (-1.0 + root) / (2.0 * alpha), 1.0 / root


def compact_kernel():
    ratio, gain = decay(compact_alpha)

    def green(n):
        return gain * ratio ** abs(n)

    def kernel(d):
        return near_weight * (green(d + 1) - green(d - 1)) + wide_weight * (green(d + 2) - green(d - 2))

    amplitude = kernel(2) / ratio**2
    return ratio, amplitude, kernel(1) - amplitude * ratio


def local_compact(size):
    ratio, amplitude, corner = compact_kernel()
    table = np.zeros((size, size))
    for i in range(size):
        for j in range(size):
            d = abs(i - j)
            if d:
                value = amplitude * ratio**d + (corner if d == 1 else 0.0)
                table[i, j] = value if i > j else -value
    return table


def table_thomas(lower_band, main_band, upper_band, source):
    count = source.shape[0]
    c_all = np.zeros(count)
    d_all = np.zeros(source.shape)
    c_prev = 0.0
    d_prev = np.zeros(source.shape[1:])
    for place in range(count):
        denom = main_band[place] - lower_band[place] * c_prev
        c_prev = upper_band[place] / denom
        d_prev = (source[place] - lower_band[place] * d_prev) / denom
        c_all[place] = c_prev
        d_all[place] = d_prev
    solved = np.zeros(source.shape)
    x_next = np.zeros(source.shape[1:])
    for place in range(count - 1, -1, -1):
        x_next = d_all[place] - c_all[place] * x_next
        solved[place] = x_next
    return solved


def wall_bands(total):
    lower = np.full(total, compact_alpha)
    upper = np.full(total, compact_alpha)
    lower[0], lower[1], lower[total - 2], lower[total - 1] = 0.0, 0.25, 0.25, 2.0
    upper[0], upper[1], upper[total - 2], upper[total - 1] = 2.0, 0.25, 0.25, 0.0
    return lower, upper


def wall_table(total):
    lower, upper = wall_bands(total)
    stencil = np.zeros((total, total))
    for i in range(2, total - 2):
        stencil[i, i + 1], stencil[i, i - 1] = near_weight, -near_weight
        stencil[i, i + 2], stencil[i, i - 2] = wide_weight, -wide_weight
    for i in (1, total - 2):
        stencil[i, i + 1], stencil[i, i - 1] = 0.75, -0.75
    stencil[0, :3] = (-2.5, 2.0, 0.5)
    stencil[total - 1, total - 3 :] = (-0.5, -2.0, 2.5)
    return table_thomas(lower, np.ones(total), upper, stencil)


@functools.cache
def wall_tables(blocks, size):
    total = blocks * size
    table = wall_table(total)
    lower, upper = wall_bands(total)
    down = np.zeros(total)
    for i in range(total - 1, 0, -1):
        down[i - 1] = -lower[i] / (1.0 + upper[i] * down[i])
    up = np.zeros(total)
    for i in range(total - 1):
        up[i + 1] = -upper[i] / (1.0 + lower[i] * up[i])
    carry_l, carry_r, corner_l, corner_r = [], [], [], []
    moment_l, moment_r = np.zeros((blocks, size)), np.zeros((blocks, size))
    for b in range(blocks):
        head, tail = b * size, b * size + size - 1
        carry_l.append(np.concatenate([[1.0], np.cumprod(down[head:tail])]))
        carry_r.append(np.concatenate([[1.0], np.cumprod(up[head + 1 : tail + 1][::-1])])[::-1])
        corner_l.append(table[head, head - 1] - table[head + 1, head - 1] / down[head] if b else 0.0)
        corner_r.append(table[tail, tail + 1] - table[tail - 1, tail + 1] / up[tail] if b < blocks - 1 else 0.0)
        if b < blocks - 1:
            to = tail + 1
            moment_l[b] = table[to, head:to]
            moment_l[b, size - 1] = table[to + 1, tail] / down[to]
        if b:
            to = head - 1
            moment_r[b] = table[to, head : tail + 1]
            moment_r[b, 0] = table[to - 1, head] / up[to]
    apply = np.zeros((blocks, 8 * size + 32, 8 * size))
    carry = np.zeros((blocks, 8 * size, 8 * len(KINDS_Y)))
    eye = np.eye(8)
    for b in range(blocks):
        rows = slice(b * size, (b + 1) * size)
        apply[b, : 8 * size] = np.kron(eye, table[rows, rows])
        first, last = np.eye(size)[0], np.eye(size)[size - 1]
        for kind, weights in enumerate((last, moment_l[b], moment_r[b], first)):
            apply[b, 8 * size + 8 * kind : 8 * size + 8 * kind + 8] = np.kron(eye, weights[None])
        for place, (offset, kind) in enumerate(KINDS_Y):
            column = np.zeros(size)
            if b - offset >= 0:
                if kind == "ml":
                    scale = 1.0
                    for c in range(b - offset + 1, b):
                        scale *= np.prod(down[c * size : (c + 1) * size])
                    column = scale * carry_l[b]
                elif kind == "last" and offset == 1:
                    column[0] = corner_l[b]
            else:
                distance = blocks - offset
                if kind == "mr":
                    scale = 1.0
                    for c in range(b + 1, b + distance):
                        scale *= np.prod(up[c * size : (c + 1) * size])
                    column = scale * carry_r[b]
                elif kind == "first" and distance == 1:
                    column[size - 1] = corner_r[b]
            carry[b, :, 8 * place : 8 * place + 8] = np.kron(eye, column[:, None])
    return apply.astype(np.float32), np.concatenate([carry] * 3, axis=2).astype(np.float32)


def table_split(table):
    high = table.astype(bfloat16)
    return high, (table - high.astype(np.float64)).astype(bfloat16)


@functools.cache
def span_tables(blocks, size):
    ratio, amplitude, corner = compact_kernel()
    places = np.arange(size)
    images = 1.0 / (1.0 - ratio ** (blocks * size))
    moments = np.zeros((4, size))
    moments[0, size - 1] = 1.0
    moments[1] = ratio ** (size - places)
    moments[2] = ratio ** (places + 1.0)
    moments[3, 0] = 1.0
    carries = np.zeros((blocks, 4, size))
    for slot in range(blocks):
        behind = slot if slot else blocks
        ahead = blocks - slot
        carries[slot, 1] = amplitude * images * ratio ** (size * (behind - 1.0)) * ratio**places
        carries[slot, 2] = -amplitude * images * ratio ** (size * (ahead - 1.0)) * ratio ** (size - 1.0 - places)
        if behind == 1:
            carries[slot, 0, 0] = corner
        if ahead == 1:
            carries[slot, 3, size - 1] = -corner
    both_moments = np.zeros((8, 2 * size))
    both_moments[:4, :size] = moments
    both_moments[4:, size:] = moments
    both_carries = np.zeros((blocks, 8, 2 * size))
    both_carries[:, :4, :size] = carries
    both_carries[:, 4:, size:] = carries
    local_high, local_low = table_split(local_compact(size).T)
    carry_high, carry_low = table_split(both_carries.reshape(8 * blocks, 2 * size))
    return (
        np.block([[local_high, local_low], [local_high, np.zeros_like(local_low)]]),
        np.concatenate(table_split(both_moments)),
        np.concatenate([carry_high, carry_high, carry_low]),
    )


def stream_weights(size):
    ratio, _, _ = compact_kernel()
    filter_ratio, _ = decay(filter_alpha)
    places = np.arange(size)
    return np.stack(
        [
            filter_ratio ** (size - places),
            filter_ratio ** (places + 1.0),
            ratio ** (size - places),
            ratio ** (places + 1.0),
        ]
    )


def filtered_derivative():
    ratio, amplitude, corner = compact_kernel()
    filter_ratio, _ = decay(filter_alpha)
    over, times = ratio / filter_ratio, ratio * filter_ratio
    gain = amplitude * (over / (1.0 - over) - times / (1.0 - times)) + corner * (1.0 / filter_ratio - filter_ratio)
    return gain, amplitude / (1.0 - over), amplitude * filter_ratio / (1.0 - times), corner, corner * filter_ratio


def split(values):
    high = values.astype(bfloat16)
    return high, (values - high.astype(jnp.float32)).astype(bfloat16)


def product(left, right, sides=((1,), (0,))):
    return lax.dot_general(left, right, (sides, ((), ())), preferred_element_type=jnp.float32)


def exchange_kernel(
    nx,
    ny,
    nz,
    den_hbm,
    mom_hbm,
    ene_hbm,
    metric_hbm,
    wtab_hbm,
    ky_hbm,
    py_hbm,
    kz_hbm,
    qz_hbm,
    pz_hbm,
    tend,
    carry_x,
    carry_f,
    carry_d,
    carry_n,
    den,
    mom,
    ene,
    metric,
    wtab,
    ky,
    py,
    kz,
    qz,
    pz,
    ky_high,
    ky_low,
    py_both,
    fx,
    fy,
    fz,
    uv0,
    moments_x,
    sy,
    sz,
    dys,
    dzs,
    ys_out,
    ys_in,
    zs_in,
    yb_out,
    yb_in,
    zm_in,
    xn_out,
    xn_in,
    pair_in,
    xm_out,
    xm_in,
    uv_out,
    uv_in,
    xo_out,
    xo_in,
    xp_in,
    io_out,
    io_in,
    state_sem,
    load_sem,
    send_sem,
    recv_sem,
):
    fields, size_x, size_y, size_z = fx.shape
    me_x, me_y, me_z = lax.axis_index("gx"), lax.axis_index("gy"), lax.axis_index("gz")
    rows = size_y // nx
    ratio, amplitude, corner = compact_kernel()
    filter_ratio, _ = decay(filter_alpha)
    gain_d, _, far_d, corner_d, first_d = filtered_derivative()
    half_rows = fields * rows
    chips = nx // 2
    chip, core = me_x // 2, lax.rem(me_x, 2)
    pair = 1 - 2 * core
    half_y = size_y // 2

    def farthest(count):
        return sorted(range(1, count), key=lambda k: -min(k, count - k))

    def along(axis, offset):
        me, count = {"gx": (me_x, nx), "gy": (me_y, ny), "gz": (me_z, nz)}[axis]
        return lax.rem(me + offset + count, count)

    class Group:
        def __init__(self, copies, sent, received):
            self.copies, self.sent, self.received = copies, sent, received

        def start(self):
            for copy in self.copies:
                copy.start()

        def wait(self):
            for region, sem in (self.sent, self.received):
                pltpu.make_async_copy(region, region, sem).wait()

    def state_loads(chunk):
        ys = pl.ds(pl.multiple_of(chunk * 8, 8), 8)
        return [
            pltpu.make_async_copy(den_hbm.at[:, ys], den.at[:, ys], state_sem.at[0, chunk]),
            pltpu.make_async_copy(mom_hbm.at[:, :, ys], mom.at[:, :, ys], state_sem.at[1, chunk]),
            pltpu.make_async_copy(ene_hbm.at[:, ys], ene.at[:, ys], state_sem.at[2, chunk]),
        ]

    sources = (wtab_hbm, ky_hbm.at[me_y], py_hbm.at[me_y], metric_hbm, kz_hbm, qz_hbm, pz_hbm)
    targets = (wtab, ky, py, metric, kz, qz, pz)
    loads = [
        pltpu.make_async_copy(source, target, load_sem.at[place])
        for place, (source, target) in enumerate(zip(sources, targets))
    ]
    loads[0].start()
    for chunk in range(size_y // 8):
        for load in state_loads(chunk):
            load.start()
    for load in loads[1:]:
        load.start()

    yb_in[...] = jnp.zeros(yb_in.shape, jnp.float32)

    barrier = pltpu.get_barrier_semaphore()
    for axis, count in (("gx", nx), ("gy", ny), ("gz", nz)):
        for offset in range(1, count):
            pl.semaphore_signal(barrier, inc=1, device_id={axis: along(axis, offset)}, device_id_type=MESH)

    next_sem = [0]

    def remote(src, dst, axis, offset):
        place = next_sem[0]
        next_sem[0] = place + 1
        return pltpu.make_async_remote_copy(
            src_ref=src,
            dst_ref=dst,
            send_sem=send_sem.at[place],
            recv_sem=recv_sem.at[place],
            device_id={axis: along(axis, offset)},
            device_id_type=MESH,
        )

    def remote_group(blocks, step, source, target):
        place = next_sem[0]
        next_sem[0] = place + 1
        sems = send_sem.at[place], recv_sem.at[place]
        copies = [
            pltpu.make_async_remote_copy(
                src_ref=source(k),
                dst_ref=target(k),
                send_sem=sems[0],
                recv_sem=sems[1],
                device_id={"gx": along("gx", step * k)},
                device_id_type=MESH,
            )
            for k in farthest(blocks)
        ]
        return lambda out, arrived: Group(
            copies, (out.at[pl.ds(0, blocks - 1)], sems[0]), (arrived.at[pl.ds(0, blocks - 1)], sems[1])
        )

    loads[0].wait()

    unroll = 4
    zero = jnp.zeros((8, size_z), jnp.float32)

    def flux_chunk(chunk, _):
        ys = pl.ds(pl.multiple_of(chunk * 8, 8), 8)
        for load in state_loads(chunk):
            load.wait()

        def cells(step, acc):
            acc = list(acc)
            for inner in range(unroll):
                x = step * unroll + inner
                w = [wtab[k, x] for k in range(4)]
                rho, energy = den[x, ys, :], ene[x, ys, :]
                m = [mom[j, x, ys, :] for j in range(3)]
                inverse = 1.0 / rho
                v = [m[j] * inverse for j in range(3)]
                own = [m[j] * v[j] for j in range(3)]
                pressure = (heat_ratio - 1.0) * (energy - 0.5 * (own[0] + own[1] + own[2]))
                m12, m13, m23 = m[0] * v[1], m[0] * v[2], m[1] * v[2]
                total = energy + pressure
                flux_x = (m[0], own[0] + pressure, m12, m13, total * v[0])
                flux_y = (m[1], m12, own[1] + pressure, m23, total * v[1])
                flux_z = (m[2], m13, m23, own[2] + pressure, total * v[2])
                state = (rho, m[0], m[1], m[2], energy)
                for f in range(fields):
                    fx[f, x, ys, :] = flux_x[f]
                    fy[f, x, ys, :] = flux_y[f]
                    fz[f, x, ys, :] = flux_z[f]
                    change = (time_step * gain_d) * flux_x[f]
                    acc[f] = acc[f] + w[0] * (state[f] - change)
                    acc[5 + f] = acc[5 + f] + w[1] * (state[f] + change)
                    acc[10 + f] = acc[10 + f] + w[2] * flux_x[f]
                    acc[15 + f] = acc[15 + f] + w[3] * flux_x[f]
            return tuple(acc)

        acc = lax.fori_loop(0, size_x // unroll, cells, (zero,) * 20)
        for f in range(fields):
            uv0[0, f, ys, :] = acc[f]
            uv0[1, f, ys, :] = acc[5 + f]
            moments_x[0, f, ys, :] = acc[10 + f]
            moments_x[1, f, ys, :] = acc[15 + f]
            xn_out[0, f, ys, :] = fx[f, size_x - 1, ys, :]
            xn_out[1, f, ys, :] = fx[f, 0, ys, :]
        return 0

    sy[10:16] = jnp.zeros((6, size_y, size_z), jnp.float32)
    sz[:, 5:8] = jnp.zeros((2, 3, size_y, size_z), jnp.float32)
    lax.fori_loop(0, size_y // 8, flux_chunk, 0)

    def deal(message, side, f, values):
        for owner in range(values.shape[0] // rows):
            place = side * half_rows + rows * f
            message[owner, place : place + rows, :] = values[rows * owner : rows * owner + rows]

    pl.semaphore_wait(barrier, nx + ny + nz - 3)
    to_pair = remote(moments_x, pair_in, "gx", pair)
    to_pair.start()

    def sums_chunk(chunk, _):
        ys = pl.ds(pl.multiple_of(chunk * 8, 8), 8)

        def sums(step, acc):
            acc = list(acc)
            for inner in range(unroll):
                x = step * unroll + inner
                w = [wtab[k, x] for k in range(2)]
                for f in range(fields):
                    value_y, value_z = fy[f, x, ys, :], fz[f, x, ys, :]
                    acc[f] = acc[f] + w[0] * value_y
                    acc[5 + f] = acc[5 + f] + w[1] * value_y
                    acc[10 + f] = acc[10 + f] + w[0] * value_z
                    acc[15 + f] = acc[15 + f] + w[1] * value_z
            return tuple(acc)

        acc = lax.fori_loop(0, size_x // unroll, sums, (zero,) * 20)
        for f in range(fields):
            sy[f, ys, :] = acc[f]
            sy[5 + f, ys, :] = acc[5 + f]
            sz[0, f, ys, :] = acc[10 + f]
            sz[1, f, ys, :] = acc[15 + f]
        return 0

    lax.fori_loop(0, size_y // 8, sums_chunk, 0)

    for load in loads[1:]:
        load.wait()
    shape = (8 * size_y, ny * size_y)
    row_place = lax.broadcasted_iota(jnp.int32, shape, 0)
    col_place = lax.broadcasted_iota(jnp.int32, shape, 1)
    mine = col_place == me_y * size_y + lax.rem(row_place, size_y)
    metric_rows = jnp.sum(jnp.where(mine, metric[...], 0.0), axis=1, keepdims=True)
    ky[: 8 * size_y, :] = ky[: 8 * size_y, :] * metric_rows
    ky_high[...], ky_low[...] = split(ky[...])
    high, low = split(py[...] * metric_rows)
    py_both[...] = jnp.where(lax.broadcasted_iota(jnp.int32, py.shape, 1) < 128, high, low)

    def apply_wall(first, second):
        cells = jnp.concatenate(
            [first.reshape(8 * size_y, size_z), second.reshape(8 * size_y, size_z)], axis=1
        )
        high, low = split(cells)
        result = product(ky_high[...], high) + product(ky_high[...], low) + product(ky_low[...], high)
        return [
            (
                result[: 8 * size_y, lanes].reshape(8, size_y, size_z),
                result[8 * size_y :, lanes].reshape(4, 8, size_z),
            )
            for lanes in (slice(0, size_z), slice(size_z, 2 * size_z))
        ]

    def wall_carries(first, second):
        cells = jnp.concatenate([first.reshape(64, size_z), second.reshape(64, size_z)], axis=1)
        high, low = split(cells)
        return product(py_both[...], jnp.concatenate([high, low, high], axis=0))

    def span_local(cells):
        result = product(jnp.concatenate(split(cells), axis=1), kz[...])
        return result[:, :size_z] + result[:, size_z:]

    def span_moments(first, second):
        high, low = split(jnp.concatenate([first, second], axis=1))
        from_high = product(qz[...], high, ((1,), (1,)))
        from_low = product(qz[...], low, ((1,), (1,)))
        return from_high[:8] + from_high[8:] + (from_low[:8] + from_low[8:])

    def span_carries(received):
        high, low = split(received)
        return product(jnp.concatenate([high, low, high], axis=0), pz[...], ((0,), (0,)))

    for group, (local, moments) in enumerate(apply_wall(sy[0:8], sy[8:16])):
        dys[8 * group : 8 * group + 8] = local
        ys_out[:, 8 * group : 8 * group + 8, :] = moments
    ys = [
        remote(ys_out.at[pl.ds(0, 3)], ys_in.at[pl.ds(0, 3)], "gy", 1),
        remote(ys_out.at[pl.ds(1, 2)], ys_in.at[pl.ds(3, 2)], "gy", 2),
        remote(ys_out.at[pl.ds(1, 3)], ys_in.at[pl.ds(5, 3)], "gy", 3),
    ]
    for copy in ys:
        copy.start()
    zs_in[0] = span_moments(sz[0].reshape(8 * size_y, size_z), sz[1].reshape(8 * size_y, size_z))
    zs = [remote(zs_in.at[0], zs_in.at[k], "gz", k) for k in range(1, nz)]
    for copy in zs:
        copy.start()
    dzs[...] = span_local(sz[...].reshape(16 * size_y, size_z)).reshape(2, 8, size_y, size_z)

    to_pair.wait()
    power = float(ratio**size_x)
    second = core == 1
    mine = pl.ds(pl.multiple_of(half_y * core, 8), half_y)
    for side in range(2):
        is_near = second if side == 0 else jnp.logical_not(second)
        own_gain, pair_gain = jnp.where(is_near, 1.0, power), jnp.where(is_near, power, 1.0)
        for f in range(fields):
            deal(xm_out, side, f, own_gain * moments_x[side, f, mine, :] + pair_gain * pair_in[side, f, mine, :])
        carry_n[side] = jnp.where(is_near, 1.0, 0.0) * pair_in[side]
    xm = remote_group(chips, 2, lambda k: xm_out.at[lax.rem(chip + k, chips)], lambda k: xm_in.at[k])(xm_out, xm_in)
    xm.start()
    xm_in[0] = xm_out[chip]

    def wall_field(f, _):
        for part in range(size_x // 16):
            pair = [pl.ds(16 * part + 8 * side, 8) for side in range(2)]
            for xs, (local, moments) in zip(pair, apply_wall(fy[f, pair[0]], fy[f, pair[1]])):
                tend[f, xs] = local
                yb_out[:, f, xs, :] = moments
        return 0

    lax.fori_loop(0, fields, wall_field, 0)
    yb = []
    for distance in range(1, ny):
        count = 2 if distance == 1 else 1
        up_place = KINDS_Y.index((distance, "last" if distance == 1 else "ml"))
        down_place = KINDS_Y.index((ny - distance, "mr"))
        up = remote(yb_out.at[pl.ds(2 - count, count)], yb_in.at[pl.ds(up_place, count)], "gy", distance)
        down = remote(yb_out.at[pl.ds(2, count)], yb_in.at[pl.ds(down_place, count)], "gy", -distance)
        has_above, has_below = me_y < ny - distance, me_y >= distance
        yb += [(up, has_above, has_below), (down, has_below, has_above)]
    for copy, sends, _ in yb:
        pl.when(sends)(copy.start)

    for copy in ys + zs:
        copy.wait()
    span = span_carries(zs_in[...].reshape(8 * nz, 8 * size_y))
    wall = wall_carries(ys_in[:, 0:8, :], ys_in[:, 8:16, :])
    for side in range(2):
        for f in range(fields):
            unit = 5 * side + f
            place, lane = (unit % 8) * size_y, (unit // 8) * size_z
            change = dys[unit] + wall[place : place + size_y, lane : lane + size_z]
            change = change + dzs[side, f] + span[f * size_y : (f + 1) * size_y, side * size_z : (side + 1) * size_z]
            deal(uv_out, side, f, uv0[side, f] - time_step * change)
    uv = remote_group(nx, 1, lambda k: uv_out.at[along("gx", k)], lambda k: uv_in.at[k])(uv_out, uv_in)
    uv.start()
    uv_in[0] = uv_out[me_x]

    xn = [
        remote(xn_out.at[0], xn_in.at[0], "gx", 1),
        remote(xn_out.at[1], xn_in.at[1], "gx", -1),
    ]
    for copy in xn:
        copy.start()

    half = size_x // 2

    def span_field(f, _):
        pair = [fz[f, pl.ds(part * half, half)].reshape(half * size_y, size_z) for part in range(2)]
        zm_in[0, f] = span_moments(*pair)
        return 0

    lax.fori_loop(0, fields, span_field, 0)
    zm = [remote(zm_in.at[0], zm_in.at[k], "gz", k) for k in range(1, nz)]
    for copy in zm:
        copy.start()

    def span_cells(f, _):
        for part in range(size_x // 8):
            xs = pl.ds(8 * part, 8)
            tend[f, xs] += span_local(fz[f, xs].reshape(8 * size_y, size_z)).reshape(8, size_y, size_z)
        return 0

    lax.fori_loop(0, fields, span_cells, 0)

    def sweep(behind, power, values):
        step, count = 1 if behind else -1, len(values)
        total = values[0] if behind else values[count - 1]
        for k in range(1, count):
            total = total + float(power**k) * (values[k] if behind else values[count - 1 - k])
        total = total * float(1.0 / (1.0 - power**count))
        place = count - 1 if behind else 0
        result = [None] * count
        result[place] = total
        for _ in range(count - 1):
            total = values[place] + float(power) * total
            place = place - step
            result[place] = total
        return result

    from_behind = lax.broadcasted_iota(jnp.int32, (2 * half_rows, size_z), 0) < half_rows

    def solve_lines(received, power, answers):
        values = [received[k] for k in range(received.shape[0])]
        behind, ahead = sweep(True, power, values), sweep(False, power, values)
        for k in range(len(values)):
            answers[k] = jnp.where(from_behind, behind[k], ahead[k])

    xm.wait()
    solve_lines(xm_in, ratio ** (2 * size_x), xo_out)
    xo = remote_group(chips, -2, lambda k: xo_out.at[k], lambda k: xo_in.at[chip])(xo_out, xo_in)
    xo.start()
    xo_in[chip] = xo_out[0]

    uv.wait()
    solve_lines(uv_in, filter_ratio**size_x, io_out)
    io = remote_group(nx, -1, lambda k: io_out.at[k], lambda k: io_in.at[me_x])(io_out, io_in)
    io.start()
    io_in[me_x] = io_out[0]

    for copy in xn:
        copy.wait()
    tend[:, 0] += corner * xn_in[0]
    tend[:, size_x - 1] -= corner * xn_in[1]

    for side in range(2):
        sign = -time_step if side else time_step
        carry_d[side] = sign * (corner_d * xn_in[side] + far_d * moments_x[1 - side] + first_d * xn_out[1 - side])

    def scan_chunk(chunk, _):
        ys = pl.ds(pl.multiple_of(chunk * 8, 8), 8)

        def scan(side, step, carried):
            carried = list(carried)
            for inner in range(unroll):
                x = step * unroll + inner
                x = size_x - 1 - x if side else x
                gains = (-amplitude, -corner) if side else (amplitude, corner)
                for f in range(fields):
                    total, last = carried[f], carried[5 + f]
                    tend[f, x, ys, :] += gains[0] * total + gains[1] * last
                    here = fx[f, x, ys, :]
                    carried[f], carried[5 + f] = ratio * (total + here), here
            return tuple(carried)

        for side in range(2):
            lax.fori_loop(0, size_x // unroll, functools.partial(scan, side), (zero,) * 10)
        return 0

    lax.fori_loop(0, size_y // 8, scan_chunk, 0)

    xo.wait()
    halves = remote(xo_in, xp_in, "gx", pair)
    halves.start()

    for copy in zm:
        copy.wait()
    for copy, sends, receives in yb:
        pl.when(sends)(copy.wait_send)
        pl.when(receives)(copy.wait_recv)

    def carries(f, _):
        both = span_carries(zm_in[:, f].reshape(8 * nz, half * size_y))
        for part in range(size_x // 16):
            pair = [pl.ds(16 * part + 8 * side, 8) for side in range(2)]
            wall = wall_carries(yb_in[:, f, pair[0], :], yb_in[:, f, pair[1], :])
            for side, xs in enumerate(pair):
                row = (16 * part + 8 * side) % half * size_y
                lane = (16 * part + 8 * side) // half * size_z
                change = wall[:, side * size_z : (side + 1) * size_z]
                change = change + both[row : row + 8 * size_y, lane : lane + size_z]
                tend[f, xs] += change.reshape(8, size_y, size_z)
        return 0

    lax.fori_loop(0, fields, carries, 0)

    halves.wait()
    gains = jnp.where(from_behind, jnp.where(second, power, 1.0), jnp.where(second, 1.0, power))
    carry_x[pl.ds(chips * core, chips)] = xo_in[...] * gains
    carry_x[pl.ds(chips * (1 - core), chips)] = xp_in[...] * gains
    io.wait()
    carry_f[...] = io_in[...]


def filter_kernel(den, mom, ene, part, carry_x, carry_f, carry_d, carry_n, tend_hbm, after_hbm, tend, after, sems):
    chunks, fields, size_x = tend.shape[:3]
    half_rows = carry_x.shape[1] // 2
    rows = half_rows // fields
    owners = 8 // rows
    ratio, far_gain, _ = compact_kernel()
    filter_ratio, gain = decay(filter_alpha)
    straight = 0.5 * (0.5 + filter_alpha) / filter_alpha
    amplitude = (0.5 + filter_alpha - straight) * gain
    _, near_d, far_d, _, _ = filtered_derivative()
    power = ratio**size_x
    unroll = 4

    def copies(chunk):
        ys = pl.ds(pl.multiple_of(chunk * 8, 8), 8)
        return (
            pltpu.make_async_copy(tend.at[chunk], tend_hbm.at[:, :, ys], sems.at[0, chunk]),
            pltpu.make_async_copy(after.at[chunk], after_hbm.at[:, :, ys], sems.at[1, chunk]),
        )

    def chunk_body(chunk, _):
        ys = pl.ds(pl.multiple_of(chunk * 8, 8), 8)

        def carried_in(ref, side, f):
            place = side * half_rows + rows * f
            return jnp.concatenate(
                [ref[chunk * owners + o, place : place + rows, :] for o in range(owners)], axis=0
            )

        def state(f, x):
            return den[x, ys, :] if f == 0 else ene[x, ys, :] if f == 4 else mom[f - 1, x, ys, :]

        from_l = [carried_in(carry_x, 0, f) + carry_n[0, f, ys, :] for f in range(fields)]
        from_r = [carried_in(carry_x, 1, f) + carry_n[1, f, ys, :] for f in range(fields)]
        start_l = [
            carried_in(carry_f, 0, f)
            + carry_d[0, f, ys, :]
            + time_step * (near_d * from_l[f] + float(far_d * power) * from_r[f])
            for f in range(fields)
        ]
        start_r = [
            carried_in(carry_f, 1, f)
            + carry_d[1, f, ys, :]
            - time_step * (near_d * from_r[f] + float(far_d * power) * from_l[f])
            for f in range(fields)
        ]
        head = [float(far_gain * ratio ** (size_x - 1)) * from_l[f] for f in range(fields)]
        tail = [far_gain * from_r[f] for f in range(fields)]

        def back(step, carried):
            carried = list(carried)
            for inner in range(unroll):
                x = size_x - 1 - (step * unroll + inner)
                for f in range(fields):
                    behind, ahead = carried[5 + f], carried[10 + f]
                    rate = ahead - behind - part[f, x, ys, :]
                    tend[chunk, f, x] = rate
                    after[chunk, f, x] = amplitude * carried[f]
                    carried[f] = filter_ratio * (carried[f] + (state(f, x) + time_step * rate))
                    carried[5 + f], carried[10 + f] = (1.0 / ratio) * behind, ratio * ahead
            return tuple(carried)

        def ahead(step, carried):
            carried = list(carried)
            for inner in range(unroll):
                x = step * unroll + inner
                for f in range(fields):
                    middle = state(f, x) + time_step * tend[chunk, f, x]
                    after[chunk, f, x] += (straight + amplitude) * middle + amplitude * carried[f]
                    carried[f] = filter_ratio * (carried[f] + middle)
            return tuple(carried)

        lax.fori_loop(0, size_x // unroll, back, tuple(start_r + head + tail))
        rate_copy, after_copy = copies(chunk)
        rate_copy.start()
        lax.fori_loop(0, size_x // unroll, ahead, tuple(start_l))
        after_copy.start()
        return 0

    lax.fori_loop(0, chunks, chunk_body, 0)
    for chunk in range(chunks):
        for copy in copies(chunk):
            copy.wait()


def solution(mesh):
    nx, ny, nz = mesh.shape["gx"], mesh.shape["gy"], mesh.shape["gz"]

    def on_device(density, momentum, energy, metric):
        size_x, size_y, size_z = density.shape
        fields = 5
        rows = size_y // nx
        float32 = jnp.float32
        ky, py = wall_tables(ny, size_y)
        kz, qz, pz = span_tables(nz, size_z)
        wtab = stream_weights(size_x).astype(np.float32)
        cells = (fields, size_x, size_y, size_z)
        owned = (nx, 2 * fields * rows, size_z)
        chipwise = (nx // 2, 2 * fields * rows, size_z)
        sides = (2, fields, size_y, size_z)
        vmem = pl.BlockSpec(memory_space=pltpu.VMEM)
        stays = pl.BlockSpec(memory_space=pltpu.HBM)
        copies = 11 + 2 * (ny - 1) + 2 * (nz - 1)
        chunks = size_y // 8
        part, carry_x, carry_f, carry_d, carry_n = pl.pallas_call(
            functools.partial(exchange_kernel, nx, ny, nz),
            out_shape=[
                jax.ShapeDtypeStruct(cells, float32),
                jax.ShapeDtypeStruct(owned, float32),
                jax.ShapeDtypeStruct(owned, float32),
                jax.ShapeDtypeStruct(sides, float32),
                jax.ShapeDtypeStruct(sides, float32),
            ],
            in_specs=[stays] * 10,
            out_specs=[vmem] * 5,
            scratch_shapes=[
                pltpu.VMEM(cells[1:], float32),
                pltpu.VMEM((3,) + cells[1:], float32),
                pltpu.VMEM(cells[1:], float32),
                pltpu.VMEM((1, ny * size_y), float32),
                pltpu.SMEM(wtab.shape, float32),
                pltpu.VMEM(ky.shape[1:], float32),
                pltpu.VMEM(py.shape[1:], float32),
                pltpu.VMEM(kz.shape, bfloat16),
                pltpu.VMEM(qz.shape, bfloat16),
                pltpu.VMEM(pz.shape, bfloat16),
                pltpu.VMEM(ky.shape[1:], bfloat16),
                pltpu.VMEM(ky.shape[1:], bfloat16),
                pltpu.VMEM(py.shape[1:], bfloat16),
                pltpu.VMEM(cells, float32),
                pltpu.VMEM(cells, float32),
                pltpu.VMEM(cells, float32),
                pltpu.VMEM(sides, float32),
                pltpu.VMEM(sides, float32),
                pltpu.VMEM((16, size_y, size_z), float32),
                pltpu.VMEM((2, 8, size_y, size_z), float32),
                pltpu.VMEM((16, size_y, size_z), float32),
                pltpu.VMEM((2, 8, size_y, size_z), float32),
                pltpu.VMEM((4, 16, size_z), float32),
                pltpu.VMEM((8, 16, size_z), float32),
                pltpu.VMEM((nz, 8, 8 * size_y), float32),
                pltpu.VMEM((4, fields, size_x, size_z), float32),
                pltpu.VMEM((8, fields, size_x, size_z), float32),
                pltpu.VMEM((nz, fields, 8, size_x // 2 * size_y), float32),
                pltpu.VMEM(sides, float32),
                pltpu.VMEM(sides, float32),
                pltpu.VMEM(sides, float32),
                pltpu.VMEM(chipwise, float32),
                pltpu.VMEM(chipwise, float32),
                pltpu.VMEM(owned, float32),
                pltpu.VMEM(owned, float32),
                pltpu.VMEM(chipwise, float32),
                pltpu.VMEM(chipwise, float32),
                pltpu.VMEM(chipwise, float32),
                pltpu.VMEM(owned, float32),
                pltpu.VMEM(owned, float32),
                pltpu.SemaphoreType.DMA((3, chunks)),
                pltpu.SemaphoreType.DMA((7,)),
                pltpu.SemaphoreType.DMA((copies,)),
                pltpu.SemaphoreType.DMA((copies,)),
            ],
            compiler_params=pltpu.CompilerParams(
                collective_id=0, has_side_effects=True, vmem_limit_bytes=24 * 1024 * 1024
            ),
            cost_estimate=pl.CostEstimate(flops=4 * 10**9, bytes_accessed=10**7, transcendentals=0),
        )(
            *[
                pltpu.with_memory_space_constraint(jnp.asarray(value), pltpu.HBM)
                for value in (density, momentum, energy, metric.reshape(1, -1), wtab, ky, py, kz, qz, pz)
            ]
        )
        return pl.pallas_call(
            filter_kernel,
            out_shape=[jax.ShapeDtypeStruct(cells, float32), jax.ShapeDtypeStruct(cells, float32)],
            in_specs=[vmem] * 8,
            out_specs=[stays] * 2,
            scratch_shapes=[
                pltpu.VMEM((chunks, fields, size_x, 8, size_z), float32),
                pltpu.VMEM((chunks, fields, size_x, 8, size_z), float32),
                pltpu.SemaphoreType.DMA((2, chunks)),
            ],
            compiler_params=pltpu.CompilerParams(vmem_limit_bytes=16 * 1024 * 1024),
            cost_estimate=pl.CostEstimate(flops=10**7, bytes_accessed=10**7, transcendentals=0),
        )(density, momentum, energy, part, carry_x, carry_f, carry_d, carry_n)

    return jax.shard_map(
        on_device,
        mesh=mesh,
        in_specs=(P("gx", "gy", "gz"), P(None, "gx", "gy", "gz"), P("gx", "gy", "gz"), P()),
        out_specs=(P(None, "gx", "gy", "gz"), P(None, "gx", "gy", "gz")),
        check_vma=False,
    )
```

```python
import functools

import jax
import jax.numpy as jnp
import numpy as np
from jax import lax
from jax.experimental import pallas as pl
from jax.experimental.pallas import tpu as pltpu
from jax.sharding import PartitionSpec as P

heat_ratio = 1.4
compact_alpha = 1.0 / 3.0
filter_alpha = 0.499
time_step = 0.05
near_weight = 7.0 / 9.0
wide_weight = 1.0 / 36.0
bfloat16 = jnp.bfloat16
MESH = pl.DeviceIdType.MESH
KINDS_Y = ((1, "last"), (1, "ml"), (1, "mr"), (2, "ml"), (2, "mr"), (3, "ml"), (3, "mr"), (3, "first"))


def decay(alpha):
    root = np.sqrt(1.0 - 4.0 * alpha * alpha)
    return (-1.0 + root) / (2.0 * alpha), 1.0 / root


def compact_kernel():
    ratio, gain = decay(compact_alpha)

    def green(n):
        return gain * ratio ** abs(n)

    def kernel(d):
        return near_weight * (green(d + 1) - green(d - 1)) + wide_weight * (green(d + 2) - green(d - 2))

    amplitude = kernel(2) / ratio**2
    return ratio, amplitude, kernel(1) - amplitude * ratio


def local_compact(size):
    ratio, amplitude, corner = compact_kernel()
    table = np.zeros((size, size))
    for i in range(size):
        for j in range(size):
            d = abs(i - j)
            if d:
                value = amplitude * ratio**d + (corner if d == 1 else 0.0)
                table[i, j] = value if i > j else -value
    return table


def table_thomas(lower_band, main_band, upper_band, source):
    count = source.shape[0]
    c_all = np.zeros(count)
    d_all = np.zeros(source.shape)
    c_prev = 0.0
    d_prev = np.zeros(source.shape[1:])
    for place in range(count):
        denom = main_band[place] - lower_band[place] * c_prev
        c_prev = upper_band[place] / denom
        d_prev = (source[place] - lower_band[place] * d_prev) / denom
        c_all[place] = c_prev
        d_all[place] = d_prev
    solved = np.zeros(source.shape)
    x_next = np.zeros(source.shape[1:])
    for place in range(count - 1, -1, -1):
        x_next = d_all[place] - c_all[place] * x_next
        solved[place] = x_next
    return solved


def wall_bands(total):
    lower = np.full(total, compact_alpha)
    upper = np.full(total, compact_alpha)
    lower[0], lower[1], lower[total - 2], lower[total - 1] = 0.0, 0.25, 0.25, 2.0
    upper[0], upper[1], upper[total - 2], upper[total - 1] = 2.0, 0.25, 0.25, 0.0
    return lower, upper


def wall_table(total):
    lower, upper = wall_bands(total)
    stencil = np.zeros((total, total))
    for i in range(2, total - 2):
        stencil[i, i + 1], stencil[i, i - 1] = near_weight, -near_weight
        stencil[i, i + 2], stencil[i, i - 2] = wide_weight, -wide_weight
    for i in (1, total - 2):
        stencil[i, i + 1], stencil[i, i - 1] = 0.75, -0.75
    stencil[0, :3] = (-2.5, 2.0, 0.5)
    stencil[total - 1, total - 3 :] = (-0.5, -2.0, 2.5)
    return table_thomas(lower, np.ones(total), upper, stencil)


@functools.cache
def wall_tables(blocks, size):
    total = blocks * size
    table = wall_table(total)
    lower, upper = wall_bands(total)
    down = np.zeros(total)
    for i in range(total - 1, 0, -1):
        down[i - 1] = -lower[i] / (1.0 + upper[i] * down[i])
    up = np.zeros(total)
    for i in range(total - 1):
        up[i + 1] = -upper[i] / (1.0 + lower[i] * up[i])
    carry_l, carry_r, corner_l, corner_r = [], [], [], []
    moment_l, moment_r = np.zeros((blocks, size)), np.zeros((blocks, size))
    for b in range(blocks):
        head, tail = b * size, b * size + size - 1
        carry_l.append(np.concatenate([[1.0], np.cumprod(down[head:tail])]))
        carry_r.append(np.concatenate([[1.0], np.cumprod(up[head + 1 : tail + 1][::-1])])[::-1])
        corner_l.append(table[head, head - 1] - table[head + 1, head - 1] / down[head] if b else 0.0)
        corner_r.append(table[tail, tail + 1] - table[tail - 1, tail + 1] / up[tail] if b < blocks - 1 else 0.0)
        if b < blocks - 1:
            to = tail + 1
            moment_l[b] = table[to, head:to]
            moment_l[b, size - 1] = table[to + 1, tail] / down[to]
        if b:
            to = head - 1
            moment_r[b] = table[to, head : tail + 1]
            moment_r[b, 0] = table[to - 1, head] / up[to]
    apply = np.zeros((blocks, 8 * size + 32, 8 * size))
    carry = np.zeros((blocks, 8 * size, 8 * len(KINDS_Y)))
    eye = np.eye(8)
    for b in range(blocks):
        rows = slice(b * size, (b + 1) * size)
        apply[b, : 8 * size] = np.kron(eye, table[rows, rows])
        first, last = np.eye(size)[0], np.eye(size)[size - 1]
        for kind, weights in enumerate((last, moment_l[b], moment_r[b], first)):
            apply[b, 8 * size + 8 * kind : 8 * size + 8 * kind + 8] = np.kron(eye, weights[None])
        for place, (offset, kind) in enumerate(KINDS_Y):
            column = np.zeros(size)
            if b - offset >= 0:
                if kind == "ml":
                    scale = 1.0
                    for c in range(b - offset + 1, b):
                        scale *= np.prod(down[c * size : (c + 1) * size])
                    column = scale * carry_l[b]
                elif kind == "last" and offset == 1:
                    column[0] = corner_l[b]
            else:
                distance = blocks - offset
                if kind == "mr":
                    scale = 1.0
                    for c in range(b + 1, b + distance):
                        scale *= np.prod(up[c * size : (c + 1) * size])
                    column = scale * carry_r[b]
                elif kind == "first" and distance == 1:
                    column[size - 1] = corner_r[b]
            carry[b, :, 8 * place : 8 * place + 8] = np.kron(eye, column[:, None])
    return apply.astype(np.float32), np.concatenate([carry] * 3, axis=2).astype(np.float32)


def table_split(table):
    high = table.astype(bfloat16)
    return high, (table - high.astype(np.float64)).astype(bfloat16)


@functools.cache
def span_tables(blocks, size):
    ratio, amplitude, corner = compact_kernel()
    places = np.arange(size)
    images = 1.0 / (1.0 - ratio ** (blocks * size))
    moments = np.zeros((4, size))
    moments[0, size - 1] = 1.0
    moments[1] = ratio ** (size - places)
    moments[2] = ratio ** (places + 1.0)
    moments[3, 0] = 1.0
    carries = np.zeros((blocks, 4, size))
    for slot in range(blocks):
        behind = slot if slot else blocks
        ahead = blocks - slot
        carries[slot, 1] = amplitude * images * ratio ** (size * (behind - 1.0)) * ratio**places
        carries[slot, 2] = -amplitude * images * ratio ** (size * (ahead - 1.0)) * ratio ** (size - 1.0 - places)
        if behind == 1:
            carries[slot, 0, 0] = corner
        if ahead == 1:
            carries[slot, 3, size - 1] = -corner
    both_moments = np.zeros((8, 2 * size))
    both_moments[:4, :size] = moments
    both_moments[4:, size:] = moments
    both_carries = np.zeros((blocks, 8, 2 * size))
    both_carries[:, :4, :size] = carries
    both_carries[:, 4:, size:] = carries
    local_high, local_low = table_split(local_compact(size).T)
    carry_high, carry_low = table_split(both_carries.reshape(8 * blocks, 2 * size))
    return (
        np.block([[local_high, local_low], [local_high, np.zeros_like(local_low)]]),
        np.concatenate(table_split(both_moments)),
        np.concatenate([carry_high, carry_high, carry_low]),
    )


def stream_weights(size):
    ratio, _, _ = compact_kernel()
    filter_ratio, _ = decay(filter_alpha)
    places = np.arange(size)
    return np.stack(
        [
            filter_ratio ** (size - places),
            filter_ratio ** (places + 1.0),
            ratio ** (size - places),
            ratio ** (places + 1.0),
        ]
    )


def filtered_derivative():
    ratio, amplitude, corner = compact_kernel()
    filter_ratio, _ = decay(filter_alpha)
    over, times = ratio / filter_ratio, ratio * filter_ratio
    gain = amplitude * (over / (1.0 - over) - times / (1.0 - times)) + corner * (1.0 / filter_ratio - filter_ratio)
    return gain, amplitude / (1.0 - over), amplitude * filter_ratio / (1.0 - times), corner, corner * filter_ratio


def split(values):
    high = values.astype(bfloat16)
    return high, (values - high.astype(jnp.float32)).astype(bfloat16)


def product(left, right, sides=((1,), (0,))):
    return lax.dot_general(left, right, (sides, ((), ())), preferred_element_type=jnp.float32)


def exchange_kernel(
    nx,
    ny,
    nz,
    den_hbm,
    mom_hbm,
    ene_hbm,
    metric_hbm,
    wtab_hbm,
    ky_hbm,
    py_hbm,
    kz_hbm,
    qz_hbm,
    pz_hbm,
    tend,
    carry_x,
    carry_f,
    carry_d,
    carry_n,
    den,
    mom,
    ene,
    metric,
    wtab,
    ky,
    py,
    kz,
    qz,
    pz,
    ky_high,
    ky_low,
    py_both,
    fx,
    fy,
    fz,
    uv0,
    moments_x,
    sy,
    sz,
    dys,
    dzs,
    ys_out,
    ys_in,
    zs_in,
    yb_out,
    yb_in,
    zm_in,
    xn_out,
    xn_in,
    pair_in,
    xm_out,
    xm_in,
    uv_out,
    uv_in,
    xo_out,
    xo_in,
    xp_in,
    io_out,
    io_in,
    state_sem,
    load_sem,
    send_sem,
    recv_sem,
):
    fields, size_x, size_y, size_z = fx.shape
    me_x, me_y, me_z = lax.axis_index("gx"), lax.axis_index("gy"), lax.axis_index("gz")
    rows = size_y // nx
    ratio, amplitude, corner = compact_kernel()
    filter_ratio, _ = decay(filter_alpha)
    gain_d, _, far_d, corner_d, first_d = filtered_derivative()
    half_rows = fields * rows
    chips = nx // 2
    chip, core = me_x // 2, lax.rem(me_x, 2)
    pair = 1 - 2 * core
    half_y = size_y // 2

    def farthest(count):
        return sorted(range(1, count), key=lambda k: -min(k, count - k))

    def along(axis, offset):
        me, count = {"gx": (me_x, nx), "gy": (me_y, ny), "gz": (me_z, nz)}[axis]
        return lax.rem(me + offset + count, count)

    class Group:
        def __init__(self, copies, sent, received):
            self.copies, self.sent, self.received = copies, sent, received

        def start(self):
            for copy in self.copies:
                copy.start()

        def wait(self):
            pltpu.make_async_copy(self.received[0], self.received[0], self.received[1]).wait()

        def wait_sent(self):
            pltpu.make_async_copy(self.sent[0], self.sent[0], self.sent[1]).wait()

    def state_loads(chunk):
        ys = pl.ds(pl.multiple_of(chunk * 8, 8), 8)
        return [
            pltpu.make_async_copy(den_hbm.at[:, ys], den.at[:, ys], state_sem.at[0, chunk]),
            pltpu.make_async_copy(mom_hbm.at[:, :, ys], mom.at[:, :, ys], state_sem.at[1, chunk]),
            pltpu.make_async_copy(ene_hbm.at[:, ys], ene.at[:, ys], state_sem.at[2, chunk]),
        ]

    sources = (wtab_hbm, ky_hbm.at[me_y], py_hbm.at[me_y], metric_hbm, kz_hbm, qz_hbm, pz_hbm)
    targets = (wtab, ky, py, metric, kz, qz, pz)
    loads = [
        pltpu.make_async_copy(source, target, load_sem.at[place])
        for place, (source, target) in enumerate(zip(sources, targets))
    ]
    loads[0].start()
    for chunk in range(size_y // 8):
        for load in state_loads(chunk):
            load.start()
    for load in loads[1:]:
        load.start()

    yb_in[...] = jnp.zeros(yb_in.shape, jnp.float32)

    barrier = pltpu.get_barrier_semaphore()
    for axis, count in (("gx", nx), ("gy", ny), ("gz", nz)):
        for offset in range(1, count):
            pl.semaphore_signal(barrier, inc=1, device_id={axis: along(axis, offset)}, device_id_type=MESH)

    next_sem = [0]

    def remote(src, dst, axis, offset):
        place = next_sem[0]
        next_sem[0] = place + 1
        return pltpu.make_async_remote_copy(
            src_ref=src,
            dst_ref=dst,
            send_sem=send_sem.at[place],
            recv_sem=recv_sem.at[place],
            device_id={axis: along(axis, offset)},
            device_id_type=MESH,
        )

    def remote_group(blocks, step, source, target):
        place = next_sem[0]
        next_sem[0] = place + 1
        sems = send_sem.at[place], recv_sem.at[place]
        copies = [
            pltpu.make_async_remote_copy(
                src_ref=source(k),
                dst_ref=target(k),
                send_sem=sems[0],
                recv_sem=sems[1],
                device_id={"gx": along("gx", step * k)},
                device_id_type=MESH,
            )
            for k in farthest(blocks)
        ]
        return lambda out, arrived: Group(
            copies, (out.at[pl.ds(0, blocks - 1)], sems[0]), (arrived.at[pl.ds(0, blocks - 1)], sems[1])
        )

    loads[0].wait()

    unroll = 4
    zero = jnp.zeros((8, size_z), jnp.float32)

    def flux_chunk(chunk, _):
        ys = pl.ds(pl.multiple_of(chunk * 8, 8), 8)
        for load in state_loads(chunk):
            load.wait()

        def cells(step, acc):
            acc = list(acc)
            for inner in range(unroll):
                x = step * unroll + inner
                w = [wtab[k, x] for k in range(4)]
                rho, energy = den[x, ys, :], ene[x, ys, :]
                m = [mom[j, x, ys, :] for j in range(3)]
                inverse = 1.0 / rho
                v = [m[j] * inverse for j in range(3)]
                own = [m[j] * v[j] for j in range(3)]
                pressure = (heat_ratio - 1.0) * (energy - 0.5 * (own[0] + own[1] + own[2]))
                m12, m13, m23 = m[0] * v[1], m[0] * v[2], m[1] * v[2]
                total = energy + pressure
                flux_x = (m[0], own[0] + pressure, m12, m13, total * v[0])
                flux_y = (m[1], m12, own[1] + pressure, m23, total * v[1])
                flux_z = (m[2], m13, m23, own[2] + pressure, total * v[2])
                state = (rho, m[0], m[1], m[2], energy)
                for f in range(fields):
                    fx[f, x, ys, :] = flux_x[f]
                    fy[f, x, ys, :] = flux_y[f]
                    fz[f, x, ys, :] = flux_z[f]
                    change = (time_step * gain_d) * flux_x[f]
                    acc[f] = acc[f] + w[0] * (state[f] - change)
                    acc[5 + f] = acc[5 + f] + w[1] * (state[f] + change)
                    acc[10 + f] = acc[10 + f] + w[2] * flux_x[f]
                    acc[15 + f] = acc[15 + f] + w[3] * flux_x[f]
            return tuple(acc)

        acc = lax.fori_loop(0, size_x // unroll, cells, (zero,) * 20)
        for f in range(fields):
            uv0[0, f, ys, :] = acc[f]
            uv0[1, f, ys, :] = acc[5 + f]
            moments_x[0, f, ys, :] = acc[10 + f]
            moments_x[1, f, ys, :] = acc[15 + f]
            xn_out[0, f, ys, :] = fx[f, size_x - 1, ys, :]
            xn_out[1, f, ys, :] = fx[f, 0, ys, :]
        return 0

    sy[10:16] = jnp.zeros((6, size_y, size_z), jnp.float32)
    sz[:, 5:8] = jnp.zeros((2, 3, size_y, size_z), jnp.float32)
    lax.fori_loop(0, size_y // 8, flux_chunk, 0)

    def deal(message, side, f, values):
        for owner in range(values.shape[0] // rows):
            place = side * half_rows + rows * f
            message[owner, place : place + rows, :] = values[rows * owner : rows * owner + rows]

    pl.semaphore_wait(barrier, nx + ny + nz - 3)
    to_pair = remote(moments_x, pair_in, "gx", pair)
    to_pair.start()

    def sums_chunk(chunk, _):
        ys = pl.ds(pl.multiple_of(chunk * 8, 8), 8)

        def sums(step, acc):
            acc = list(acc)
            for inner in range(unroll):
                x = step * unroll + inner
                w = [wtab[k, x] for k in range(2)]
                for f in range(fields):
                    value_y, value_z = fy[f, x, ys, :], fz[f, x, ys, :]
                    acc[f] = acc[f] + w[0] * value_y
                    acc[5 + f] = acc[5 + f] + w[1] * value_y
                    acc[10 + f] = acc[10 + f] + w[0] * value_z
                    acc[15 + f] = acc[15 + f] + w[1] * value_z
            return tuple(acc)

        acc = lax.fori_loop(0, size_x // unroll, sums, (zero,) * 20)
        for f in range(fields):
            sy[f, ys, :] = acc[f]
            sy[5 + f, ys, :] = acc[5 + f]
            sz[0, f, ys, :] = acc[10 + f]
            sz[1, f, ys, :] = acc[15 + f]
        return 0

    lax.fori_loop(0, size_y // 8, sums_chunk, 0)

    for load in loads[1:]:
        load.wait()
    shape = (8 * size_y, ny * size_y)
    row_place = lax.broadcasted_iota(jnp.int32, shape, 0)
    col_place = lax.broadcasted_iota(jnp.int32, shape, 1)
    mine = col_place == me_y * size_y + lax.rem(row_place, size_y)
    metric_rows = jnp.sum(jnp.where(mine, metric[...], 0.0), axis=1, keepdims=True)
    ky[: 8 * size_y, :] = ky[: 8 * size_y, :] * metric_rows
    ky_high[...], ky_low[...] = split(ky[...])
    high, low = split(py[...] * metric_rows)
    py_both[...] = jnp.where(lax.broadcasted_iota(jnp.int32, py.shape, 1) < 128, high, low)

    def apply_wall(first, second):
        cells = jnp.concatenate(
            [first.reshape(8 * size_y, size_z), second.reshape(8 * size_y, size_z)], axis=1
        )
        high, low = split(cells)
        result = product(ky_high[...], high) + product(ky_high[...], low) + product(ky_low[...], high)
        return [
            (
                result[: 8 * size_y, lanes].reshape(8, size_y, size_z),
                result[8 * size_y :, lanes].reshape(4, 8, size_z),
            )
            for lanes in (slice(0, size_z), slice(size_z, 2 * size_z))
        ]

    def wall_carries(first, second):
        cells = jnp.concatenate([first.reshape(64, size_z), second.reshape(64, size_z)], axis=1)
        high, low = split(cells)
        return product(py_both[...], jnp.concatenate([high, low, high], axis=0))

    def span_local(cells):
        result = product(jnp.concatenate(split(cells), axis=1), kz[...])
        return result[:, :size_z] + result[:, size_z:]

    def span_moments(first, second):
        high, low = split(jnp.concatenate([first, second], axis=1))
        from_high = product(qz[...], high, ((1,), (1,)))
        from_low = product(qz[...], low, ((1,), (1,)))
        return from_high[:8] + from_high[8:] + (from_low[:8] + from_low[8:])

    def span_carries(received):
        high, low = split(received)
        return product(jnp.concatenate([high, low, high], axis=0), pz[...], ((0,), (0,)))

    for group, (local, moments) in enumerate(apply_wall(sy[0:8], sy[8:16])):
        dys[8 * group : 8 * group + 8] = local
        ys_out[:, 8 * group : 8 * group + 8, :] = moments
    ys = [
        remote(ys_out.at[pl.ds(0, 3)], ys_in.at[pl.ds(0, 3)], "gy", 1),
        remote(ys_out.at[pl.ds(1, 2)], ys_in.at[pl.ds(3, 2)], "gy", 2),
        remote(ys_out.at[pl.ds(1, 3)], ys_in.at[pl.ds(5, 3)], "gy", 3),
    ]
    for copy in ys:
        copy.start()
    zs_in[0] = span_moments(sz[0].reshape(8 * size_y, size_z), sz[1].reshape(8 * size_y, size_z))
    zs = [remote(zs_in.at[0], zs_in.at[k], "gz", k) for k in range(1, nz)]
    for copy in zs:
        copy.start()
    dzs[...] = span_local(sz[...].reshape(16 * size_y, size_z)).reshape(2, 8, size_y, size_z)

    to_pair.wait()
    power = float(ratio**size_x)
    second = core == 1
    mine = pl.ds(pl.multiple_of(half_y * core, 8), half_y)
    for side in range(2):
        is_near = second if side == 0 else jnp.logical_not(second)
        own_gain, pair_gain = jnp.where(is_near, 1.0, power), jnp.where(is_near, power, 1.0)
        for f in range(fields):
            deal(xm_out, side, f, own_gain * moments_x[side, f, mine, :] + pair_gain * pair_in[side, f, mine, :])
        carry_n[side] = jnp.where(is_near, 1.0, 0.0) * pair_in[side]
    xm = remote_group(chips, 2, lambda k: xm_out.at[lax.rem(chip + k, chips)], lambda k: xm_in.at[k])(xm_out, xm_in)
    xm.start()
    xm_in[0] = xm_out[chip]

    def wall_field(f, _):
        for part in range(size_x // 16):
            pair = [pl.ds(16 * part + 8 * side, 8) for side in range(2)]
            for xs, (local, moments) in zip(pair, apply_wall(fy[f, pair[0]], fy[f, pair[1]])):
                tend[f, xs] = local
                yb_out[:, f, xs, :] = moments
        return 0

    lax.fori_loop(0, fields, wall_field, 0)
    yb = []
    for distance in range(1, ny):
        count = 2 if distance == 1 else 1
        up_place = KINDS_Y.index((distance, "last" if distance == 1 else "ml"))
        down_place = KINDS_Y.index((ny - distance, "mr"))
        up = remote(yb_out.at[pl.ds(2 - count, count)], yb_in.at[pl.ds(up_place, count)], "gy", distance)
        down = remote(yb_out.at[pl.ds(2, count)], yb_in.at[pl.ds(down_place, count)], "gy", -distance)
        has_above, has_below = me_y < ny - distance, me_y >= distance
        yb += [(up, has_above, has_below), (down, has_below, has_above)]
    for copy, sends, _ in yb:
        pl.when(sends)(copy.start)

    for copy in ys + zs:
        copy.wait()
    span = span_carries(zs_in[...].reshape(8 * nz, 8 * size_y))
    wall = wall_carries(ys_in[:, 0:8, :], ys_in[:, 8:16, :])
    for side in range(2):
        for f in range(fields):
            unit = 5 * side + f
            place, lane = (unit % 8) * size_y, (unit // 8) * size_z
            change = dys[unit] + wall[place : place + size_y, lane : lane + size_z]
            change = change + dzs[side, f] + span[f * size_y : (f + 1) * size_y, side * size_z : (side + 1) * size_z]
            deal(uv_out, side, f, uv0[side, f] - time_step * change)
    uv = remote_group(nx, 1, lambda k: uv_out.at[along("gx", k)], lambda k: uv_in.at[k])(uv_out, uv_in)
    uv.start()
    uv_in[0] = uv_out[me_x]

    xn = [
        remote(xn_out.at[0], xn_in.at[0], "gx", 1),
        remote(xn_out.at[1], xn_in.at[1], "gx", -1),
    ]
    for copy in xn:
        copy.start()

    half = size_x // 2

    def span_field(f, _):
        pair = [fz[f, pl.ds(part * half, half)].reshape(half * size_y, size_z) for part in range(2)]
        zm_in[0, f] = span_moments(*pair)
        return 0

    lax.fori_loop(0, fields, span_field, 0)
    zm = [remote(zm_in.at[0], zm_in.at[k], "gz", k) for k in range(1, nz)]
    for copy in zm:
        copy.start()

    def span_cells(f, _):
        for part in range(size_x // 8):
            xs = pl.ds(8 * part, 8)
            tend[f, xs] += span_local(fz[f, xs].reshape(8 * size_y, size_z)).reshape(8, size_y, size_z)
        return 0

    lax.fori_loop(0, fields, span_cells, 0)

    def sweep(behind, power, values):
        step, count = 1 if behind else -1, len(values)
        total = values[0] if behind else values[count - 1]
        for k in range(1, count):
            total = total + float(power**k) * (values[k] if behind else values[count - 1 - k])
        total = total * float(1.0 / (1.0 - power**count))
        place = count - 1 if behind else 0
        result = [None] * count
        result[place] = total
        for _ in range(count - 1):
            total = values[place] + float(power) * total
            place = place - step
            result[place] = total
        return result

    from_behind = lax.broadcasted_iota(jnp.int32, (2 * half_rows, size_z), 0) < half_rows

    def solve_lines(received, power, answers):
        values = [received[k] for k in range(received.shape[0])]
        behind, ahead = sweep(True, power, values), sweep(False, power, values)
        for k in range(len(values)):
            answers[k] = jnp.where(from_behind, behind[k], ahead[k])

    xm.wait()
    solve_lines(xm_in, ratio ** (2 * size_x), xo_out)
    xo = remote_group(chips, -2, lambda k: xo_out.at[k], lambda k: xo_in.at[chip])(xo_out, xo_in)
    xo.start()
    xo_in[chip] = xo_out[0]

    def scan_chunk(chunk, _):
        ys = pl.ds(pl.multiple_of(chunk * 8, 8), 8)

        def scan(side, step, carried):
            carried = list(carried)
            for inner in range(unroll):
                x = step * unroll + inner
                x = size_x - 1 - x if side else x
                gains = (-amplitude, -corner) if side else (amplitude, corner)
                for f in range(fields):
                    total, last = carried[f], carried[5 + f]
                    tend[f, x, ys, :] += gains[0] * total + gains[1] * last
                    here = fx[f, x, ys, :]
                    carried[f], carried[5 + f] = ratio * (total + here), here
            return tuple(carried)

        for side in range(2):
            lax.fori_loop(0, size_x // unroll, functools.partial(scan, side), (zero,) * 10)
        return 0

    lax.fori_loop(0, size_y // 8, scan_chunk, 0)

    uv.wait()
    solve_lines(uv_in, filter_ratio**size_x, io_out)
    io = remote_group(nx, -1, lambda k: io_out.at[k], lambda k: io_in.at[me_x])(io_out, io_in)
    io.start()
    io_in[me_x] = io_out[0]

    for copy in xn:
        copy.wait()
    tend[:, 0] += corner * xn_in[0]
    tend[:, size_x - 1] -= corner * xn_in[1]

    for side in range(2):
        sign = -time_step if side else time_step
        carry_d[side] = sign * (corner_d * xn_in[side] + far_d * moments_x[1 - side] + first_d * xn_out[1 - side])

    xo.wait()
    halves = remote(xo_in, xp_in, "gx", pair)
    halves.start()

    for copy in zm:
        copy.wait()
    for copy, sends, receives in yb:
        pl.when(sends)(copy.wait_send)
        pl.when(receives)(copy.wait_recv)

    def carries(f, _):
        both = span_carries(zm_in[:, f].reshape(8 * nz, half * size_y))
        for part in range(size_x // 16):
            pair = [pl.ds(16 * part + 8 * side, 8) for side in range(2)]
            wall = wall_carries(yb_in[:, f, pair[0], :], yb_in[:, f, pair[1], :])
            for side, xs in enumerate(pair):
                row = (16 * part + 8 * side) % half * size_y
                lane = (16 * part + 8 * side) // half * size_z
                change = wall[:, side * size_z : (side + 1) * size_z]
                change = change + both[row : row + 8 * size_y, lane : lane + size_z]
                tend[f, xs] += change.reshape(8, size_y, size_z)
        return 0

    lax.fori_loop(0, fields, carries, 0)

    for group in (xm, uv, xo, io):
        group.wait_sent()
    halves.wait()
    gains = jnp.where(from_behind, jnp.where(second, power, 1.0), jnp.where(second, 1.0, power))
    carry_x[pl.ds(chips * core, chips)] = xo_in[...] * gains
    carry_x[pl.ds(chips * (1 - core), chips)] = xp_in[...] * gains
    io.wait()
    carry_f[...] = io_in[...]


def filter_kernel(den, mom, ene, part, carry_x, carry_f, carry_d, carry_n, tend_hbm, after_hbm, tend, after, sems):
    chunks, fields, size_x = tend.shape[:3]
    half_rows = carry_x.shape[1] // 2
    rows = half_rows // fields
    owners = 8 // rows
    ratio, far_gain, _ = compact_kernel()
    filter_ratio, gain = decay(filter_alpha)
    straight = 0.5 * (0.5 + filter_alpha) / filter_alpha
    amplitude = (0.5 + filter_alpha - straight) * gain
    _, near_d, far_d, _, _ = filtered_derivative()
    power = ratio**size_x
    unroll = 4

    def copies(chunk):
        ys = pl.ds(pl.multiple_of(chunk * 8, 8), 8)
        return (
            pltpu.make_async_copy(tend.at[chunk], tend_hbm.at[:, :, ys], sems.at[0, chunk]),
            pltpu.make_async_copy(after.at[chunk], after_hbm.at[:, :, ys], sems.at[1, chunk]),
        )

    def chunk_body(chunk, _):
        ys = pl.ds(pl.multiple_of(chunk * 8, 8), 8)

        def carried_in(ref, side, f):
            place = side * half_rows + rows * f
            return jnp.concatenate(
                [ref[chunk * owners + o, place : place + rows, :] for o in range(owners)], axis=0
            )

        def state(f, x):
            return den[x, ys, :] if f == 0 else ene[x, ys, :] if f == 4 else mom[f - 1, x, ys, :]

        from_l = [carried_in(carry_x, 0, f) + carry_n[0, f, ys, :] for f in range(fields)]
        from_r = [carried_in(carry_x, 1, f) + carry_n[1, f, ys, :] for f in range(fields)]
        start_l = [
            carried_in(carry_f, 0, f)
            + carry_d[0, f, ys, :]
            + time_step * (near_d * from_l[f] + float(far_d * power) * from_r[f])
            for f in range(fields)
        ]
        start_r = [
            carried_in(carry_f, 1, f)
            + carry_d[1, f, ys, :]
            - time_step * (near_d * from_r[f] + float(far_d * power) * from_l[f])
            for f in range(fields)
        ]
        head = [float(far_gain * ratio ** (size_x - 1)) * from_l[f] for f in range(fields)]
        tail = [far_gain * from_r[f] for f in range(fields)]

        def back(step, carried):
            carried = list(carried)
            for inner in range(unroll):
                x = size_x - 1 - (step * unroll + inner)
                for f in range(fields):
                    behind, ahead = carried[5 + f], carried[10 + f]
                    rate = ahead - behind - part[f, x, ys, :]
                    tend[chunk, f, x] = rate
                    after[chunk, f, x] = amplitude * carried[f]
                    carried[f] = filter_ratio * (carried[f] + (state(f, x) + time_step * rate))
                    carried[5 + f], carried[10 + f] = (1.0 / ratio) * behind, ratio * ahead
            return tuple(carried)

        def ahead(step, carried):
            carried = list(carried)
            for inner in range(unroll):
                x = step * unroll + inner
                for f in range(fields):
                    middle = state(f, x) + time_step * tend[chunk, f, x]
                    after[chunk, f, x] += (straight + amplitude) * middle + amplitude * carried[f]
                    carried[f] = filter_ratio * (carried[f] + middle)
            return tuple(carried)

        lax.fori_loop(0, size_x // unroll, back, tuple(start_r + head + tail))
        rate_copy, after_copy = copies(chunk)
        rate_copy.start()
        lax.fori_loop(0, size_x // unroll, ahead, tuple(start_l))
        after_copy.start()
        return 0

    lax.fori_loop(0, chunks, chunk_body, 0)
    for chunk in range(chunks):
        for copy in copies(chunk):
            copy.wait()


def solution(mesh):
    nx, ny, nz = mesh.shape["gx"], mesh.shape["gy"], mesh.shape["gz"]

    def on_device(density, momentum, energy, metric):
        size_x, size_y, size_z = density.shape
        fields = 5
        rows = size_y // nx
        float32 = jnp.float32
        ky, py = wall_tables(ny, size_y)
        kz, qz, pz = span_tables(nz, size_z)
        wtab = stream_weights(size_x).astype(np.float32)
        cells = (fields, size_x, size_y, size_z)
        owned = (nx, 2 * fields * rows, size_z)
        chipwise = (nx // 2, 2 * fields * rows, size_z)
        sides = (2, fields, size_y, size_z)
        vmem = pl.BlockSpec(memory_space=pltpu.VMEM)
        stays = pl.BlockSpec(memory_space=pltpu.HBM)
        copies = 11 + 2 * (ny - 1) + 2 * (nz - 1)
        chunks = size_y // 8
        part, carry_x, carry_f, carry_d, carry_n = pl.pallas_call(
            functools.partial(exchange_kernel, nx, ny, nz),
            out_shape=[
                jax.ShapeDtypeStruct(cells, float32),
                jax.ShapeDtypeStruct(owned, float32),
                jax.ShapeDtypeStruct(owned, float32),
                jax.ShapeDtypeStruct(sides, float32),
                jax.ShapeDtypeStruct(sides, float32),
            ],
            in_specs=[stays] * 10,
            out_specs=[vmem] * 5,
            scratch_shapes=[
                pltpu.VMEM(cells[1:], float32),
                pltpu.VMEM((3,) + cells[1:], float32),
                pltpu.VMEM(cells[1:], float32),
                pltpu.VMEM((1, ny * size_y), float32),
                pltpu.SMEM(wtab.shape, float32),
                pltpu.VMEM(ky.shape[1:], float32),
                pltpu.VMEM(py.shape[1:], float32),
                pltpu.VMEM(kz.shape, bfloat16),
                pltpu.VMEM(qz.shape, bfloat16),
                pltpu.VMEM(pz.shape, bfloat16),
                pltpu.VMEM(ky.shape[1:], bfloat16),
                pltpu.VMEM(ky.shape[1:], bfloat16),
                pltpu.VMEM(py.shape[1:], bfloat16),
                pltpu.VMEM(cells, float32),
                pltpu.VMEM(cells, float32),
                pltpu.VMEM(cells, float32),
                pltpu.VMEM(sides, float32),
                pltpu.VMEM(sides, float32),
                pltpu.VMEM((16, size_y, size_z), float32),
                pltpu.VMEM((2, 8, size_y, size_z), float32),
                pltpu.VMEM((16, size_y, size_z), float32),
                pltpu.VMEM((2, 8, size_y, size_z), float32),
                pltpu.VMEM((4, 16, size_z), float32),
                pltpu.VMEM((8, 16, size_z), float32),
                pltpu.VMEM((nz, 8, 8 * size_y), float32),
                pltpu.VMEM((4, fields, size_x, size_z), float32),
                pltpu.VMEM((8, fields, size_x, size_z), float32),
                pltpu.VMEM((nz, fields, 8, size_x // 2 * size_y), float32),
                pltpu.VMEM(sides, float32),
                pltpu.VMEM(sides, float32),
                pltpu.VMEM(sides, float32),
                pltpu.VMEM(chipwise, float32),
                pltpu.VMEM(chipwise, float32),
                pltpu.VMEM(owned, float32),
                pltpu.VMEM(owned, float32),
                pltpu.VMEM(chipwise, float32),
                pltpu.VMEM(chipwise, float32),
                pltpu.VMEM(chipwise, float32),
                pltpu.VMEM(owned, float32),
                pltpu.VMEM(owned, float32),
                pltpu.SemaphoreType.DMA((3, chunks)),
                pltpu.SemaphoreType.DMA((7,)),
                pltpu.SemaphoreType.DMA((copies,)),
                pltpu.SemaphoreType.DMA((copies,)),
            ],
            compiler_params=pltpu.CompilerParams(
                collective_id=0, has_side_effects=True, vmem_limit_bytes=24 * 1024 * 1024
            ),
            cost_estimate=pl.CostEstimate(flops=4 * 10**9, bytes_accessed=10**7, transcendentals=0),
        )(
            *[
                pltpu.with_memory_space_constraint(jnp.asarray(value), pltpu.HBM)
                for value in (density, momentum, energy, metric.reshape(1, -1), wtab, ky, py, kz, qz, pz)
            ]
        )
        return pl.pallas_call(
            filter_kernel,
            out_shape=[jax.ShapeDtypeStruct(cells, float32), jax.ShapeDtypeStruct(cells, float32)],
            in_specs=[vmem] * 8,
            out_specs=[stays] * 2,
            scratch_shapes=[
                pltpu.VMEM((chunks, fields, size_x, 8, size_z), float32),
                pltpu.VMEM((chunks, fields, size_x, 8, size_z), float32),
                pltpu.SemaphoreType.DMA((2, chunks)),
            ],
            compiler_params=pltpu.CompilerParams(vmem_limit_bytes=16 * 1024 * 1024),
            cost_estimate=pl.CostEstimate(flops=10**7, bytes_accessed=10**7, transcendentals=0),
        )(density, momentum, energy, part, carry_x, carry_f, carry_d, carry_n)

    return jax.shard_map(
        on_device,
        mesh=mesh,
        in_specs=(P("gx", "gy", "gz"), P(None, "gx", "gy", "gz"), P("gx", "gy", "gz"), P()),
        out_specs=(P(None, "gx", "gy", "gz"), P(None, "gx", "gy", "gz")),
        check_vma=False,
    )
```

```python
import functools

import jax
import jax.numpy as jnp
import numpy as np
from jax import lax
from jax.experimental import pallas as pl
from jax.experimental.pallas import tpu as pltpu
from jax.sharding import PartitionSpec as P

heat_ratio = 1.4
compact_alpha = 1.0 / 3.0
filter_alpha = 0.499
time_step = 0.05
near_weight = 7.0 / 9.0
wide_weight = 1.0 / 36.0
bfloat16 = jnp.bfloat16
MESH = pl.DeviceIdType.MESH
KINDS_Y = ((1, "last"), (1, "ml"), (1, "mr"), (2, "ml"), (2, "mr"), (3, "ml"), (3, "mr"), (3, "first"))


def decay(alpha):
    root = np.sqrt(1.0 - 4.0 * alpha * alpha)
    return (-1.0 + root) / (2.0 * alpha), 1.0 / root


def compact_kernel():
    ratio, gain = decay(compact_alpha)

    def green(n):
        return gain * ratio ** abs(n)

    def kernel(d):
        return near_weight * (green(d + 1) - green(d - 1)) + wide_weight * (green(d + 2) - green(d - 2))

    amplitude = kernel(2) / ratio**2
    return ratio, amplitude, kernel(1) - amplitude * ratio


def local_compact(size):
    ratio, amplitude, corner = compact_kernel()
    table = np.zeros((size, size))
    for i in range(size):
        for j in range(size):
            d = abs(i - j)
            if d:
                value = amplitude * ratio**d + (corner if d == 1 else 0.0)
                table[i, j] = value if i > j else -value
    return table


def table_thomas(lower_band, main_band, upper_band, source):
    count = source.shape[0]
    c_all = np.zeros(count)
    d_all = np.zeros(source.shape)
    c_prev = 0.0
    d_prev = np.zeros(source.shape[1:])
    for place in range(count):
        denom = main_band[place] - lower_band[place] * c_prev
        c_prev = upper_band[place] / denom
        d_prev = (source[place] - lower_band[place] * d_prev) / denom
        c_all[place] = c_prev
        d_all[place] = d_prev
    solved = np.zeros(source.shape)
    x_next = np.zeros(source.shape[1:])
    for place in range(count - 1, -1, -1):
        x_next = d_all[place] - c_all[place] * x_next
        solved[place] = x_next
    return solved


def wall_bands(total):
    lower = np.full(total, compact_alpha)
    upper = np.full(total, compact_alpha)
    lower[0], lower[1], lower[total - 2], lower[total - 1] = 0.0, 0.25, 0.25, 2.0
    upper[0], upper[1], upper[total - 2], upper[total - 1] = 2.0, 0.25, 0.25, 0.0
    return lower, upper


def wall_table(total):
    lower, upper = wall_bands(total)
    stencil = np.zeros((total, total))
    for i in range(2, total - 2):
        stencil[i, i + 1], stencil[i, i - 1] = near_weight, -near_weight
        stencil[i, i + 2], stencil[i, i - 2] = wide_weight, -wide_weight
    for i in (1, total - 2):
        stencil[i, i + 1], stencil[i, i - 1] = 0.75, -0.75
    stencil[0, :3] = (-2.5, 2.0, 0.5)
    stencil[total - 1, total - 3 :] = (-0.5, -2.0, 2.5)
    return table_thomas(lower, np.ones(total), upper, stencil)


@functools.cache
def wall_tables(blocks, size):
    total = blocks * size
    table = wall_table(total)
    lower, upper = wall_bands(total)
    down = np.zeros(total)
    for i in range(total - 1, 0, -1):
        down[i - 1] = -lower[i] / (1.0 + upper[i] * down[i])
    up = np.zeros(total)
    for i in range(total - 1):
        up[i + 1] = -upper[i] / (1.0 + lower[i] * up[i])
    carry_l, carry_r, corner_l, corner_r = [], [], [], []
    moment_l, moment_r = np.zeros((blocks, size)), np.zeros((blocks, size))
    for b in range(blocks):
        head, tail = b * size, b * size + size - 1
        carry_l.append(np.concatenate([[1.0], np.cumprod(down[head:tail])]))
        carry_r.append(np.concatenate([[1.0], np.cumprod(up[head + 1 : tail + 1][::-1])])[::-1])
        corner_l.append(table[head, head - 1] - table[head + 1, head - 1] / down[head] if b else 0.0)
        corner_r.append(table[tail, tail + 1] - table[tail - 1, tail + 1] / up[tail] if b < blocks - 1 else 0.0)
        if b < blocks - 1:
            to = tail + 1
            moment_l[b] = table[to, head:to]
            moment_l[b, size - 1] = table[to + 1, tail] / down[to]
        if b:
            to = head - 1
            moment_r[b] = table[to, head : tail + 1]
            moment_r[b, 0] = table[to - 1, head] / up[to]
    apply = np.zeros((blocks, 8 * size + 32, 8 * size))
    carry = np.zeros((blocks, 8 * size, 8 * len(KINDS_Y)))
    eye = np.eye(8)
    for b in range(blocks):
        rows = slice(b * size, (b + 1) * size)
        apply[b, : 8 * size] = np.kron(eye, table[rows, rows])
        first, last = np.eye(size)[0], np.eye(size)[size - 1]
        for kind, weights in enumerate((last, moment_l[b], moment_r[b], first)):
            apply[b, 8 * size + 8 * kind : 8 * size + 8 * kind + 8] = np.kron(eye, weights[None])
        for place, (offset, kind) in enumerate(KINDS_Y):
            column = np.zeros(size)
            if b - offset >= 0:
                if kind == "ml":
                    scale = 1.0
                    for c in range(b - offset + 1, b):
                        scale *= np.prod(down[c * size : (c + 1) * size])
                    column = scale * carry_l[b]
                elif kind == "last" and offset == 1:
                    column[0] = corner_l[b]
            else:
                distance = blocks - offset
                if kind == "mr":
                    scale = 1.0
                    for c in range(b + 1, b + distance):
                        scale *= np.prod(up[c * size : (c + 1) * size])
                    column = scale * carry_r[b]
                elif kind == "first" and distance == 1:
                    column[size - 1] = corner_r[b]
            carry[b, :, 8 * place : 8 * place + 8] = np.kron(eye, column[:, None])
    return apply.astype(np.float32), np.concatenate([carry] * 3, axis=2).astype(np.float32)


def table_split(table):
    high = table.astype(bfloat16)
    return high, (table - high.astype(np.float64)).astype(bfloat16)


@functools.cache
def span_tables(blocks, size):
    ratio, amplitude, corner = compact_kernel()
    places = np.arange(size)
    images = 1.0 / (1.0 - ratio ** (blocks * size))
    moments = np.zeros((4, size))
    moments[0, size - 1] = 1.0
    moments[1] = ratio ** (size - places)
    moments[2] = ratio ** (places + 1.0)
    moments[3, 0] = 1.0
    carries = np.zeros((blocks, 4, size))
    for slot in range(blocks):
        behind = slot if slot else blocks
        ahead = blocks - slot
        carries[slot, 1] = amplitude * images * ratio ** (size * (behind - 1.0)) * ratio**places
        carries[slot, 2] = -amplitude * images * ratio ** (size * (ahead - 1.0)) * ratio ** (size - 1.0 - places)
        if behind == 1:
            carries[slot, 0, 0] = corner
        if ahead == 1:
            carries[slot, 3, size - 1] = -corner
    both_moments = np.zeros((8, 2 * size))
    both_moments[:4, :size] = moments
    both_moments[4:, size:] = moments
    both_carries = np.zeros((blocks, 8, 2 * size))
    both_carries[:, :4, :size] = carries
    both_carries[:, 4:, size:] = carries
    local_high, local_low = table_split(local_compact(size).T)
    carry_high, carry_low = table_split(both_carries.reshape(8 * blocks, 2 * size))
    return (
        np.block([[local_high, local_low], [local_high, np.zeros_like(local_low)]]),
        np.concatenate(table_split(both_moments)),
        np.concatenate([carry_high, carry_high, carry_low]),
    )


def stream_weights(size):
    ratio, _, _ = compact_kernel()
    filter_ratio, _ = decay(filter_alpha)
    places = np.arange(size)
    return np.stack(
        [
            filter_ratio ** (size - places),
            filter_ratio ** (places + 1.0),
            ratio ** (size - places),
            ratio ** (places + 1.0),
        ]
    )


def filtered_derivative():
    ratio, amplitude, corner = compact_kernel()
    filter_ratio, _ = decay(filter_alpha)
    over, times = ratio / filter_ratio, ratio * filter_ratio
    gain = amplitude * (over / (1.0 - over) - times / (1.0 - times)) + corner * (1.0 / filter_ratio - filter_ratio)
    return gain, amplitude / (1.0 - over), amplitude * filter_ratio / (1.0 - times), corner, corner * filter_ratio


def split(values):
    high = values.astype(bfloat16)
    return high, (values - high.astype(jnp.float32)).astype(bfloat16)


def product(left, right, sides=((1,), (0,))):
    return lax.dot_general(left, right, (sides, ((), ())), preferred_element_type=jnp.float32)


def exchange_kernel(
    nx,
    ny,
    nz,
    den_hbm,
    mom_hbm,
    ene_hbm,
    metric_hbm,
    wtab_hbm,
    ky_hbm,
    py_hbm,
    kz_hbm,
    qz_hbm,
    pz_hbm,
    tend,
    carry_x,
    carry_f,
    carry_d,
    carry_n,
    den,
    mom,
    ene,
    metric,
    wtab,
    ky,
    py,
    kz,
    qz,
    pz,
    ky_high,
    ky_low,
    py_both,
    fx,
    fy,
    fz,
    uv0,
    moments_x,
    sy,
    sz,
    dys,
    dzs,
    ys_out,
    ys_in,
    zs_in,
    yb_out,
    yb_in,
    zm_in,
    xn_out,
    xn_in,
    pair_in,
    xm_out,
    xm_in,
    uv_out,
    uv_in,
    xo_out,
    xo_in,
    xp_in,
    io_out,
    io_in,
    state_sem,
    load_sem,
    send_sem,
    recv_sem,
):
    fields, size_x, size_y, size_z = fx.shape
    me_x, me_y, me_z = lax.axis_index("gx"), lax.axis_index("gy"), lax.axis_index("gz")
    rows = size_y // nx
    ratio, amplitude, corner = compact_kernel()
    filter_ratio, _ = decay(filter_alpha)
    gain_d, _, far_d, corner_d, first_d = filtered_derivative()
    half_rows = fields * rows
    chips = nx // 2
    chip, core = me_x // 2, lax.rem(me_x, 2)
    pair = 1 - 2 * core
    half_y = size_y // 2

    def farthest(count):
        return sorted(range(1, count), key=lambda k: -min(k, count - k))

    def along(axis, offset):
        me, count = {"gx": (me_x, nx), "gy": (me_y, ny), "gz": (me_z, nz)}[axis]
        return lax.rem(me + offset + count, count)

    class Group:
        def __init__(self, copies, sent, received):
            self.copies, self.sent, self.received = copies, sent, received

        def start(self):
            for copy in self.copies:
                copy.start()

        def wait(self):
            pltpu.make_async_copy(self.received[0], self.received[0], self.received[1]).wait()

        def wait_sent(self):
            pltpu.make_async_copy(self.sent[0], self.sent[0], self.sent[1]).wait()

    def state_loads(chunk):
        ys = pl.ds(pl.multiple_of(chunk * 8, 8), 8)
        return [
            pltpu.make_async_copy(den_hbm.at[:, ys], den.at[:, ys], state_sem.at[0, chunk]),
            pltpu.make_async_copy(mom_hbm.at[:, :, ys], mom.at[:, :, ys], state_sem.at[1, chunk]),
            pltpu.make_async_copy(ene_hbm.at[:, ys], ene.at[:, ys], state_sem.at[2, chunk]),
        ]

    sources = (wtab_hbm, ky_hbm.at[me_y], py_hbm.at[me_y], metric_hbm, kz_hbm, qz_hbm, pz_hbm)
    targets = (wtab, ky, py, metric, kz, qz, pz)
    loads = [
        pltpu.make_async_copy(source, target, load_sem.at[place])
        for place, (source, target) in enumerate(zip(sources, targets))
    ]
    loads[0].start()
    for chunk in range(size_y // 8):
        for load in state_loads(chunk):
            load.start()
    for load in loads[1:]:
        load.start()

    yb_in[...] = jnp.zeros(yb_in.shape, jnp.float32)

    barrier = pltpu.get_barrier_semaphore()
    for axis, count in (("gx", nx), ("gy", ny), ("gz", nz)):
        for offset in range(1, count):
            pl.semaphore_signal(barrier, inc=1, device_id={axis: along(axis, offset)}, device_id_type=MESH)

    next_sem = [0]

    def remote(src, dst, axis, offset):
        place = next_sem[0]
        next_sem[0] = place + 1
        return pltpu.make_async_remote_copy(
            src_ref=src,
            dst_ref=dst,
            send_sem=send_sem.at[place],
            recv_sem=recv_sem.at[place],
            device_id={axis: along(axis, offset)},
            device_id_type=MESH,
        )

    def remote_group(blocks, step, source, target):
        place = next_sem[0]
        next_sem[0] = place + 1
        sems = send_sem.at[place], recv_sem.at[place]
        copies = [
            pltpu.make_async_remote_copy(
                src_ref=source(k),
                dst_ref=target(k),
                send_sem=sems[0],
                recv_sem=sems[1],
                device_id={"gx": along("gx", step * k)},
                device_id_type=MESH,
            )
            for k in farthest(blocks)
        ]
        return lambda out, arrived: Group(
            copies, (out.at[pl.ds(0, blocks - 1)], sems[0]), (arrived.at[pl.ds(0, blocks - 1)], sems[1])
        )

    loads[0].wait()

    unroll = 8
    zero = jnp.zeros((8, size_z), jnp.float32)

    def flux_chunk(chunk, _):
        ys = pl.ds(pl.multiple_of(chunk * 8, 8), 8)
        for load in state_loads(chunk):
            load.wait()

        def cells(step, acc):
            acc = list(acc)
            for inner in range(unroll):
                x = step * unroll + inner
                w = [wtab[k, x] for k in range(4)]
                rho, energy = den[x, ys, :], ene[x, ys, :]
                m = [mom[j, x, ys, :] for j in range(3)]
                inverse = 1.0 / rho
                v = [m[j] * inverse for j in range(3)]
                own = [m[j] * v[j] for j in range(3)]
                pressure = (heat_ratio - 1.0) * (energy - 0.5 * (own[0] + own[1] + own[2]))
                m12, m13, m23 = m[0] * v[1], m[0] * v[2], m[1] * v[2]
                total = energy + pressure
                flux_x = (m[0], own[0] + pressure, m12, m13, total * v[0])
                flux_y = (m[1], m12, own[1] + pressure, m23, total * v[1])
                flux_z = (m[2], m13, m23, own[2] + pressure, total * v[2])
                state = (rho, m[0], m[1], m[2], energy)
                for f in range(fields):
                    fx[f, x, ys, :] = flux_x[f]
                    fy[f, x, ys, :] = flux_y[f]
                    fz[f, x, ys, :] = flux_z[f]
                    change = (time_step * gain_d) * flux_x[f]
                    acc[f] = acc[f] + w[0] * (state[f] - change)
                    acc[5 + f] = acc[5 + f] + w[1] * (state[f] + change)
                    acc[10 + f] = acc[10 + f] + w[2] * flux_x[f]
                    acc[15 + f] = acc[15 + f] + w[3] * flux_x[f]
            return tuple(acc)

        acc = lax.fori_loop(0, size_x // unroll, cells, (zero,) * 20)
        for f in range(fields):
            uv0[0, f, ys, :] = acc[f]
            uv0[1, f, ys, :] = acc[5 + f]
            moments_x[0, f, ys, :] = acc[10 + f]
            moments_x[1, f, ys, :] = acc[15 + f]
            xn_out[0, f, ys, :] = fx[f, size_x - 1, ys, :]
            xn_out[1, f, ys, :] = fx[f, 0, ys, :]
        return 0

    sy[10:16] = jnp.zeros((6, size_y, size_z), jnp.float32)
    sz[:, 5:8] = jnp.zeros((2, 3, size_y, size_z), jnp.float32)
    lax.fori_loop(0, size_y // 8, flux_chunk, 0)

    def deal(message, side, f, values):
        for owner in range(values.shape[0] // rows):
            place = side * half_rows + rows * f
            message[owner, place : place + rows, :] = values[rows * owner : rows * owner + rows]

    pl.semaphore_wait(barrier, nx + ny + nz - 3)
    to_pair = remote(moments_x, pair_in, "gx", pair)
    to_pair.start()

    def sums_chunk(chunk, _):
        ys = pl.ds(pl.multiple_of(chunk * 8, 8), 8)

        def sums(step, acc):
            acc = list(acc)
            for inner in range(unroll):
                x = step * unroll + inner
                w = [wtab[k, x] for k in range(2)]
                for f in range(fields):
                    value_y, value_z = fy[f, x, ys, :], fz[f, x, ys, :]
                    acc[f] = acc[f] + w[0] * value_y
                    acc[5 + f] = acc[5 + f] + w[1] * value_y
                    acc[10 + f] = acc[10 + f] + w[0] * value_z
                    acc[15 + f] = acc[15 + f] + w[1] * value_z
            return tuple(acc)

        acc = lax.fori_loop(0, size_x // unroll, sums, (zero,) * 20)
        for f in range(fields):
            sy[f, ys, :] = acc[f]
            sy[5 + f, ys, :] = acc[5 + f]
            sz[0, f, ys, :] = acc[10 + f]
            sz[1, f, ys, :] = acc[15 + f]
        return 0

    lax.fori_loop(0, size_y // 8, sums_chunk, 0)

    for load in loads[1:]:
        load.wait()
    shape = (8 * size_y, ny * size_y)
    row_place = lax.broadcasted_iota(jnp.int32, shape, 0)
    col_place = lax.broadcasted_iota(jnp.int32, shape, 1)
    mine = col_place == me_y * size_y + lax.rem(row_place, size_y)
    metric_rows = jnp.sum(jnp.where(mine, metric[...], 0.0), axis=1, keepdims=True)
    ky[: 8 * size_y, :] = ky[: 8 * size_y, :] * metric_rows
    ky_high[...], ky_low[...] = split(ky[...])
    high, low = split(py[...] * metric_rows)
    py_both[...] = jnp.where(lax.broadcasted_iota(jnp.int32, py.shape, 1) < 128, high, low)

    def apply_wall(first, second):
        cells = jnp.concatenate(
            [first.reshape(8 * size_y, size_z), second.reshape(8 * size_y, size_z)], axis=1
        )
        high, low = split(cells)
        result = product(ky_high[...], high) + product(ky_high[...], low) + product(ky_low[...], high)
        return [
            (
                result[: 8 * size_y, lanes].reshape(8, size_y, size_z),
                result[8 * size_y :, lanes].reshape(4, 8, size_z),
            )
            for lanes in (slice(0, size_z), slice(size_z, 2 * size_z))
        ]

    def wall_carries(first, second):
        cells = jnp.concatenate([first.reshape(64, size_z), second.reshape(64, size_z)], axis=1)
        high, low = split(cells)
        return product(py_both[...], jnp.concatenate([high, low, high], axis=0))

    def span_local(cells):
        result = product(jnp.concatenate(split(cells), axis=1), kz[...])
        return result[:, :size_z] + result[:, size_z:]

    def span_moments(first, second):
        high, low = split(jnp.concatenate([first, second], axis=1))
        from_high = product(qz[...], high, ((1,), (1,)))
        from_low = product(qz[...], low, ((1,), (1,)))
        return from_high[:8] + from_high[8:] + (from_low[:8] + from_low[8:])

    def span_carries(received):
        high, low = split(received)
        return product(jnp.concatenate([high, low, high], axis=0), pz[...], ((0,), (0,)))

    for group, (local, moments) in enumerate(apply_wall(sy[0:8], sy[8:16])):
        dys[8 * group : 8 * group + 8] = local
        ys_out[:, 8 * group : 8 * group + 8, :] = moments
    ys = [
        remote(ys_out.at[pl.ds(0, 3)], ys_in.at[pl.ds(0, 3)], "gy", 1),
        remote(ys_out.at[pl.ds(1, 2)], ys_in.at[pl.ds(3, 2)], "gy", 2),
        remote(ys_out.at[pl.ds(1, 3)], ys_in.at[pl.ds(5, 3)], "gy", 3),
    ]
    for copy in ys:
        copy.start()
    zs_in[0] = span_moments(sz[0].reshape(8 * size_y, size_z), sz[1].reshape(8 * size_y, size_z))
    zs = [remote(zs_in.at[0], zs_in.at[k], "gz", k) for k in range(1, nz)]
    for copy in zs:
        copy.start()
    dzs[...] = span_local(sz[...].reshape(16 * size_y, size_z)).reshape(2, 8, size_y, size_z)

    to_pair.wait()
    power = float(ratio**size_x)
    second = core == 1
    mine = pl.ds(pl.multiple_of(half_y * core, 8), half_y)
    for side in range(2):
        is_near = second if side == 0 else jnp.logical_not(second)
        own_gain, pair_gain = jnp.where(is_near, 1.0, power), jnp.where(is_near, power, 1.0)
        for f in range(fields):
            deal(xm_out, side, f, own_gain * moments_x[side, f, mine, :] + pair_gain * pair_in[side, f, mine, :])
        carry_n[side] = jnp.where(is_near, 1.0, 0.0) * pair_in[side]
    xm = remote_group(chips, 2, lambda k: xm_out.at[lax.rem(chip + k, chips)], lambda k: xm_in.at[k])(xm_out, xm_in)
    xm.start()
    xm_in[0] = xm_out[chip]

    def wall_field(f, _):
        for part in range(size_x // 16):
            pair = [pl.ds(16 * part + 8 * side, 8) for side in range(2)]
            for xs, (local, moments) in zip(pair, apply_wall(fy[f, pair[0]], fy[f, pair[1]])):
                tend[f, xs] = local
                yb_out[:, f, xs, :] = moments
        return 0

    lax.fori_loop(0, fields, wall_field, 0)
    yb = []
    for distance in range(1, ny):
        count = 2 if distance == 1 else 1
        up_place = KINDS_Y.index((distance, "last" if distance == 1 else "ml"))
        down_place = KINDS_Y.index((ny - distance, "mr"))
        up = remote(yb_out.at[pl.ds(2 - count, count)], yb_in.at[pl.ds(up_place, count)], "gy", distance)
        down = remote(yb_out.at[pl.ds(2, count)], yb_in.at[pl.ds(down_place, count)], "gy", -distance)
        has_above, has_below = me_y < ny - distance, me_y >= distance
        yb += [(up, has_above, has_below), (down, has_below, has_above)]
    for copy, sends, _ in yb:
        pl.when(sends)(copy.start)

    for copy in ys + zs:
        copy.wait()
    span = span_carries(zs_in[...].reshape(8 * nz, 8 * size_y))
    wall = wall_carries(ys_in[:, 0:8, :], ys_in[:, 8:16, :])
    for side in range(2):
        for f in range(fields):
            unit = 5 * side + f
            place, lane = (unit % 8) * size_y, (unit // 8) * size_z
            change = dys[unit] + wall[place : place + size_y, lane : lane + size_z]
            change = change + dzs[side, f] + span[f * size_y : (f + 1) * size_y, side * size_z : (side + 1) * size_z]
            deal(uv_out, side, f, uv0[side, f] - time_step * change)
    uv = remote_group(nx, 1, lambda k: uv_out.at[along("gx", k)], lambda k: uv_in.at[k])(uv_out, uv_in)
    uv.start()
    uv_in[0] = uv_out[me_x]

    xn = [
        remote(xn_out.at[0], xn_in.at[0], "gx", 1),
        remote(xn_out.at[1], xn_in.at[1], "gx", -1),
    ]
    for copy in xn:
        copy.start()

    half = size_x // 2

    def span_field(f, _):
        pair = [fz[f, pl.ds(part * half, half)].reshape(half * size_y, size_z) for part in range(2)]
        zm_in[0, f] = span_moments(*pair)
        return 0

    lax.fori_loop(0, fields, span_field, 0)
    zm = [remote(zm_in.at[0], zm_in.at[k], "gz", k) for k in range(1, nz)]
    for copy in zm:
        copy.start()

    def span_cells(f, _):
        for part in range(size_x // 8):
            xs = pl.ds(8 * part, 8)
            tend[f, xs] += span_local(fz[f, xs].reshape(8 * size_y, size_z)).reshape(8, size_y, size_z)
        return 0

    lax.fori_loop(0, fields, span_cells, 0)

    def sweep(behind, power, values):
        step, count = 1 if behind else -1, len(values)
        total = values[0] if behind else values[count - 1]
        for k in range(1, count):
            total = total + float(power**k) * (values[k] if behind else values[count - 1 - k])
        total = total * float(1.0 / (1.0 - power**count))
        place = count - 1 if behind else 0
        result = [None] * count
        result[place] = total
        for _ in range(count - 1):
            total = values[place] + float(power) * total
            place = place - step
            result[place] = total
        return result

    from_behind = lax.broadcasted_iota(jnp.int32, (2 * half_rows, size_z), 0) < half_rows

    def solve_lines(received, power, answers):
        values = [received[k] for k in range(received.shape[0])]
        behind, ahead = sweep(True, power, values), sweep(False, power, values)
        for k in range(len(values)):
            answers[k] = jnp.where(from_behind, behind[k], ahead[k])

    xm.wait()
    solve_lines(xm_in, ratio ** (2 * size_x), xo_out)
    xo = remote_group(chips, -2, lambda k: xo_out.at[k], lambda k: xo_in.at[chip])(xo_out, xo_in)
    xo.start()
    xo_in[chip] = xo_out[0]

    def scan_chunk(chunk, _):
        ys = pl.ds(pl.multiple_of(chunk * 8, 8), 8)

        def scan(side, step, carried):
            carried = list(carried)
            for inner in range(unroll):
                x = step * unroll + inner
                x = size_x - 1 - x if side else x
                gains = (-amplitude, -corner) if side else (amplitude, corner)
                for f in range(fields):
                    total, last = carried[f], carried[5 + f]
                    tend[f, x, ys, :] += gains[0] * total + gains[1] * last
                    here = fx[f, x, ys, :]
                    carried[f], carried[5 + f] = ratio * (total + here), here
            return tuple(carried)

        for side in range(2):
            lax.fori_loop(0, size_x // unroll, functools.partial(scan, side), (zero,) * 10)
        return 0

    lax.fori_loop(0, size_y // 8, scan_chunk, 0)

    uv.wait()
    solve_lines(uv_in, filter_ratio**size_x, io_out)
    io = remote_group(nx, -1, lambda k: io_out.at[k], lambda k: io_in.at[me_x])(io_out, io_in)
    io.start()
    io_in[me_x] = io_out[0]

    for copy in xn:
        copy.wait()
    tend[:, 0] += corner * xn_in[0]
    tend[:, size_x - 1] -= corner * xn_in[1]

    for side in range(2):
        sign = -time_step if side else time_step
        carry_d[side] = sign * (corner_d * xn_in[side] + far_d * moments_x[1 - side] + first_d * xn_out[1 - side])

    xo.wait()
    halves = remote(xo_in, xp_in, "gx", pair)
    halves.start()

    for copy in zm:
        copy.wait()
    for copy, sends, receives in yb:
        pl.when(sends)(copy.wait_send)
        pl.when(receives)(copy.wait_recv)

    def carries(f, _):
        both = span_carries(zm_in[:, f].reshape(8 * nz, half * size_y))
        for part in range(size_x // 16):
            pair = [pl.ds(16 * part + 8 * side, 8) for side in range(2)]
            wall = wall_carries(yb_in[:, f, pair[0], :], yb_in[:, f, pair[1], :])
            for side, xs in enumerate(pair):
                row = (16 * part + 8 * side) % half * size_y
                lane = (16 * part + 8 * side) // half * size_z
                change = wall[:, side * size_z : (side + 1) * size_z]
                change = change + both[row : row + 8 * size_y, lane : lane + size_z]
                tend[f, xs] += change.reshape(8, size_y, size_z)
        return 0

    lax.fori_loop(0, fields, carries, 0)

    for group in (xm, uv, xo, io):
        group.wait_sent()
    halves.wait()
    gains = jnp.where(from_behind, jnp.where(second, power, 1.0), jnp.where(second, 1.0, power))
    carry_x[pl.ds(chips * core, chips)] = xo_in[...] * gains
    carry_x[pl.ds(chips * (1 - core), chips)] = xp_in[...] * gains
    io.wait()
    carry_f[...] = io_in[...]


def filter_kernel(den, mom, ene, part, carry_x, carry_f, carry_d, carry_n, tend_hbm, after_hbm, tend, after, sems):
    chunks, fields, size_x = tend.shape[:3]
    half_rows = carry_x.shape[1] // 2
    rows = half_rows // fields
    owners = 8 // rows
    ratio, far_gain, _ = compact_kernel()
    filter_ratio, gain = decay(filter_alpha)
    straight = 0.5 * (0.5 + filter_alpha) / filter_alpha
    amplitude = (0.5 + filter_alpha - straight) * gain
    _, near_d, far_d, _, _ = filtered_derivative()
    power = ratio**size_x
    unroll = 8

    def copies(chunk):
        ys = pl.ds(pl.multiple_of(chunk * 8, 8), 8)
        return (
            pltpu.make_async_copy(tend.at[chunk], tend_hbm.at[:, :, ys], sems.at[0, chunk]),
            pltpu.make_async_copy(after.at[chunk], after_hbm.at[:, :, ys], sems.at[1, chunk]),
        )

    def chunk_body(chunk, _):
        ys = pl.ds(pl.multiple_of(chunk * 8, 8), 8)

        def carried_in(ref, side, f):
            place = side * half_rows + rows * f
            return jnp.concatenate(
                [ref[chunk * owners + o, place : place + rows, :] for o in range(owners)], axis=0
            )

        def state(f, x):
            return den[x, ys, :] if f == 0 else ene[x, ys, :] if f == 4 else mom[f - 1, x, ys, :]

        from_l = [carried_in(carry_x, 0, f) + carry_n[0, f, ys, :] for f in range(fields)]
        from_r = [carried_in(carry_x, 1, f) + carry_n[1, f, ys, :] for f in range(fields)]
        start_l = [
            carried_in(carry_f, 0, f)
            + carry_d[0, f, ys, :]
            + time_step * (near_d * from_l[f] + float(far_d * power) * from_r[f])
            for f in range(fields)
        ]
        start_r = [
            carried_in(carry_f, 1, f)
            + carry_d[1, f, ys, :]
            - time_step * (near_d * from_r[f] + float(far_d * power) * from_l[f])
            for f in range(fields)
        ]
        head = [float(far_gain * ratio ** (size_x - 1)) * from_l[f] for f in range(fields)]
        tail = [far_gain * from_r[f] for f in range(fields)]

        def back(step, carried):
            carried = list(carried)
            for inner in range(unroll):
                x = size_x - 1 - (step * unroll + inner)
                for f in range(fields):
                    behind, ahead = carried[5 + f], carried[10 + f]
                    rate = ahead - behind - part[f, x, ys, :]
                    tend[chunk, f, x] = rate
                    after[chunk, f, x] = amplitude * carried[f]
                    carried[f] = filter_ratio * (carried[f] + (state(f, x) + time_step * rate))
                    carried[5 + f], carried[10 + f] = (1.0 / ratio) * behind, ratio * ahead
            return tuple(carried)

        def ahead(step, carried):
            carried = list(carried)
            for inner in range(unroll):
                x = step * unroll + inner
                for f in range(fields):
                    middle = state(f, x) + time_step * tend[chunk, f, x]
                    after[chunk, f, x] += (straight + amplitude) * middle + amplitude * carried[f]
                    carried[f] = filter_ratio * (carried[f] + middle)
            return tuple(carried)

        lax.fori_loop(0, size_x // unroll, back, tuple(start_r + head + tail))
        rate_copy, after_copy = copies(chunk)
        rate_copy.start()
        lax.fori_loop(0, size_x // unroll, ahead, tuple(start_l))
        after_copy.start()
        return 0

    lax.fori_loop(0, chunks, chunk_body, 0)
    for chunk in range(chunks):
        for copy in copies(chunk):
            copy.wait()


def solution(mesh):
    nx, ny, nz = mesh.shape["gx"], mesh.shape["gy"], mesh.shape["gz"]

    def on_device(density, momentum, energy, metric):
        size_x, size_y, size_z = density.shape
        fields = 5
        rows = size_y // nx
        float32 = jnp.float32
        ky, py = wall_tables(ny, size_y)
        kz, qz, pz = span_tables(nz, size_z)
        wtab = stream_weights(size_x).astype(np.float32)
        cells = (fields, size_x, size_y, size_z)
        owned = (nx, 2 * fields * rows, size_z)
        chipwise = (nx // 2, 2 * fields * rows, size_z)
        sides = (2, fields, size_y, size_z)
        vmem = pl.BlockSpec(memory_space=pltpu.VMEM)
        stays = pl.BlockSpec(memory_space=pltpu.HBM)
        copies = 11 + 2 * (ny - 1) + 2 * (nz - 1)
        chunks = size_y // 8
        part, carry_x, carry_f, carry_d, carry_n = pl.pallas_call(
            functools.partial(exchange_kernel, nx, ny, nz),
            out_shape=[
                jax.ShapeDtypeStruct(cells, float32),
                jax.ShapeDtypeStruct(owned, float32),
                jax.ShapeDtypeStruct(owned, float32),
                jax.ShapeDtypeStruct(sides, float32),
                jax.ShapeDtypeStruct(sides, float32),
            ],
            in_specs=[stays] * 10,
            out_specs=[vmem] * 5,
            scratch_shapes=[
                pltpu.VMEM(cells[1:], float32),
                pltpu.VMEM((3,) + cells[1:], float32),
                pltpu.VMEM(cells[1:], float32),
                pltpu.VMEM((1, ny * size_y), float32),
                pltpu.SMEM(wtab.shape, float32),
                pltpu.VMEM(ky.shape[1:], float32),
                pltpu.VMEM(py.shape[1:], float32),
                pltpu.VMEM(kz.shape, bfloat16),
                pltpu.VMEM(qz.shape, bfloat16),
                pltpu.VMEM(pz.shape, bfloat16),
                pltpu.VMEM(ky.shape[1:], bfloat16),
                pltpu.VMEM(ky.shape[1:], bfloat16),
                pltpu.VMEM(py.shape[1:], bfloat16),
                pltpu.VMEM(cells, float32),
                pltpu.VMEM(cells, float32),
                pltpu.VMEM(cells, float32),
                pltpu.VMEM(sides, float32),
                pltpu.VMEM(sides, float32),
                pltpu.VMEM((16, size_y, size_z), float32),
                pltpu.VMEM((2, 8, size_y, size_z), float32),
                pltpu.VMEM((16, size_y, size_z), float32),
                pltpu.VMEM((2, 8, size_y, size_z), float32),
                pltpu.VMEM((4, 16, size_z), float32),
                pltpu.VMEM((8, 16, size_z), float32),
                pltpu.VMEM((nz, 8, 8 * size_y), float32),
                pltpu.VMEM((4, fields, size_x, size_z), float32),
                pltpu.VMEM((8, fields, size_x, size_z), float32),
                pltpu.VMEM((nz, fields, 8, size_x // 2 * size_y), float32),
                pltpu.VMEM(sides, float32),
                pltpu.VMEM(sides, float32),
                pltpu.VMEM(sides, float32),
                pltpu.VMEM(chipwise, float32),
                pltpu.VMEM(chipwise, float32),
                pltpu.VMEM(owned, float32),
                pltpu.VMEM(owned, float32),
                pltpu.VMEM(chipwise, float32),
                pltpu.VMEM(chipwise, float32),
                pltpu.VMEM(chipwise, float32),
                pltpu.VMEM(owned, float32),
                pltpu.VMEM(owned, float32),
                pltpu.SemaphoreType.DMA((3, chunks)),
                pltpu.SemaphoreType.DMA((7,)),
                pltpu.SemaphoreType.DMA((copies,)),
                pltpu.SemaphoreType.DMA((copies,)),
            ],
            compiler_params=pltpu.CompilerParams(
                collective_id=0, has_side_effects=True, vmem_limit_bytes=24 * 1024 * 1024
            ),
            cost_estimate=pl.CostEstimate(flops=4 * 10**9, bytes_accessed=10**7, transcendentals=0),
        )(
            *[
                pltpu.with_memory_space_constraint(jnp.asarray(value), pltpu.HBM)
                for value in (density, momentum, energy, metric.reshape(1, -1), wtab, ky, py, kz, qz, pz)
            ]
        )
        return pl.pallas_call(
            filter_kernel,
            out_shape=[jax.ShapeDtypeStruct(cells, float32), jax.ShapeDtypeStruct(cells, float32)],
            in_specs=[vmem] * 8,
            out_specs=[stays] * 2,
            scratch_shapes=[
                pltpu.VMEM((chunks, fields, size_x, 8, size_z), float32),
                pltpu.VMEM((chunks, fields, size_x, 8, size_z), float32),
                pltpu.SemaphoreType.DMA((2, chunks)),
            ],
            compiler_params=pltpu.CompilerParams(vmem_limit_bytes=16 * 1024 * 1024),
            cost_estimate=pl.CostEstimate(flops=10**7, bytes_accessed=10**7, transcendentals=0),
        )(density, momentum, energy, part, carry_x, carry_f, carry_d, carry_n)

    return jax.shard_map(
        on_device,
        mesh=mesh,
        in_specs=(P("gx", "gy", "gz"), P(None, "gx", "gy", "gz"), P("gx", "gy", "gz"), P()),
        out_specs=(P(None, "gx", "gy", "gz"), P(None, "gx", "gy", "gz")),
        check_vma=False,
    )
```
